32 devices in a mesh: dp: 8 (over y, x, core), tensor: 4 (over z).
Axes of the slice: x: 2, y: 2, z: 4, core: 2. Of those that a mesh axis runs over, the one named last changes fastest.
Arguments:
- inputs: bfloat16 [16384, 1280], P(('dp', 'tensor')), may hold values from -6 to 6
- cotangent: bfloat16 [16384, 1280], P(('dp', 'tensor')), may hold values from -6 to 6
- gain_attn: float32 [1280], replicated, may hold values from 0.1 to 1.9
- gain_mlp: float32 [1280], replicated, may hold values from 0.1 to 1.9
- query_scale: float32 [80], replicated, may hold values from -0.5 to 1.5
- w_query: bfloat16 [1280, 1280], P(None, 'tensor'), may hold values from -0.15625 to 0.15625
- w_key: bfloat16 [1280, 1280], P(None, 'tensor'), may hold values from -0.15625 to 0.15625
- w_value: bfloat16 [1280, 1280], P(None, 'tensor'), may hold values from -0.15625 to 0.15625
- w_out: bfloat16 [1280, 1280], P('tensor'), may hold values from -1 to 1
- w_up: bfloat16 [1280, 1280], P(None, 'tensor'), may hold values from -0.15625 to 0.15625
- w_down: bfloat16 [1280, 1280], P('tensor'), may hold values from -0.15625 to 0.15625
- lengths: int32 [8], P('dp'), may hold values from 1024 to 2048, as said below
- offsets: int32 [8], P('dp'), may hold values from 0 to 1024, as said below
Outputs:
- output: bfloat16 [16384, 1280], P(('dp', 'tensor'))
- grad_input: float32 [16384, 1280], P(('dp', 'tensor'))
- grad_gain_attn: float32 [1280], replicated
- grad_gain_mlp: float32 [1280], replicated
- grad_query_scale: float32 [80], replicated
- grad_query: float32 [1280, 1280], P(None, 'tensor')
- grad_key: float32 [1280, 1280], P(None, 'tensor')
- grad_value: float32 [1280, 1280], P(None, 'tensor')
- grad_out: float32 [1280, 1280], P('tensor')
- grad_up: float32 [1280, 1280], P(None, 'tensor')
- grad_down: float32 [1280, 1280], P('tensor')
The draws below stay inside these ranges and needn't reach their ends.
Inputs may be any that keep to these rules, and one draw needn't show every extreme that they name: `lengths`: one group's sequence fills all 2048 slots and another's is exactly 1024 long. `offsets`: a sequence never runs past its group's 2048 slots; the group whose length is 1024 starts at 1024.
All inputs are finite; a program needn't handle non-finite values.
Results may differ from the reference program's by a relative error of at most 0.018.
Values may be sent and summed in bfloat16 or wider, within the bound.
A program may use at most 256 MiB of HBM per device.

```python
import math
import jax
import jax.numpy as jnp
from jax import lax

D = 1280
H = 16
E = 80
FF = 1280
SLOTS = 2048
TOKENS = 16384
N_DP = 8


def chosen_groups(key):
    order = jax.random.permutation(jax.random.fold_in(key, 5), N_DP)
    return (order[0], order[1])


def draw_lengths(key, part):
    first_group, second_group = chosen_groups(key)
    key = jax.random.fold_in(key, 11)
    values = jax.random.randint(key, (N_DP,), SLOTS // 2, SLOTS + 1)
    values = values.at[first_group].set(SLOTS).at[second_group].set(SLOTS // 2)
    return values.astype(jnp.int32)


def draw_offsets(key, part):
    first_group, second_group = chosen_groups(key)
    seq_lengths = draw_lengths(key, part)
    key = jax.random.fold_in(key, 23)
    values = jax.random.randint(key, (N_DP,), 0, SLOTS - seq_lengths + 1)
    values = values.at[second_group].set(SLOTS - SLOTS // 2).at[first_group].set(0)
    return values.astype(jnp.int32)


def block_levels(rng, dims, split, smallest, high):
    factor_of, own = 1.0, jax.random.fold_in(rng, 6)
    for axis_at, blocks in split:
        draws = jnp.exp(jax.random.uniform(jax.random.fold_in(own, axis_at), (blocks,), jnp.float32, smallest / len(split), high / len(split)))
        factor_of = factor_of * jnp.repeat(draws, dims[axis_at] // blocks).reshape([-1 if axis == axis_at else 1 for axis in range(len(dims))])
    return factor_of


def noise(key, dims, spread, limit, pieces=(), kind=jnp.bfloat16):
    factor_of = block_levels(key, dims, pieces, -0.22, 0.18) if pieces else 1.0
    values = jax.random.normal(key, dims, jnp.float32) * spread * factor_of
    return jnp.minimum(jnp.maximum(values, -limit), limit).astype(kind)


def setup_inputs(seed: int = 0) -> dict:
    keys = jax.random.split(jax.random.key(seed), 14)
    inputs = noise(keys[0], (TOKENS, D), 1.0, 6.0, ((0, 32),))
    cotangent = noise(keys[1], (TOKENS, D), 1.0, 6.0, ((0, 32),))
    gain_attn = jnp.clip(1.0 + 0.18 * jax.random.normal(keys[2], (D,), jnp.float32), 0.1, 1.9)
    gain_mlp = jnp.clip(1.0 + 0.18 * jax.random.normal(keys[3], (D,), jnp.float32), 0.1, 1.9)
    query_scale = jnp.clip(jax.random.uniform(keys[4], (E,), jnp.float32, -0.5, 1.5), -0.5, 1.5)
    w_query = noise(keys[5], (D, H * E), D ** -0.5, 0.15625, ((1, 4),))
    w_key = noise(keys[6], (D, H * E), D ** -0.5, 0.15625, ((1, 4),))
    w_value = noise(keys[7], (D, H * E), D ** -0.5, 0.15625, ((1, 4),))
    w_out = noise(keys[8], (H * E, D), (H * E // 32) ** -0.5, 1.0, ((0, 4),))
    w_up = noise(keys[9], (D, FF), D ** -0.5, 0.15625, ((1, 4),))
    w_down = noise(keys[10], (FF, D), FF ** -0.5, 0.15625, ((0, 4),))
    lengths = draw_lengths(jax.random.fold_in(keys[13], 71), 0)
    offsets = draw_offsets(jax.random.fold_in(keys[13], 71), 0)
    return {"inputs": inputs, "cotangent": cotangent, "gain_attn": gain_attn, "gain_mlp": gain_mlp, "query_scale": query_scale, "w_query": w_query, "w_key": w_key, "w_value": w_value, "w_out": w_out, "w_up": w_up, "w_down": w_down, "lengths": lengths, "offsets": offsets}


EPSILON = 1e-06
LOG_TWO_E = 1.4426950408889634

@jax.custom_vjp
def low(v):
    return lax.optimization_barrier(v.astype(jnp.bfloat16)).astype(jnp.float32)

@jax.custom_vjp
def low_back(v):
    return v

def low_keep(v):
    return (low(v), None)

def low_pass(kept, grad):
    return (grad,)

def back_keep(v):
    return (v, None)

def back_low(kept, grad):
    return (low(grad),)
low.defvjp(low_keep, low_pass)
low_back.defvjp(back_keep, back_low)

def rms_norm(values, gain):
    return values * lax.rsqrt(lax.optimization_barrier(jnp.mean(values * values, axis=-1, keepdims=True)) + EPSILON) * gain

def matmul(left, right):
    return jnp.dot(left, right, precision=lax.Precision.HIGHEST)

def attend_block(queries, positions, key_rows, value_rows, key_ok):
    scores = low_back(jnp.einsum('qhe,khe->hqk', queries, key_rows, precision=lax.Precision.HIGHEST))
    slot_index = jnp.arange(key_rows.shape[0], dtype=jnp.int32)
    allowed = key_ok[None, :] & (slot_index[None, :] <= positions[:, None]) | (slot_index[None, :] == positions[:, None])
    scores = jnp.where(allowed[None], scores, -1e+30)
    weights = jax.nn.softmax(scores, axis=-1)
    return jnp.einsum('hqk,khe->qhe', low(weights), value_rows, precision=lax.Precision.HIGHEST)

def layer(params, inputs, length, offset):
    gain_attn, gain_mlp, query_scale, w_query, w_key, w_value, w_out, w_up, w_down = params
    positions = jnp.arange(SLOTS, dtype=jnp.int32)
    key_ok = (positions >= offset) & (positions < offset + length)
    normed = low(rms_norm(inputs, gain_attn))
    factor = jax.nn.softplus(query_scale) * (LOG_TWO_E / math.sqrt(E))
    queries = low_back(matmul(normed, w_query)).reshape(SLOTS, H, E)
    queries = low(queries * factor)
    key_rows = low(low_back(matmul(normed, w_key))).reshape(SLOTS, H, E)
    value_rows = low(low_back(matmul(normed, w_value))).reshape(SLOTS, H, E)
    block_rows = min(512, SLOTS)
    block_count = SLOTS // block_rows
    query_blocks = queries.reshape(block_count, block_rows, H, E)
    position_blocks = positions.reshape(block_count, block_rows)
    attended = lax.map(jax.checkpoint(lambda entry_pair: attend_block(entry_pair[0], entry_pair[1], key_rows, value_rows, key_ok)), (query_blocks, position_blocks))
    attended = low(low_back(attended.reshape(SLOTS, H * E)))
    hidden_one = inputs + low_back(matmul(attended, w_out))
    second = low(rms_norm(hidden_one, gain_mlp))
    before_act = low_back(matmul(second, w_up))
    activated = low(jax.nn.silu(before_act))
    return hidden_one + low_back(matmul(activated, w_down))

def reference(inputs, cotangent, gain_attn, gain_mlp, query_scale, w_query, w_key, w_value, w_out, w_up, w_down, lengths, offsets):
    params = tuple((weight.astype(jnp.float32) for weight in (gain_attn, gain_mlp, query_scale, w_query, w_key, w_value, w_out, w_up, w_down)))
    groups_in = inputs.astype(jnp.float32).reshape(N_DP, SLOTS, D)
    groups_cot = cotangent.astype(jnp.float32).reshape(N_DP, SLOTS, D)

    def scan_step(running, entry):
        group_in, group_cot, length, offset = entry
        slot_index = jnp.arange(SLOTS, dtype=jnp.int32)
        valid = ((slot_index >= offset) & (slot_index < offset + length)).astype(jnp.float32)
        result, pullback = jax.vjp(lambda weights, values: layer(weights, values, length, offset), params, group_in)
        grad_params, grad_values = pullback(group_cot * valid[:, None])
        running = jax.tree.map(lambda left, right: left + right, running, grad_params)
        return (running, (result.astype(jnp.bfloat16), grad_values))
    initial = jax.tree.map(jnp.zeros_like, params)
    totals, (outputs, grad_inputs) = lax.scan(scan_step, initial, (groups_in, groups_cot, lengths, offsets))
    return (outputs.reshape(TOKENS, D), grad_inputs.reshape(TOKENS, D), totals[0], totals[1], totals[2], totals[3], totals[4], totals[5], totals[6], totals[7], totals[8])
```

```python
import functools
import math

import jax
import jax.numpy as jnp
from jax import lax
from jax.experimental import pallas as pl
from jax.experimental.pallas import tpu as pltpu
from jax.sharding import PartitionSpec as P

EPSILON = 1e-06
LOG_TWO_E = 1.4426950408889634
MESH_ID = pl.DeviceIdType.MESH
CHUNKS = 4


def rms_forward(values, gain):
    inverse = lax.rsqrt(jnp.mean(values * values, axis=-1, keepdims=True) + EPSILON)
    return (values * inverse * gain, inverse)


def rms_backward(values, inverse, gain, grad_normed):
    scaled = values * inverse
    grad_scaled = grad_normed * gain
    return inverse * (
        grad_scaled - scaled * jnp.mean(grad_scaled * scaled, axis=-1, keepdims=True)
    )


def contract_rows(left, right):
    return lax.dot_general(
        left, right, (((0,), (0,)), ((), ())), preferred_element_type=jnp.float32
    )


def contract_cols(left, right):
    return lax.dot_general(
        left, right, (((1,), (1,)), ((), ())), preferred_element_type=jnp.float32
    )


def silu_slope(values):
    sigmoid_v = jax.nn.sigmoid(values)
    return sigmoid_v * (1.0 + values * (1.0 - sigmoid_v))


class Place:
    def __init__(self):
        self.d = lax.axis_index("dp")
        self.t = lax.axis_index("tensor")
        self.c = lax.rem(self.d, 2)
        self.g = self.t // 2
        self.base = self.d - self.c
        self.main = self.c == self.g
        self.pos = jnp.where(self.c == 0, self.t, 3 - self.t)

    def device(self, seq, pos):
        return (self.base + seq, jnp.where(seq == 0, pos, 3 - pos))

    def partner(self):
        return (self.base + 1 - self.c, self.t)

    def quarter(self):
        return jnp.where(self.main, self.t, lax.rem(self.t + 2, 4))


def pair_barrier(here):
    barrier = pltpu.get_barrier_semaphore()
    for step in range(1, 8):
        code = lax.rem(here.c * 4 + here.t + step, 8)
        pl.semaphore_signal(
            barrier, inc=1, device_id=(here.base + code // 4, lax.rem(code, 4)), device_id_type=MESH_ID
        )
    pl.semaphore_wait(barrier, 7)


def remote(src, dst, send, recv, device):
    return pltpu.make_async_remote_copy(
        src_ref=src, dst_ref=dst, send_sem=send, recv_sem=recv, device_id=device, device_id_type=MESH_ID
    )


def gather_kernel(own, out, send_z, send_c, recv, local_sem):
    here = Place()
    rows = own.shape[0]
    part = rows // CHUNKS
    pair_barrier(here)
    partner = here.partner()

    def place(seq, k, ch):
        block = jnp.where(seq == 0, k, 3 - k)
        return out.at[pl.ds(pl.multiple_of(block * rows + ch * part, part), part)]

    def own_part(ch):
        return own.at[pl.ds(ch * part, part)]

    def copy(src, k, ch, seq, device, send):
        return remote(src, place(seq, k, ch), send.at[k, ch], recv.at[k, ch], device)

    def arrived(k, ch, seq):
        copy(place(seq, k, ch), k, ch, seq, partner, send_z).wait_recv()

    for k in (2, 3):
        @pl.when(here.pos == k)
        def _(k=k):
            target = here.device(here.c, 1)
            for ch in range(CHUNKS):
                copy(own_part(ch), k, ch, here.c, target, send_z).start()
            for ch in range(CHUNKS):
                for kk in range(4):
                    arrived(kk, ch, 1 - here.c)
            for ch in range(CHUNKS):
                copy(own_part(ch), k, ch, here.c, target, send_z).wait_send()

    def keep(k):
        return pltpu.make_async_copy(
            own, out.at[pl.ds(pl.multiple_of(jnp.where(here.c == 0, k, 3 - k) * rows, rows), rows)], local_sem
        )

    @pl.when(here.pos == 1)
    def _():
        seq = here.c
        near = here.device(seq, 0)
        sent = []

        def send(src, k, ch, device, sem):
            copy(src, k, ch, seq, device, sem).start()
            sent.append((src, k, ch, device, sem))

        keep(1).start()
        for ch in range(CHUNKS):
            send(own_part(ch), 1, ch, near, send_z)
            send(own_part(ch), 1, ch, partner, send_c)
        for ch in range(CHUNKS):
            for k in (2, 3):
                arrived(k, ch, seq)
                send(place(seq, k, ch), k, ch, near, send_z)
                send(place(seq, k, ch), k, ch, partner, send_c)
            arrived(0, ch, seq)
            send(place(seq, 0, ch), 0, ch, partner, send_c)
        for src, k, ch, device, sem in sent:
            copy(src, k, ch, seq, device, sem).wait_send()
        keep(1).wait()

    @pl.when(here.pos == 0)
    def _():
        seq = here.c
        far = here.device(seq, 1)
        sent = []

        def send(src, k, ch, device, sem):
            copy(src, k, ch, seq, device, sem).start()
            sent.append((src, k, ch, device, sem))

        keep(0).start()
        for ch in range(CHUNKS):
            send(own_part(ch), 0, ch, far, send_z)
            send(own_part(ch), 0, ch, partner, send_c)
        for ch in range(CHUNKS):
            arrived(1, ch, seq)
            send(place(seq, 1, ch), 1, ch, partner, send_c)
        for ch in range(CHUNKS):
            for k in (2, 3):
                arrived(k, ch, seq)
                send(place(seq, k, ch), k, ch, partner, send_c)
        for src, k, ch, device, sem in sent:
            copy(src, k, ch, seq, device, sem).wait_send()
        keep(0).wait()


def gather_rows(own):
    rows, width = own.shape
    return pl.pallas_call(
        gather_kernel,
        out_shape=jax.ShapeDtypeStruct((4 * rows, width), own.dtype),
        in_specs=[pl.BlockSpec(memory_space=pl.ANY)],
        out_specs=pl.BlockSpec(memory_space=pl.ANY),
        scratch_shapes=[
            pltpu.SemaphoreType.DMA((4, CHUNKS)),
            pltpu.SemaphoreType.DMA((4, CHUNKS)),
            pltpu.SemaphoreType.DMA((4, CHUNKS)),
            pltpu.SemaphoreType.DMA,
        ],
        compiler_params=pltpu.CompilerParams(collective_id=0, has_side_effects=True),
        name="gather_rows",
    )(own)


def heads_to_rows_kernel(heads, out, send, recv, local_sem):
    here = Place()
    rows = out.shape[1]
    pair_barrier(here)
    quarter = here.quarter()
    mine = here.main

    def copy(block):
        return remote(
            heads.at[pl.ds(block * rows, rows)],
            out.at[quarter],
            send.at[block],
            recv.at[quarter],
            (here.base + here.g, block),
        )

    keep = pltpu.make_async_copy(
        heads.at[pl.ds(pl.multiple_of(here.t * rows, rows), rows)], out.at[here.t], local_sem
    )
    for block in range(4):
        @pl.when(mine & (here.t == block))
        def _():
            keep.start()

        @pl.when(jnp.logical_not(mine & (here.t == block)))
        def _(block=block):
            copy(block).start()

    for q in range(4):
        @pl.when(jnp.logical_not(mine & (here.t == q)))
        def _(q=q):
            remote(
                heads.at[pl.ds(0, rows)], out.at[q], send.at[0], recv.at[q], here.partner()
            ).wait_recv()

    for block in range(4):
        @pl.when(mine & (here.t == block))
        def _():
            keep.wait()

        @pl.when(jnp.logical_not(mine & (here.t == block)))
        def _(block=block):
            copy(block).wait_send()


def heads_to_rows(heads):
    rows, width = heads.shape[0] // 4, heads.shape[1]
    return pl.pallas_call(
        heads_to_rows_kernel,
        out_shape=jax.ShapeDtypeStruct((4, rows, width), heads.dtype),
        in_specs=[pl.BlockSpec(memory_space=pl.ANY)],
        out_specs=pl.BlockSpec(memory_space=pl.ANY),
        scratch_shapes=[
            pltpu.SemaphoreType.DMA((4,)),
            pltpu.SemaphoreType.DMA((4,)),
            pltpu.SemaphoreType.DMA,
        ],
        compiler_params=pltpu.CompilerParams(collective_id=1, has_side_effects=True),
        name="heads_to_rows",
    )(heads)


def rows_to_heads_kernel(split, out, send, recv, local_sem):
    here = Place()
    rows = split.shape[1]
    pair_barrier(here)

    def copy(q):
        native = (q // 2) == here.c
        seq = jnp.where(native, here.c, 1 - here.c)
        line = jnp.where(native, q, (q + 2) % 4)
        return remote(
            split.at[q],
            out.at[pl.ds(pl.multiple_of(here.t * rows, rows), rows)],
            send.at[q],
            recv.at[here.t],
            (here.base + seq, line),
        )

    keep = pltpu.make_async_copy(
        split.at[here.t], out.at[pl.ds(pl.multiple_of(here.t * rows, rows), rows)], local_sem
    )
    for q in range(4):
        @pl.when(here.main & (here.t == q))
        def _():
            keep.start()

        @pl.when(jnp.logical_not(here.main & (here.t == q)))
        def _(q=q):
            copy(q).start()

    for block in range(4):
        @pl.when(jnp.logical_not(here.main & (here.t == block)))
        def _(block=block):
            remote(
                split.at[0], out.at[pl.ds(block * rows, rows)], send.at[0], recv.at[block], here.partner()
            ).wait_recv()

    for q in range(4):
        @pl.when(here.main & (here.t == q))
        def _():
            keep.wait()

        @pl.when(jnp.logical_not(here.main & (here.t == q)))
        def _(q=q):
            copy(q).wait_send()


def rows_to_heads(split):
    _, rows, width = split.shape
    return pl.pallas_call(
        rows_to_heads_kernel,
        out_shape=jax.ShapeDtypeStruct((4 * rows, width), split.dtype),
        in_specs=[pl.BlockSpec(memory_space=pl.ANY)],
        out_specs=pl.BlockSpec(memory_space=pl.ANY),
        scratch_shapes=[
            pltpu.SemaphoreType.DMA((4,)),
            pltpu.SemaphoreType.DMA((4,)),
            pltpu.SemaphoreType.DMA,
        ],
        compiler_params=pltpu.CompilerParams(collective_id=2, has_side_effects=True),
        name="rows_to_heads",
    )(split)


def scatter_kernel(partial, out, from_core, from_line, outgoing, send_c, send_z, recv_c, recv_z):
    here = Place()
    rows = out.shape[0]
    part = rows // CHUNKS
    pair_barrier(here)
    partner = here.partner()
    f32 = jnp.float32

    def span(seq, k, ch):
        block = jnp.where(seq == 0, k, 3 - k)
        return pl.ds(pl.multiple_of(block * rows + ch * part, part), part)

    def piece(k, ch):
        return pl.ds(k * rows + ch * part, part)

    def line(ch):
        return pl.ds(ch * part, part)

    order = (3, 2, 1, 0)

    for k in (2, 3):
        @pl.when(here.pos == k)
        def _(k=k):
            seq = 1 - here.c
            copies = []
            for kk in order:
                for ch in range(CHUNKS):
                    cp = remote(
                        partial.at[span(seq, kk, ch)],
                        from_core.at[piece(kk, ch)],
                        send_c.at[kk, ch],
                        recv_c.at[kk, ch],
                        partner,
                    )
                    cp.start()
                    copies.append(cp)
            for ch in range(CHUNKS):
                remote(
                    outgoing.at[piece(0, ch)], out.at[line(ch)], send_z.at[0, ch], recv_z.at[k, ch], partner
                ).wait_recv()
            for cp in copies:
                cp.wait_send()

    def core_sum(k, ch):
        remote(
            partial.at[piece(k, ch)], from_core.at[piece(k, ch)], send_c.at[k, ch], recv_c.at[k, ch], partner
        ).wait_recv()
        return partial[span(here.c, k, ch)].astype(f32) + from_core[piece(k, ch)].astype(f32)

    def line_wait(k, ch):
        remote(
            outgoing.at[piece(k, ch)], from_line.at[piece(k, ch)], send_z.at[k, ch], recv_z.at[k, ch], partner
        ).wait_recv()
        return from_line[piece(k, ch)].astype(f32)

    @pl.when(here.pos == 0)
    def _():
        copies = []
        for k in (3, 2, 1):
            for ch in range(CHUNKS):
                outgoing[piece(k, ch)] = core_sum(k, ch).astype(outgoing.dtype)
                cp = remote(
                    outgoing.at[piece(k, ch)],
                    from_line.at[piece(k, ch)],
                    send_z.at[k, ch],
                    recv_z.at[k, ch],
                    here.device(here.c, 1),
                )
                cp.start()
                copies.append(cp)
        for ch in range(CHUNKS):
            total = core_sum(0, ch)
            out[line(ch)] = (total + line_wait(0, ch)).astype(out.dtype)
        for cp in copies:
            cp.wait_send()

    @pl.when(here.pos == 1)
    def _():
        copies = []
        for ch in range(CHUNKS):
            outgoing[piece(0, ch)] = core_sum(0, ch).astype(outgoing.dtype)
            cp = remote(
                outgoing.at[piece(0, ch)],
                from_line.at[piece(0, ch)],
                send_z.at[0, ch],
                recv_z.at[0, ch],
                here.device(here.c, 0),
            )
            cp.start()
            copies.append(cp)
        for k in (3, 2):
            for ch in range(CHUNKS):
                total = core_sum(k, ch)
                outgoing[piece(k, ch)] = (total + line_wait(k, ch)).astype(outgoing.dtype)
                cp = remote(
                    outgoing.at[piece(k, ch)],
                    out.at[line(ch)],
                    send_z.at[k, ch],
                    recv_z.at[k, ch],
                    here.device(here.c, k),
                )
                cp.start()
                copies.append(cp)
        for ch in range(CHUNKS):
            total = core_sum(1, ch)
            out[line(ch)] = (total + line_wait(1, ch)).astype(out.dtype)
        for cp in copies:
            cp.wait_send()


def scatter_rows(partial):
    rows, width = partial.shape[0] // 4, partial.shape[1]
    vmem = pl.BlockSpec(memory_space=pltpu.VMEM)
    return pl.pallas_call(
        scatter_kernel,
        out_shape=jax.ShapeDtypeStruct((rows, width), partial.dtype),
        in_specs=[vmem],
        out_specs=vmem,
        scratch_shapes=[
            pltpu.VMEM((4 * rows, width), partial.dtype),
            pltpu.VMEM((4 * rows, width), partial.dtype),
            pltpu.VMEM((4 * rows, width), partial.dtype),
            pltpu.SemaphoreType.DMA((4, CHUNKS)),
            pltpu.SemaphoreType.DMA((4, CHUNKS)),
            pltpu.SemaphoreType.DMA((4, CHUNKS)),
            pltpu.SemaphoreType.DMA((4, CHUNKS)),
        ],
        compiler_params=pltpu.CompilerParams(
            collective_id=3, has_side_effects=True, vmem_limit_bytes=40 * 1024 * 1024
        ),
        name="scatter_rows",
    )(partial)


def attention_forward(query_low, key_low, value_low, key_ok):
    seq_slots, heads_local, head_dim = query_low.shape
    slot_index = jnp.arange(seq_slots, dtype=jnp.int32)
    block_rows = min(512, seq_slots)
    block_count = seq_slots // block_rows

    def block_scores(block_index):
        first_row = block_index * block_rows
        last_row = first_row + block_rows
        query_pos = slot_index[first_row:last_row]
        key_pos = slot_index[:last_row]
        allowed = key_ok[None, :last_row] & (key_pos[None, :] <= query_pos[:, None]) | (
            key_pos[None, :] == query_pos[:, None]
        )
        scores = jnp.einsum(
            "qhe,khe->hqk",
            query_low[first_row:last_row],
            key_low[:last_row],
            preferred_element_type=jnp.float32,
        )
        return jnp.where(allowed[None], scores, -1e30)

    attended_parts = []
    logsum_parts = []
    for block_index in range(block_count):
        last_row = (block_index + 1) * block_rows
        scores = block_scores(block_index)
        highest = jnp.max(scores, axis=-1, keepdims=True)
        expo = jnp.exp(scores - highest)
        summed = jnp.sum(expo, axis=-1, keepdims=True)
        probs = (expo / summed).astype(jnp.bfloat16)
        attended_parts.append(
            jnp.einsum(
                "hqk,khe->qhe", probs, value_low[:last_row], preferred_element_type=jnp.float32
            )
        )
        logsum_parts.append(highest + jnp.log(summed))
    attended = jnp.concatenate(attended_parts, axis=0).reshape(seq_slots, -1)
    return attended, (block_scores, logsum_parts)


def attention_backward(query_low, key_low, value_low, attended, grad_att_low, saved):
    block_scores, logsum_parts = saved
    seq_slots, heads_local, head_dim = query_low.shape
    block_rows = min(512, seq_slots)
    block_count = seq_slots // block_rows
    row_term = jnp.sum(
        (grad_att_low.astype(jnp.float32) * attended).reshape(seq_slots, heads_local, head_dim),
        axis=-1,
    )
    grad_att_heads = grad_att_low.reshape(seq_slots, heads_local, head_dim)
    grad_query_parts = []
    grad_key_acc = jnp.zeros((seq_slots, heads_local, head_dim), jnp.float32)
    grad_value_acc = jnp.zeros((seq_slots, heads_local, head_dim), jnp.float32)
    for block_index in range(block_count):
        first_row = block_index * block_rows
        last_row = first_row + block_rows
        probs_full = jnp.exp(block_scores(block_index) - logsum_parts[block_index])
        grad_att_block = grad_att_heads[first_row:last_row]
        grad_probs = jnp.einsum(
            "qhe,khe->hqk", grad_att_block, value_low[:last_row], preferred_element_type=jnp.float32
        )
        block_term = jnp.transpose(row_term[first_row:last_row])[:, :, None]
        grad_scores = (probs_full * (grad_probs - block_term)).astype(jnp.bfloat16)
        grad_query_parts.append(
            jnp.einsum(
                "hqk,khe->qhe", grad_scores, key_low[:last_row], preferred_element_type=jnp.float32
            )
        )
        grad_key_acc = grad_key_acc.at[:last_row].add(
            jnp.einsum(
                "hqk,qhe->khe",
                grad_scores,
                query_low[first_row:last_row],
                preferred_element_type=jnp.float32,
            )
        )
        grad_value_acc = grad_value_acc.at[:last_row].add(
            jnp.einsum(
                "hqk,qhe->khe",
                probs_full.astype(jnp.bfloat16),
                grad_att_block,
                preferred_element_type=jnp.float32,
            )
        )
    return (
        jnp.concatenate(grad_query_parts, axis=0).reshape(seq_slots, -1),
        grad_key_acc.reshape(seq_slots, -1),
        grad_value_acc.reshape(seq_slots, -1),
    )


def per_device(
    inputs,
    cotangent,
    gain_attn,
    gain_mlp,
    query_scale,
    w_query,
    w_key,
    w_value,
    w_out,
    w_up,
    w_down,
    lengths,
    offsets,
):
    low = jnp.bfloat16
    f32 = jnp.float32
    here = Place()
    n_dp = lax.axis_size("dp")
    local_rows, model = inputs.shape
    seq_slots = local_rows * 4
    width_local = w_query.shape[1]
    head_dim = query_scale.shape[0]
    heads_local = width_local // head_dim
    slot_index = jnp.arange(seq_slots, dtype=jnp.int32)
    swap_core = [(i, i ^ 1) for i in range(n_dp)]
    swap_line = [(i, (i + 2) % 4) for i in range(4)]

    slice_rows = w_out.shape[0] // n_dp

    def own_slice(weight):
        return lax.dynamic_slice_in_dim(weight, here.d * slice_rows, slice_rows, 0)

    def gather_weight(weight):
        return lax.all_gather(own_slice(weight), ("tensor", "dp"), axis=0, tiled=True)

    up_slice = jnp.transpose(
        lax.dynamic_slice_in_dim(w_up, here.d * slice_rows, slice_rows, 1)
    )
    native_w = jnp.concatenate([w_query, w_key, w_value], axis=1)
    qkv_rows = model // n_dp
    foreign_slice = lax.ppermute(
        lax.dynamic_slice_in_dim(native_w, here.d * qkv_rows, qkv_rows, 0), "tensor", swap_line
    )
    foreign_w = lax.all_gather(foreign_slice, "dp", axis=0, tiled=True)
    stacked_w = jnp.where(here.main, native_w, foreign_w)
    own_span = jnp.concatenate([lengths, offsets])
    other_span = lax.ppermute(own_span, "dp", swap_core)
    group_span = jnp.where(here.main, own_span, other_span)

    key_ok = (slot_index >= group_span[1]) & (slot_index < group_span[1] + group_span[0])
    own_rows = here.t * local_rows + jnp.arange(local_rows, dtype=jnp.int32)
    row_valid = ((own_rows >= offsets[0]) & (own_rows < offsets[0] + lengths[0])).astype(f32)

    residual = inputs.astype(f32)
    normed, inverse_one = rms_forward(residual, gain_attn)
    gathered = gather_rows(normed.astype(low))
    w_out_all = gather_weight(w_out)
    w_up_all = lax.all_gather(up_slice, ("tensor", "dp"), axis=0, tiled=True)
    w_down_all = gather_weight(w_down)

    projected = jnp.dot(gathered, stacked_w, preferred_element_type=f32)
    scale_const = LOG_TWO_E / math.sqrt(head_dim)
    soft = jax.nn.softplus(query_scale)
    factor = jnp.tile(soft * scale_const, heads_local)
    shape = (seq_slots, heads_local, head_dim)
    query_low = (projected[:, :width_local] * factor).astype(low).reshape(shape)
    key_low = projected[:, width_local : 2 * width_local].astype(low).reshape(shape)
    value_low = projected[:, 2 * width_local :].astype(low).reshape(shape)
    attended, saved = attention_forward(query_low, key_low, value_low, key_ok)

    attended_rows = heads_to_rows(attended.astype(low))
    w_out_split = w_out_all.reshape(4, width_local, model)
    hidden_one = residual + jnp.einsum(
        "qre,qed->rd", attended_rows, w_out_split, preferred_element_type=f32
    )
    second, inverse_two = rms_forward(hidden_one, gain_mlp)
    second_low = second.astype(low)
    before_act = contract_cols(second_low, w_up_all)
    activated = jax.nn.silu(before_act).astype(low)
    output = hidden_one + jnp.dot(activated, w_down_all, preferred_element_type=f32)
    grad_hidden_out = cotangent.astype(f32) * row_valid[:, None]
    grad_low = grad_hidden_out.astype(low)
    grad_act = contract_cols(grad_low, w_down_all)
    grad_pre = (grad_act * silu_slope(before_act)).astype(low)
    grad_second = jnp.dot(grad_pre, w_up_all, preferred_element_type=f32)
    grad_hidden = grad_hidden_out + rms_backward(hidden_one, inverse_two, gain_mlp, grad_second)
    branch_low = grad_hidden.astype(low)
    grad_att_rows = jnp.einsum(
        "rd,qed->qre", branch_low, w_out_split, preferred_element_type=f32
    ).astype(low)
    grad_att_low = rows_to_heads(grad_att_rows)

    grad_w_down = contract_rows(activated, grad_low)
    grad_w_up_t = contract_rows(grad_pre, second_low)
    grad_w_out = jnp.einsum(
        "qre,rd->qed", attended_rows, branch_low, preferred_element_type=f32
    ).reshape(model, model)
    gain_two_part = jnp.sum(grad_w_up_t * w_up_all.astype(f32), axis=0)

    def reduce_weight(grad):
        split = jnp.transpose(grad.astype(low).reshape(4, n_dp, slice_rows, model), (1, 0, 2, 3))
        return split

    mlp_split = jnp.concatenate(
        [reduce_weight(grad_w_out), reduce_weight(grad_w_up_t), reduce_weight(grad_w_down)], axis=2
    ).reshape(n_dp * 12 * slice_rows, model)
    mlp_part = lax.psum_scatter(mlp_split, "dp", scatter_dimension=0, tiled=True)
    mlp_part = lax.psum_scatter(mlp_part, "tensor", scatter_dimension=0, tiled=True)
    mlp_all = lax.all_gather(mlp_part, "dp", axis=0, tiled=True).astype(f32)
    mlp_all = mlp_all.reshape(n_dp, 3, slice_rows, model)
    grad_out_final = mlp_all[:, 0].reshape(width_local, model)
    grad_up_final = jnp.transpose(mlp_all[:, 1].reshape(width_local, model))
    grad_down_final = mlp_all[:, 2].reshape(width_local, model)

    grad_query, grad_key, grad_value = attention_backward(
        query_low, key_low, value_low, attended, grad_att_low, saved
    )
    grad_stacked = jnp.concatenate(
        [(grad_query * factor).astype(low), grad_key.astype(low), grad_value.astype(low)], axis=1
    )
    grad_stacked_w = contract_rows(gathered, grad_stacked)
    grad_first = scatter_rows(contract_cols(grad_stacked, stacked_w).astype(low)).astype(f32)
    grad_input = grad_hidden + rms_backward(residual, inverse_one, gain_attn, grad_first)

    weighted = grad_stacked_w * stacked_w.astype(f32)
    gain_one_part = jnp.sum(weighted, axis=1)
    scale_part = jnp.sum(
        jnp.sum(weighted[:, :width_local], axis=0).reshape(heads_local, head_dim), axis=0
    )
    small = lax.psum(
        jnp.concatenate([gain_one_part, gain_two_part, scale_part]), ("dp", "tensor")
    )
    grad_gain_one = small[:model] / gain_attn
    grad_gain_two = small[model : 2 * model] / gain_mlp
    grad_scale = small[2 * model :] * jax.nn.sigmoid(query_scale) / soft

    same_core = [[i for i in range(n_dp) if i % 2 == k] for k in range(2)]
    qkv_part = lax.psum_scatter(
        grad_stacked_w.astype(low), "dp", scatter_dimension=0, tiled=True, axis_index_groups=same_core
    )
    qkv_sum = qkv_part.astype(f32) + lax.ppermute(qkv_part, "tensor", swap_line).astype(f32)
    qkv_sum = qkv_sum.astype(low)
    qkv_sum = jnp.where(here.main, qkv_sum, lax.ppermute(qkv_sum, "dp", swap_core))
    qkv_all = lax.all_gather(
        qkv_sum, "dp", axis=0, tiled=True, axis_index_groups=same_core
    ).astype(f32)
    return (
        output.astype(low),
        grad_input,
        grad_gain_one,
        grad_gain_two,
        grad_scale,
        qkv_all[:, :width_local],
        qkv_all[:, width_local : 2 * width_local],
        qkv_all[:, 2 * width_local :],
        grad_out_final,
        grad_up_final,
        grad_down_final,
    )


def solution(mesh):
    rows = P(("dp", "tensor"), None)
    cols_t = P(None, "tensor")
    rows_t = P("tensor", None)
    return jax.shard_map(
        per_device,
        mesh=mesh,
        in_specs=(
            rows, rows, P(), P(), P(), cols_t, cols_t, cols_t, rows_t, cols_t, rows_t, P("dp"), P("dp"),
        ),
        out_specs=(
            rows, rows, P(), P(), P(), cols_t, cols_t, cols_t, rows_t, cols_t, rows_t,
        ),
        check_vma=False,
    )
```

```python
import functools
import math

import jax
import jax.numpy as jnp
from jax import lax
from jax.experimental import pallas as pl
from jax.experimental.pallas import tpu as pltpu
from jax.sharding import PartitionSpec as P

EPSILON = 1e-06
LOG_TWO_E = 1.4426950408889634
MESH_ID = pl.DeviceIdType.MESH
CHUNKS = 4


def rms_forward(values, gain):
    inverse = lax.rsqrt(jnp.mean(values * values, axis=-1, keepdims=True) + EPSILON)
    return (values * inverse * gain, inverse)


def rms_backward(values, inverse, gain, grad_normed):
    scaled = values * inverse
    grad_scaled = grad_normed * gain
    return inverse * (
        grad_scaled - scaled * jnp.mean(grad_scaled * scaled, axis=-1, keepdims=True)
    )


def contract_rows(left, right):
    return lax.dot_general(
        left, right, (((0,), (0,)), ((), ())), preferred_element_type=jnp.float32
    )


def contract_cols(left, right):
    return lax.dot_general(
        left, right, (((1,), (1,)), ((), ())), preferred_element_type=jnp.float32
    )


def silu_slope(values):
    sigmoid_v = jax.nn.sigmoid(values)
    return sigmoid_v * (1.0 + values * (1.0 - sigmoid_v))


class Place:
    def __init__(self):
        self.d = lax.axis_index("dp")
        self.t = lax.axis_index("tensor")
        self.c = lax.rem(self.d, 2)
        self.g = self.t // 2
        self.base = self.d - self.c
        self.pairs = lax.axis_size("dp") // 2
        self.pair = self.d // 2
        self.main = self.c == self.g
        self.pos = jnp.where(self.c == 0, self.t, 3 - self.t)

    def device(self, seq, pos):
        return (self.base + seq, jnp.where(seq == 0, pos, 3 - pos))

    def across(self, step):
        return (2 * lax.rem(self.pair + step, self.pairs) + self.c, self.t)

    def partner(self):
        return (self.base + 1 - self.c, self.t)

    def quarter(self):
        return jnp.where(self.main, self.t, lax.rem(self.t + 2, 4))


def pair_barrier(here, plane=False):
    barrier = pltpu.get_barrier_semaphore()
    others = []
    for step in range(1, 8):
        code = lax.rem(here.c * 4 + here.t + step, 8)
        others.append((here.base + code // 4, lax.rem(code, 4)))
    if plane:
        others += [here.across(step) for step in range(1, here.pairs)]
    for device in others:
        pl.semaphore_signal(barrier, inc=1, device_id=device, device_id_type=MESH_ID)
    pl.semaphore_wait(barrier, len(others))


def remote(src, dst, send, recv, device):
    return pltpu.make_async_remote_copy(
        src_ref=src, dst_ref=dst, send_sem=send, recv_sem=recv, device_id=device, device_id_type=MESH_ID
    )


def gather_kernel(
    own, native, out, foreign, send_z, send_c, recv, local_sem, send_w, spread_w, recv_w
):
    here = Place()
    rows = own.shape[0]
    part = rows // CHUNKS
    pair_barrier(here, plane=True)
    partner = here.partner()
    members = native.shape[0]
    line = lax.rem(here.t + 2, 4)
    weight_copy = remote(
        native.at[here.d],
        foreign.at[here.d],
        send_w,
        recv_w.at[here.d],
        (here.base + 1 - line // 2, line),
    )
    weight_copy.start()

    def weight_arrived(member):
        remote(native.at[0], foreign.at[member], send_w, recv_w.at[member], partner).wait_recv()

    def spread(core, step):
        member = here.base + core
        return remote(
            foreign.at[member],
            foreign.at[member],
            spread_w.at[core, step],
            recv_w.at[member],
            here.across(step),
        )

    def place(seq, k, ch):
        block = jnp.where(seq == 0, k, 3 - k)
        return out.at[pl.ds(pl.multiple_of(block * rows + ch * part, part), part)]

    def own_part(ch):
        return own.at[pl.ds(ch * part, part)]

    def copy(src, k, ch, seq, device, send):
        return remote(src, place(seq, k, ch), send.at[k, ch], recv.at[k, ch], device)

    def arrived(k, ch, seq):
        copy(place(seq, k, ch), k, ch, seq, partner, send_z).wait_recv()

    for k in (2, 3):
        @pl.when(here.pos == k)
        def _(k=k):
            target = here.device(here.c, 1)
            for ch in range(CHUNKS):
                copy(own_part(ch), k, ch, here.c, target, send_z).start()
            for core in range(2):
                weight_arrived(here.base + core)
                for step in range(1, here.pairs):
                    spread(core, step).start()
            for step in range(1, here.pairs):
                for core in range(2):
                    weight_arrived(2 * lax.rem(here.pair + step, here.pairs) + core)
            for ch in range(CHUNKS):
                for kk in range(4):
                    arrived(kk, ch, 1 - here.c)
            for ch in range(CHUNKS):
                copy(own_part(ch), k, ch, here.c, target, send_z).wait_send()
            for core in range(2):
                for step in range(1, here.pairs):
                    spread(core, step).wait_send()

    def keep(k):
        return pltpu.make_async_copy(
            own, out.at[pl.ds(pl.multiple_of(jnp.where(here.c == 0, k, 3 - k) * rows, rows), rows)], local_sem
        )

    @pl.when(here.pos == 1)
    def _():
        seq = here.c
        near = here.device(seq, 0)
        sent = []

        def send(src, k, ch, device, sem):
            copy(src, k, ch, seq, device, sem).start()
            sent.append((src, k, ch, device, sem))

        keep(1).start()
        for ch in range(CHUNKS):
            send(own_part(ch), 1, ch, near, send_z)
            send(own_part(ch), 1, ch, partner, send_c)
        for ch in range(CHUNKS):
            for k in (2, 3):
                arrived(k, ch, seq)
                send(place(seq, k, ch), k, ch, near, send_z)
                send(place(seq, k, ch), k, ch, partner, send_c)
            arrived(0, ch, seq)
            send(place(seq, 0, ch), 0, ch, partner, send_c)
        for src, k, ch, device, sem in sent:
            copy(src, k, ch, seq, device, sem).wait_send()
        keep(1).wait()

    @pl.when(here.pos == 0)
    def _():
        seq = here.c
        far = here.device(seq, 1)
        sent = []

        def send(src, k, ch, device, sem):
            copy(src, k, ch, seq, device, sem).start()
            sent.append((src, k, ch, device, sem))

        keep(0).start()
        for ch in range(CHUNKS):
            send(own_part(ch), 0, ch, far, send_z)
            send(own_part(ch), 0, ch, partner, send_c)
        for ch in range(CHUNKS):
            arrived(1, ch, seq)
            send(place(seq, 1, ch), 1, ch, partner, send_c)
        for ch in range(CHUNKS):
            for k in (2, 3):
                arrived(k, ch, seq)
                send(place(seq, k, ch), k, ch, partner, send_c)
        for src, k, ch, device, sem in sent:
            copy(src, k, ch, seq, device, sem).wait_send()
        keep(0).wait()

    weight_copy.wait_send()


def gather_rows(own, native):
    rows, width = own.shape
    members = native.shape[0]
    hbm = pl.BlockSpec(memory_space=pl.ANY)
    return pl.pallas_call(
        gather_kernel,
        out_shape=(
            jax.ShapeDtypeStruct((4 * rows, width), own.dtype),
            jax.ShapeDtypeStruct(native.shape, native.dtype),
        ),
        in_specs=[hbm, hbm],
        out_specs=(hbm, hbm),
        scratch_shapes=[
            pltpu.SemaphoreType.DMA((4, CHUNKS)),
            pltpu.SemaphoreType.DMA((4, CHUNKS)),
            pltpu.SemaphoreType.DMA((4, CHUNKS)),
            pltpu.SemaphoreType.DMA,
            pltpu.SemaphoreType.DMA,
            pltpu.SemaphoreType.DMA((2, members // 2)),
            pltpu.SemaphoreType.DMA((members,)),
        ],
        compiler_params=pltpu.CompilerParams(collective_id=0, has_side_effects=True),
        name="gather_rows",
    )(own, native)


def dg(left, right, left_dim, right_dim):
    return lax.dot_general(
        left, right, (((left_dim,), (right_dim,)), ((), ())), preferred_element_type=jnp.float32
    )


TILE = 512
MASKED = -1e30


def readable(span, first_key, first_query):
    shape = (TILE, TILE)
    key = first_key + lax.broadcasted_iota(jnp.int32, shape, 0)
    query = first_query + lax.broadcasted_iota(jnp.int32, shape, 1)
    valid = (key >= span[1]) & (key < span[1] + span[0])
    return (valid & (key <= query)) | (key == query)


def key_bias(span, first_key):
    key = first_key + lax.broadcasted_iota(jnp.int32, (TILE, 1), 0)
    return jnp.where((key >= span[1]) & (key < span[1] + span[0]), 0.0, MASKED)


def forward_kernel(span, qkv, out, logsum, rows_out, highest, summed, total, send, recv, local_sem):
    heads = logsum.shape[0]
    width, slots = out.shape
    dim = width // heads
    here = Place()
    pair_barrier(here)
    quarter = here.quarter()

    def into(q):
        return rows_out.at[pl.ds(pl.multiple_of(q * width, width), width)]

    def columns(i):
        return out.at[:, pl.ds(pl.multiple_of(i * TILE, TILE), TILE)]

    def copy(i):
        return remote(columns(i), into(quarter), send.at[i], recv.at[quarter], (here.base + here.g, i))

    keep = pltpu.make_async_copy(columns(here.t), into(here.t), local_sem)

    @pl.loop(0, slots // TILE)
    def _(s):
        i = slots // TILE - 1 - s
        qs = pl.ds(pl.multiple_of(i * TILE, TILE), TILE)
        highest[...] = jnp.full_like(highest, MASKED)
        summed[...] = jnp.zeros_like(summed)
        total[...] = jnp.zeros_like(total)

        def tile(j, diagonal):
            ks = pl.ds(pl.multiple_of(j * TILE, TILE), TILE)
            if diagonal:
                allowed = readable(span, j * TILE, i * TILE)
            else:
                bias = key_bias(span, j * TILE)
            for h in range(heads):
                hs = pl.ds(h * dim, dim)
                scores = dg(qkv[pl.ds(width + h * dim, dim), ks], qkv[hs, qs], 0, 0)
                scores = jnp.where(allowed, scores, MASKED) if diagonal else scores + bias
                before = highest[h : h + 1]
                after = jnp.maximum(before, jnp.max(scores, axis=0, keepdims=True))
                expo = jnp.exp(scores - after)
                scale = jnp.exp(before - after)
                summed[h : h + 1] = summed[h : h + 1] * scale + jnp.sum(expo, axis=0, keepdims=True)
                highest[h : h + 1] = after
                total[hs] = total[hs] * scale + dg(
                    qkv[pl.ds(2 * width + h * dim, dim), ks], expo.astype(qkv.dtype), 1, 0
                )

        @pl.loop(0, i)
        def _(j):
            tile(j, False)

        tile(i, True)
        for h in range(heads):
            hs = pl.ds(h * dim, dim)
            out[hs, qs] = (total[hs] / summed[h : h + 1]).astype(out.dtype)
            logsum[h : h + 1, qs] = highest[h : h + 1] + jnp.log(summed[h : h + 1])
        stays = here.main & (here.t == i)

        @pl.when(stays)
        def _():
            keep.start()

        @pl.when(jnp.logical_not(stays))
        def _():
            copy(i).start()

    for block in range(4):
        stays = here.main & (here.t == block)

        @pl.when(stays)
        def _():
            keep.wait()

        @pl.when(jnp.logical_not(stays))
        def _(block=block):
            copy(block).wait_send()
            remote(columns(0), into(block), send.at[0], recv.at[block], here.partner()).wait_recv()


def attention_forward(span, qkv, heads):
    width, slots = qkv.shape[0] // 3, qkv.shape[1]
    vmem = pl.BlockSpec(memory_space=pltpu.VMEM)
    return pl.pallas_call(
        forward_kernel,
        out_shape=(
            jax.ShapeDtypeStruct((width, slots), qkv.dtype),
            jax.ShapeDtypeStruct((heads, slots), jnp.float32),
            jax.ShapeDtypeStruct((4 * width, slots // 4), qkv.dtype),
        ),
        in_specs=[pl.BlockSpec(memory_space=pltpu.SMEM), vmem],
        out_specs=(vmem, vmem, pl.BlockSpec(memory_space=pl.ANY)),
        scratch_shapes=[
            pltpu.VMEM((heads, TILE), jnp.float32),
            pltpu.VMEM((heads, TILE), jnp.float32),
            pltpu.VMEM((width, TILE), jnp.float32),
            pltpu.SemaphoreType.DMA((4,)),
            pltpu.SemaphoreType.DMA((4,)),
            pltpu.SemaphoreType.DMA,
        ],
        compiler_params=pltpu.CompilerParams(
            collective_id=1, has_side_effects=True, vmem_limit_bytes=50 * 1024 * 1024
        ),
        name="attention_forward",
    )(span, qkv)


def backward_kernel(
    span, qkv, out, logsum, factor, weights, split, grad_out, grad_up, grad_down,
    result, rows_grad, plane_sum,
    grad, query_sum, key_sum, value_sum, term,
    partial, from_core, from_line, keep_in, chip_sum, plane_in,
    split_sent, split_got, local_sem, keep_sem,
    give_sent, give_got, plane_sent, plane_got,
    send_c, send_z, recv_c, recv_z,
):
    heads = logsum.shape[0]
    width, slots = out.shape
    dim = width // heads
    low, f32 = qkv.dtype, jnp.float32
    here = Place()
    pairs = here.pairs
    rows = split.shape[1]
    part = rows // CHUNKS
    partner = here.partner()
    pair_barrier(here, plane=True)
    blocks = slots // TILE

    def of(q):
        return split.at[pl.ds(pl.multiple_of(q * width, width), width)]

    def into(block):
        return grad.at[:, pl.ds(pl.multiple_of(block * rows, rows), rows)]

    def split_copy(q):
        native = (q // 2) == here.c
        seq = jnp.where(native, here.c, 1 - here.c)
        line = jnp.where(native, q, (q + 2) % 4)
        return remote(of(q), into(here.t), split_sent.at[q], split_got.at[here.t], (here.base + seq, line))

    keep = pltpu.make_async_copy(of(here.t), into(here.t), local_sem)
    for q in range(4):
        stays = here.main & (here.t == q)

        @pl.when(stays)
        def _():
            keep.start()

        @pl.when(jnp.logical_not(stays))
        def _(q=q):
            split_copy(q).start()

    sources = (grad_out, grad_up, grad_down)
    columns = chip_sum.shape[-1]

    def half(core):
        return pl.ds(pl.multiple_of(core * columns, columns), columns)

    def give(w):
        return remote(
            sources[w].at[:, :, :, half(1 - here.c)], chip_sum.at[w], give_sent.at[w], give_got.at[w], partner
        )

    def own_half(w, q):
        slot = (4 * w + q) % 2
        return pltpu.make_async_copy(
            sources[w].at[q, :, :, half(here.c)], keep_in.at[slot], keep_sem.at[slot]
        )

    def plane_copy(w, step):
        return remote(
            chip_sum.at[w, :, lax.rem(here.pair + step, pairs)],
            plane_in.at[step - 1, w],
            plane_sent.at[w, step - 1],
            plane_got.at[w, step - 1],
            here.across(step),
        )

    for w in range(3):
        give(w).start()
    own_half(0, 0).start()
    query_sum[...] = jnp.zeros_like(query_sum)
    key_sum[...] = jnp.zeros_like(key_sum)
    value_sum[...] = jnp.zeros_like(value_sum)
    for w in range(3):
        give(w).wait_recv()
        for q in range(4):
            own_half(w, q).wait()
            if q < 3:
                own_half(w, q + 1).start()
            elif w < 2:
                own_half(w + 1, 0).start()

            @pl.loop(0, pairs)
            def _(p, w=w, q=q):
                chip_sum[w, q, p] = (chip_sum[w, q, p].astype(f32) + keep_in[q % 2, p].astype(f32)).astype(low)

        for step in range(1, pairs):
            plane_copy(w, step).start()

    for block in range(4):
        stays = here.main & (here.t == block)

        @pl.when(stays)
        def _():
            keep.wait()

        @pl.when(jnp.logical_not(stays))
        def _(block=block):
            remote(of(0), into(block), split_sent.at[0], split_got.at[block], partner).wait_recv()

    for h in range(heads):
        hs = pl.ds(h * dim, dim)
        term[h : h + 1] = jnp.sum(grad[hs].astype(f32) * out[hs].astype(f32), axis=0, keepdims=True)

    def span_of(seq, k, ch):
        block = jnp.where(seq == 0, k, 3 - k)
        return pl.ds(pl.multiple_of(block * rows + ch * part, part), part)

    def piece(k, ch):
        return pl.ds(pl.multiple_of(k * rows + ch * part, part), part)

    def line_rows(ch):
        return pl.ds(ch * part, part)

    def core_copy(k, ch):
        at = span_of(here.g, k, ch)
        return remote(partial.at[at], from_core.at[piece(k, ch)], send_c.at[k, ch], recv_c.at[k, ch], partner)

    def line_copy(k, ch):
        at = span_of(here.g, k, ch)
        return remote(
            partial.at[at],
            from_line.at[piece((k % 3 if isinstance(k, int) else lax.rem(k, 3)), ch)],
            send_z.at[k, ch],
            recv_z.at[k, ch],
            here.device(here.c, jnp.where(here.pos == 0, 1, 0)),
        )

    def home_copy(k, ch):
        at = span_of(here.g, k, ch)
        return remote(
            partial.at[at], rows_grad.at[line_rows(ch)], send_z.at[k, ch], recv_z.at[k, ch], here.device(here.c, k)
        )

    def core_sum(k, ch):
        core_copy(k, ch).wait_recv()
        return partial[span_of(here.g, k, ch)].astype(f32) + from_core[piece(k, ch)].astype(f32)

    def with_line(k, ch):
        line_copy(k, ch).wait_recv()
        return core_sum(k, ch) + from_line[piece((k % 3 if isinstance(k, int) else lax.rem(k, 3)), ch)].astype(f32)

    def pass_on(k):
        for ch in range(CHUNKS):
            partial[span_of(here.g, k, ch)] = core_sum(k, ch).astype(low)
            line_copy(k, ch).start()

    def send_home(k):
        for ch in range(CHUNKS):
            partial[span_of(here.g, k, ch)] = with_line(k, ch).astype(low)
            home_copy(k, ch).start()

    @pl.loop(0, blocks)
    def _(s):
        b = jnp.where(here.g == 0, blocks - 1 - s, s)

        def tile(i, j, diagonal):
            qs = pl.ds(pl.multiple_of(i * TILE, TILE), TILE)
            ks = pl.ds(pl.multiple_of(j * TILE, TILE), TILE)
            if diagonal:
                allowed = readable(span, j * TILE, i * TILE)
            else:
                bias = key_bias(span, j * TILE)
            for h in range(heads):
                hs = pl.ds(h * dim, dim)
                ke = pl.ds(width + h * dim, dim)
                va = pl.ds(2 * width + h * dim, dim)
                scores = dg(qkv[ke, ks], qkv[hs, qs], 0, 0)
                scores = jnp.where(allowed, scores, MASKED) if diagonal else scores + bias
                probs = jnp.exp(scores - logsum[h : h + 1, qs])
                grad_probs = dg(qkv[va, ks], grad[hs, qs], 0, 0)
                grad_scores = (probs * (grad_probs - term[h : h + 1, qs])).astype(low)
                value_sum[hs, ks] += dg(grad[hs, qs], probs.astype(low), 1, 1)
                key_sum[hs, ks] += dg(qkv[hs, qs], grad_scores, 1, 1)
                query_sum[hs, qs] += dg(qkv[ke, ks], grad_scores, 1, 0)

        @pl.loop(0, blocks - 1 - s)
        def _(n):
            tile(jnp.where(here.g == 0, b, b + 1 + n), jnp.where(here.g == 0, n, b), False)

        tile(b, b, True)
        bs = pl.ds(pl.multiple_of(b * TILE, TILE), TILE)
        result[pl.ds(0, width), bs] = (query_sum[:, bs] * factor[...]).astype(low)
        result[pl.ds(width, width), bs] = key_sum[:, bs].astype(low)
        result[pl.ds(2 * width, width), bs] = value_sum[:, bs].astype(low)
        k = blocks - 1 - s
        partial[bs] = dg(result[:, bs], weights[...], 0, 1).astype(low)

        @pl.when(jnp.logical_not(here.main))
        def _():
            for ch in range(CHUNKS):
                core_copy(k, ch).start()

        @pl.when((here.pos == 0) & (s >= 1))
        def _():
            pass_on(k + 1)

        @pl.when((here.pos == 1) & (s >= 2))
        def _():
            send_home(k + 2)

    for w in range(3):
        for step in range(1, pairs):
            plane_copy(w, step).wait_recv()

        @pl.loop(0, 4)
        def _(q, w=w):
            total = chip_sum[w, q, here.pair].astype(f32)
            for step in range(1, pairs):
                total += plane_in[step - 1, w, q].astype(f32)
            plane_sum[q, w] = total.astype(low)

    @pl.when(here.pos == 0)
    def _():
        for ch in range(CHUNKS):
            rows_grad[line_rows(ch)] = with_line(0, ch).astype(low)
        for k in (1, 2, 3):
            for ch in range(CHUNKS):
                line_copy(k, ch).wait_send()

    @pl.when(here.pos == 1)
    def _():
        pass_on(0)
        for ch in range(CHUNKS):
            rows_grad[line_rows(ch)] = with_line(1, ch).astype(low)
        for ch in range(CHUNKS):
            line_copy(0, ch).wait_send()
            for k in (2, 3):
                home_copy(k, ch).wait_send()

    for k in (2, 3):
        @pl.when(here.pos == k)
        def _(k=k):
            for ch in range(CHUNKS):
                remote(
                    partial.at[piece(0, ch)], rows_grad.at[line_rows(ch)], send_z.at[0, ch], recv_z.at[k, ch], partner
                ).wait_recv()

    @pl.when(jnp.logical_not(here.main))
    def _():
        for k in range(4):
            for ch in range(CHUNKS):
                core_copy(k, ch).wait_send()

    for q in range(4):
        @pl.when(jnp.logical_not(here.main & (here.t == q)))
        def _(q=q):
            split_copy(q).wait_send()

    for w in range(3):
        give(w).wait_send()
        for step in range(1, pairs):
            plane_copy(w, step).wait_send()


def attention_backward(span, qkv, out, logsum, factor, weights, split, grad_out, grad_up, grad_down):
    width, slots = out.shape
    heads = logsum.shape[0]
    rows, model = split.shape[1], weights.shape[0]
    low, f32 = qkv.dtype, jnp.float32
    pairs, slice_rows = grad_out.shape[1], grad_out.shape[2]
    columns = model // 2
    vmem = pl.BlockSpec(memory_space=pltpu.VMEM)
    hbm = pl.BlockSpec(memory_space=pl.ANY)
    dma = pltpu.SemaphoreType.DMA
    return pl.pallas_call(
        backward_kernel,
        out_shape=(
            jax.ShapeDtypeStruct(qkv.shape, low),
            jax.ShapeDtypeStruct((rows, model), low),
            jax.ShapeDtypeStruct((4, 3, slice_rows, columns), low),
        ),
        in_specs=[pl.BlockSpec(memory_space=pltpu.SMEM)] + [vmem] * 5 + [hbm] * 4,
        out_specs=(vmem,) * 3,
        scratch_shapes=[
            pltpu.VMEM((width, slots), low),
            pltpu.VMEM((width, slots), f32),
            pltpu.VMEM((width, slots), f32),
            pltpu.VMEM((width, slots), f32),
            pltpu.VMEM((heads, slots), f32),
            pltpu.VMEM((slots, model), low),
            pltpu.VMEM((slots, model), low),
            pltpu.VMEM((3 * rows, model), low),
            pltpu.VMEM((2, pairs, slice_rows, columns), low),
            pltpu.VMEM((3, 4, pairs, slice_rows, columns), low),
            pltpu.VMEM((pairs - 1, 3, 4, slice_rows, columns), low),
            dma((4,)),
            dma((4,)),
            dma,
            dma((2,)),
            dma((3,)),
            dma((3,)),
            dma((3, pairs - 1)),
            dma((3, pairs - 1)),
            dma((4, CHUNKS)),
            dma((4, CHUNKS)),
            dma((4, CHUNKS)),
            dma((4, CHUNKS)),
        ],
        compiler_params=pltpu.CompilerParams(
            collective_id=2, has_side_effects=True, vmem_limit_bytes=60 * 1024 * 1024
        ),
        name="attention_backward",
    )(span, qkv, out, logsum, factor, weights, split, grad_out, grad_up, grad_down)


def weights_kernel(
    mlp, qkv, small, mlp_all, qkv_all, small_all, mlp_in, qkv_in, qkv_swap, small_pair, small_plane, small_line,
    mlp_sent, mlp_got, mlp_spread, mlp_share, mlp_have,
    qkv_sent, qkv_got, qkv_cross, qkv_crossed, qkv_spread, qkv_share, qkv_have,
    small_sent, small_got, plane_sent, plane_got, line_sent, line_got,
):
    here = Place()
    pairs = here.pairs
    pair_barrier(here, plane=True)
    partner = here.partner()
    f32 = jnp.float32

    def mlp_send(step):
        line = lax.rem(here.t + step, 4)
        return remote(
            mlp.at[line], mlp_in.at[step - 1], mlp_sent.at[step - 1], mlp_got.at[step - 1], (here.d, line)
        )

    def qkv_send(step):
        return remote(
            qkv.at[lax.rem(here.pair + step, pairs)],
            qkv_in.at[step - 1],
            qkv_sent.at[step - 1],
            qkv_got.at[step - 1],
            here.across(step),
        )

    small_copy = remote(small, small_pair, small_sent, small_got, partner)
    small_copy.start()
    for step in range(1, pairs):
        qkv_send(step).start()
    for step in range(1, 4):
        mlp_send(step).start()
    small_copy.wait_recv()
    small_plane[here.pair] = small[...] + small_pair[...]

    def small_across(step):
        return remote(
            small_plane.at[here.pair], small_plane.at[here.pair], plane_sent.at[step], plane_got.at[here.pair],
            here.across(step),
        )

    def small_along(step):
        return remote(
            small_line.at[here.t], small_line.at[here.t], line_sent.at[step], line_got.at[here.t],
            (here.d, lax.rem(here.t + step, 4)),
        )

    for step in range(1, pairs):
        small_across(step).start()
    for step in range(1, pairs):
        pair = lax.rem(here.pair + step, pairs)
        remote(
            small_plane.at[pair], small_plane.at[pair], plane_sent.at[0], plane_got.at[pair], partner
        ).wait_recv()
    plane_total = small_plane[0]
    for pair in range(1, pairs):
        plane_total += small_plane[pair]
    small_line[here.t] = plane_total
    for step in range(1, 4):
        small_along(step).start()

    for step in range(1, pairs):
        qkv_send(step).wait_recv()
    total = qkv[here.pair].astype(f32)
    for step in range(1, pairs):
        total += qkv_in[step - 1].astype(f32)
    qkv_swap[0] = total.astype(qkv_swap.dtype)
    line = lax.rem(here.t + 2, 4)
    cross = remote(
        qkv_swap.at[0], qkv_swap.at[1], qkv_cross, qkv_crossed, (here.base + line // 2, line)
    )

    def qkv_piece(step):
        return qkv_all.at[lax.rem(here.pair + step, pairs)]

    def qkv_out(step):
        return remote(
            qkv_all.at[here.pair], qkv_all.at[here.pair], qkv_spread.at[step], qkv_have.at[here.pair],
            here.across(step),
        )

    def qkv_core(step):
        piece = lax.rem(here.pair + step, pairs)
        return remote(
            qkv_all.at[piece], qkv_all.at[piece], qkv_share.at[step], qkv_have.at[piece], partner
        )

    @pl.when(jnp.logical_not(here.main))
    def _():
        cross.start()

    for step in range(1, 4):
        mlp_send(step).wait_recv()
    mlp_total = mlp[here.t].astype(f32)
    for step in range(1, 4):
        mlp_total += mlp_in[step - 1].astype(f32)
    mlp_all[here.d] = mlp_total.astype(mlp_all.dtype)

    def mlp_out(step):
        return remote(
            mlp_all.at[here.d], mlp_all.at[here.d], mlp_spread.at[step], mlp_have.at[here.d],
            here.across(step),
        )

    def mlp_core(step):
        member = 2 * lax.rem(here.pair + step, pairs) + here.c
        return remote(
            mlp_all.at[member], mlp_all.at[member], mlp_share.at[step], mlp_have.at[member], partner
        )

    def mlp_arrived(member):
        remote(
            mlp_all.at[member], mlp_all.at[member], mlp_share.at[0], mlp_have.at[member], partner
        ).wait_recv()

    for step in range(1, pairs):
        mlp_out(step).start()
    mlp_core(0).start()

    @pl.when(here.main)
    def _():
        cross.wait_recv()
        whole = qkv_swap[0].astype(f32) + qkv_swap[1].astype(f32)
        qkv_all[here.pair] = whole.astype(qkv_all.dtype)
        for step in range(1, pairs):
            qkv_out(step).start()
        qkv_core(0).start()

    for step in range(1, pairs):
        mlp_arrived(2 * lax.rem(here.pair + step, pairs) + here.c)
        mlp_core(step).start()

    @pl.when(here.main)
    def _():
        for step in range(1, pairs):
            qkv_core(step).wait_recv()
            qkv_core(step).start()
        for step in range(1, pairs):
            qkv_out(step).wait_send()
        for step in range(pairs):
            qkv_core(step).wait_send()

    @pl.when(jnp.logical_not(here.main))
    def _():
        for step in range(pairs):
            qkv_core(step).wait_recv()
        cross.wait_send()

    for step in range(pairs):
        mlp_arrived(2 * lax.rem(here.pair + step, pairs) + 1 - here.c)
    for step in range(1, 4):
        mlp_send(step).wait_send()
    for step in range(1, pairs):
        qkv_send(step).wait_send()
        mlp_out(step).wait_send()
    for step in range(pairs):
        mlp_core(step).wait_send()
    for step in range(1, 4):
        line = lax.rem(here.t + step, 4)
        remote(small_line.at[line], small_line.at[line], line_sent.at[0], line_got.at[line], partner).wait_recv()
    small_all[...] = (small_line[0] + small_line[1]) + (small_line[2] + small_line[3])
    small_copy.wait_send()
    for step in range(1, pairs):
        small_across(step).wait_send()
    for step in range(1, 4):
        small_along(step).wait_send()


def weight_sums(mlp, qkv, small):
    vmem = pl.BlockSpec(memory_space=pltpu.VMEM)
    low = mlp.dtype
    pairs = qkv.shape[0]
    dma = pltpu.SemaphoreType.DMA
    return pl.pallas_call(
        weights_kernel,
        out_shape=(
            jax.ShapeDtypeStruct((2 * pairs,) + mlp.shape[1:], low),
            jax.ShapeDtypeStruct(qkv.shape, low),
            jax.ShapeDtypeStruct(small.shape, small.dtype),
        ),
        in_specs=[vmem] * 3,
        out_specs=(vmem,) * 3,
        scratch_shapes=[
            pltpu.VMEM((3,) + mlp.shape[1:], low),
            pltpu.VMEM((pairs - 1,) + qkv.shape[1:], low),
            pltpu.VMEM((2,) + qkv.shape[1:], low),
            pltpu.VMEM(small.shape, small.dtype),
            pltpu.VMEM((pairs,) + small.shape, small.dtype),
            pltpu.VMEM((4,) + small.shape, small.dtype),
            dma((3,)),
            dma((3,)),
            dma((pairs,)),
            dma((pairs,)),
            dma((2 * pairs,)),
            dma((pairs - 1,)),
            dma((pairs - 1,)),
            dma,
            dma,
            dma((pairs,)),
            dma((pairs,)),
            dma((pairs,)),
            dma,
            dma,
            dma((pairs,)),
            dma((pairs,)),
            dma((4,)),
            dma((4,)),
        ],
        compiler_params=pltpu.CompilerParams(
            collective_id=3, has_side_effects=True, vmem_limit_bytes=56 * 1024 * 1024
        ),
        name="weight_sums",
    )(mlp, qkv, small)


def per_device(
    inputs,
    cotangent,
    gain_attn,
    gain_mlp,
    query_scale,
    w_query,
    w_key,
    w_value,
    w_out,
    w_up,
    w_down,
    lengths,
    offsets,
):
    low = jnp.bfloat16
    f32 = jnp.float32
    here = Place()
    n_dp = lax.axis_size("dp")
    local_rows, model = inputs.shape
    seq_slots = local_rows * 4
    width_local = w_query.shape[1]
    head_dim = query_scale.shape[0]
    heads_local = width_local // head_dim
    pairs = n_dp // 2
    swap_core = [(i, i ^ 1) for i in range(n_dp)]

    slice_rows = w_out.shape[0] // n_dp
    own_slice = jnp.stack(
        [
            lax.dynamic_slice_in_dim(w_out, here.d * slice_rows, slice_rows, 0),
            jnp.transpose(lax.dynamic_slice_in_dim(w_up, here.d * slice_rows, slice_rows, 1)),
            lax.dynamic_slice_in_dim(w_down, here.d * slice_rows, slice_rows, 0),
        ]
    )
    line_w = lax.all_gather(own_slice, "tensor", axis=0, tiled=False)
    mlp_w = lax.all_gather(line_w, "dp", axis=0, tiled=False)

    def whole_weight(w):
        return jnp.transpose(mlp_w[:, :, w], (1, 0, 2, 3)).reshape(model, model)

    w_out_all, w_up_all, w_down_all = whole_weight(0), whole_weight(1), whole_weight(2)

    own_span = jnp.concatenate([lengths, offsets])
    other_span = lax.ppermute(own_span, "dp", swap_core)
    group_span = jnp.where(here.main, own_span, other_span)
    own_rows = here.t * local_rows + jnp.arange(local_rows, dtype=jnp.int32)
    row_valid = ((own_rows >= offsets[0]) & (own_rows < offsets[0] + lengths[0])).astype(f32)

    residual = inputs.astype(f32)
    normed, inverse_one = rms_forward(residual, gain_attn)
    native_w = jnp.concatenate([w_query, w_key, w_value], axis=1)
    gathered, foreign_w = gather_rows(
        normed.astype(low), native_w.reshape(n_dp, model // n_dp, 3 * width_local)
    )
    stacked_w = jnp.where(here.main, native_w, foreign_w.reshape(model, 3 * width_local))

    scale_const = LOG_TWO_E / math.sqrt(head_dim)
    soft = jax.nn.softplus(query_scale)
    factor = jnp.tile(soft * scale_const, heads_local)[:, None]
    projected = dg(stacked_w, gathered, 0, 1)
    qkv = (projected * jnp.concatenate([factor, jnp.ones((2 * width_local, 1), f32)])).astype(low)
    attended, logsum, attended_rows = attention_forward(group_span, qkv, heads_local)

    hidden_one = residual + contract_rows(attended_rows, w_out_all)
    second, inverse_two = rms_forward(hidden_one, gain_mlp)
    second_low = second.astype(low)
    before_act = contract_cols(second_low, w_up_all)
    activated = jax.nn.silu(before_act).astype(low)
    output = hidden_one + jnp.dot(activated, w_down_all, preferred_element_type=f32)
    grad_hidden_out = cotangent.astype(f32) * row_valid[:, None]
    grad_low = grad_hidden_out.astype(low)
    grad_act = contract_cols(grad_low, w_down_all)
    grad_pre = (grad_act * silu_slope(before_act)).astype(low)
    grad_second = jnp.dot(grad_pre, w_up_all, preferred_element_type=f32)
    grad_hidden = grad_hidden_out + rms_backward(hidden_one, inverse_two, gain_mlp, grad_second)
    branch_low = grad_hidden.astype(low)
    grad_att_rows = contract_cols(w_out_all, branch_low).astype(low)

    grad_w_down = contract_rows(activated, grad_low)
    grad_w_up_t = contract_rows(grad_pre, second_low)
    grad_w_out = jnp.dot(attended_rows, branch_low, preferred_element_type=f32)
    gain_two_part = jnp.sum(grad_w_up_t * w_up_all.astype(f32), axis=0)

    def by_member(grad):
        return grad.astype(low).reshape(4, pairs, width_local // pairs, model)

    grad_stacked, grad_first, plane_sum = attention_backward(
        group_span, qkv, attended, logsum, factor, stacked_w, grad_att_rows,
        by_member(grad_w_out), by_member(grad_w_up_t), by_member(grad_w_down),
    )
    grad_stacked_w = dg(gathered, grad_stacked, 0, 1)
    weighted = grad_stacked_w * stacked_w.astype(f32)
    gain_one_part = jnp.sum(weighted, axis=1)
    scale_part = jnp.sum(
        jnp.sum(weighted[:, :width_local], axis=0).reshape(heads_local, head_dim), axis=0
    )
    small = jnp.concatenate([gain_one_part, gain_two_part, scale_part])
    lanes = 128
    small = jnp.pad(small, (0, -small.size % (8 * lanes))).reshape(-1, lanes)
    mlp_all, qkv_all, small = weight_sums(
        plane_sum,
        grad_stacked_w.astype(low).reshape(pairs, model // pairs, 3 * width_local),
        small,
    )
    small = small.reshape(-1)
    grad_input = grad_hidden + rms_backward(
        residual, inverse_one, gain_attn, grad_first.astype(f32)
    )
    grad_gain_one = small[:model] / gain_attn
    grad_gain_two = small[model : 2 * model] / gain_mlp
    grad_scale = small[2 * model : 2 * model + head_dim] * jax.nn.sigmoid(query_scale) / soft
    mlp_all = mlp_all.astype(f32).reshape(pairs, 2, 3, width_local // pairs, model // 2)

    def final_weight(w):
        return jnp.transpose(mlp_all[:, :, w], (0, 2, 1, 3)).reshape(width_local, model)

    grad_out_final = final_weight(0)
    grad_up_final = jnp.transpose(final_weight(1))
    grad_down_final = final_weight(2)
    qkv_all = qkv_all.astype(f32).reshape(model, 3 * width_local)
    return (
        output.astype(low),
        grad_input,
        grad_gain_one,
        grad_gain_two,
        grad_scale,
        qkv_all[:, :width_local],
        qkv_all[:, width_local : 2 * width_local],
        qkv_all[:, 2 * width_local :],
        grad_out_final,
        grad_up_final,
        grad_down_final,
    )


def solution(mesh):
    rows = P(("dp", "tensor"), None)
    cols_t = P(None, "tensor")
    rows_t = P("tensor", None)
    return jax.shard_map(
        per_device,
        mesh=mesh,
        in_specs=(
            rows, rows, P(), P(), P(), cols_t, cols_t, cols_t, rows_t, cols_t, rows_t, P("dp"), P("dp"),
        ),
        out_specs=(
            rows, rows, P(), P(), P(), cols_t, cols_t, cols_t, rows_t, cols_t, rows_t,
        ),
        check_vma=False,
    )
```

```python
import functools
import math

import jax
import jax.numpy as jnp
from jax import lax
from jax.experimental import pallas as pl
from jax.experimental.pallas import tpu as pltpu
from jax.sharding import PartitionSpec as P

EPSILON = 1e-06
LOG_TWO_E = 1.4426950408889634
MESH_ID = pl.DeviceIdType.MESH
CHUNKS = 4


def rms_forward(values, gain):
    inverse = lax.rsqrt(jnp.mean(values * values, axis=-1, keepdims=True) + EPSILON)
    return (values * inverse * gain, inverse)


def rms_backward(values, inverse, gain, grad_normed):
    scaled = values * inverse
    grad_scaled = grad_normed * gain
    return inverse * (
        grad_scaled - scaled * jnp.mean(grad_scaled * scaled, axis=-1, keepdims=True)
    )


def contract_rows(left, right):
    return lax.dot_general(
        left, right, (((0,), (0,)), ((), ())), preferred_element_type=jnp.float32
    )


def contract_cols(left, right):
    return lax.dot_general(
        left, right, (((1,), (1,)), ((), ())), preferred_element_type=jnp.float32
    )


def silu_slope(values):
    sigmoid_v = jax.nn.sigmoid(values)
    return sigmoid_v * (1.0 + values * (1.0 - sigmoid_v))


class Place:
    def __init__(self):
        self.d = lax.axis_index("dp")
        self.t = lax.axis_index("tensor")
        self.c = lax.rem(self.d, 2)
        self.g = self.t // 2
        self.base = self.d - self.c
        self.pairs = lax.axis_size("dp") // 2
        self.pair = self.d // 2
        self.main = self.c == self.g
        self.pos = jnp.where(self.c == 0, self.t, 3 - self.t)

    def device(self, seq, pos):
        return (self.base + seq, jnp.where(seq == 0, pos, 3 - pos))

    def across(self, step):
        return (2 * lax.rem(self.pair + step, self.pairs) + self.c, self.t)

    def partner(self):
        return (self.base + 1 - self.c, self.t)

    def quarter(self):
        return jnp.where(self.main, self.t, lax.rem(self.t + 2, 4))


def pair_barrier(here, plane=False):
    barrier = pltpu.get_barrier_semaphore()
    others = []
    for step in range(1, 8):
        code = lax.rem(here.c * 4 + here.t + step, 8)
        others.append((here.base + code // 4, lax.rem(code, 4)))
    if plane:
        others += [here.across(step) for step in range(1, here.pairs)]
    for device in others:
        pl.semaphore_signal(barrier, inc=1, device_id=device, device_id_type=MESH_ID)
    pl.semaphore_wait(barrier, len(others))


def remote(src, dst, send, recv, device):
    return pltpu.make_async_remote_copy(
        src_ref=src, dst_ref=dst, send_sem=send, recv_sem=recv, device_id=device, device_id_type=MESH_ID
    )


def gather_kernel(
    own, native, out, foreign, send_z, send_c, recv, local_sem, send_w, spread_w, recv_w
):
    here = Place()
    rows = own.shape[0]
    part = rows // CHUNKS
    pair_barrier(here, plane=True)
    partner = here.partner()
    members = native.shape[0]
    line = lax.rem(here.t + 2, 4)
    weight_copy = remote(
        native.at[here.d],
        foreign.at[here.d],
        send_w,
        recv_w.at[here.d],
        (here.base + 1 - line // 2, line),
    )
    weight_copy.start()

    def weight_arrived(member):
        remote(native.at[0], foreign.at[member], send_w, recv_w.at[member], partner).wait_recv()

    def spread(core, step):
        member = here.base + core
        return remote(
            foreign.at[member],
            foreign.at[member],
            spread_w.at[core, step],
            recv_w.at[member],
            here.across(step),
        )

    def place(seq, k, ch):
        block = jnp.where(seq == 0, k, 3 - k)
        return out.at[pl.ds(pl.multiple_of(block * rows + ch * part, part), part)]

    def own_part(ch):
        return own.at[pl.ds(ch * part, part)]

    def copy(src, k, ch, seq, device, send):
        return remote(src, place(seq, k, ch), send.at[k, ch], recv.at[k, ch], device)

    def arrived(k, ch, seq):
        copy(place(seq, k, ch), k, ch, seq, partner, send_z).wait_recv()

    for k in (2, 3):
        @pl.when(here.pos == k)
        def _(k=k):
            target = here.device(here.c, 1)
            for ch in range(CHUNKS):
                copy(own_part(ch), k, ch, here.c, target, send_z).start()
            for core in range(2):
                weight_arrived(here.base + core)
                for step in range(1, here.pairs):
                    spread(core, step).start()
            for step in range(1, here.pairs):
                for core in range(2):
                    weight_arrived(2 * lax.rem(here.pair + step, here.pairs) + core)
            for ch in range(CHUNKS):
                for kk in range(4):
                    arrived(kk, ch, 1 - here.c)
            for ch in range(CHUNKS):
                copy(own_part(ch), k, ch, here.c, target, send_z).wait_send()
            for core in range(2):
                for step in range(1, here.pairs):
                    spread(core, step).wait_send()

    def keep(k):
        return pltpu.make_async_copy(
            own, out.at[pl.ds(pl.multiple_of(jnp.where(here.c == 0, k, 3 - k) * rows, rows), rows)], local_sem
        )

    @pl.when(here.pos == 1)
    def _():
        seq = here.c
        near = here.device(seq, 0)
        sent = []

        def send(src, k, ch, device, sem):
            copy(src, k, ch, seq, device, sem).start()
            sent.append((src, k, ch, device, sem))

        keep(1).start()
        for ch in range(CHUNKS):
            send(own_part(ch), 1, ch, near, send_z)
            send(own_part(ch), 1, ch, partner, send_c)
        for ch in range(CHUNKS):
            for k in (2, 3):
                arrived(k, ch, seq)
                send(place(seq, k, ch), k, ch, near, send_z)
                send(place(seq, k, ch), k, ch, partner, send_c)
            arrived(0, ch, seq)
            send(place(seq, 0, ch), 0, ch, partner, send_c)
        for src, k, ch, device, sem in sent:
            copy(src, k, ch, seq, device, sem).wait_send()
        keep(1).wait()

    @pl.when(here.pos == 0)
    def _():
        seq = here.c
        far = here.device(seq, 1)
        sent = []

        def send(src, k, ch, device, sem):
            copy(src, k, ch, seq, device, sem).start()
            sent.append((src, k, ch, device, sem))

        keep(0).start()
        for ch in range(CHUNKS):
            send(own_part(ch), 0, ch, far, send_z)
            send(own_part(ch), 0, ch, partner, send_c)
        for ch in range(CHUNKS):
            arrived(1, ch, seq)
            send(place(seq, 1, ch), 1, ch, partner, send_c)
        for ch in range(CHUNKS):
            for k in (2, 3):
                arrived(k, ch, seq)
                send(place(seq, k, ch), k, ch, partner, send_c)
        for src, k, ch, device, sem in sent:
            copy(src, k, ch, seq, device, sem).wait_send()
        keep(0).wait()

    weight_copy.wait_send()


def gather_rows(own, native):
    rows, width = own.shape
    members = native.shape[0]
    hbm = pl.BlockSpec(memory_space=pl.ANY)
    return pl.pallas_call(
        gather_kernel,
        out_shape=(
            jax.ShapeDtypeStruct((4 * rows, width), own.dtype),
            jax.ShapeDtypeStruct(native.shape, native.dtype),
        ),
        in_specs=[hbm, hbm],
        out_specs=(hbm, hbm),
        scratch_shapes=[
            pltpu.SemaphoreType.DMA((4, CHUNKS)),
            pltpu.SemaphoreType.DMA((4, CHUNKS)),
            pltpu.SemaphoreType.DMA((4, CHUNKS)),
            pltpu.SemaphoreType.DMA,
            pltpu.SemaphoreType.DMA,
            pltpu.SemaphoreType.DMA((2, members // 2)),
            pltpu.SemaphoreType.DMA((members,)),
        ],
        compiler_params=pltpu.CompilerParams(collective_id=0, has_side_effects=True),
        name="gather_rows",
    )(own, native)


def dg(left, right, left_dim, right_dim):
    return lax.dot_general(
        left, right, (((left_dim,), (right_dim,)), ((), ())), preferred_element_type=jnp.float32
    )


TILE = 512
MASKED = -1e30


def readable(span, first_key, first_query):
    shape = (TILE, TILE)
    key = first_key + lax.broadcasted_iota(jnp.int32, shape, 0)
    query = first_query + lax.broadcasted_iota(jnp.int32, shape, 1)
    valid = (key >= span[1]) & (key < span[1] + span[0])
    return (valid & (key <= query)) | (key == query)


def key_bias(span, first_key):
    key = first_key + lax.broadcasted_iota(jnp.int32, (TILE, 1), 0)
    return jnp.where((key >= span[1]) & (key < span[1] + span[0]), 0.0, MASKED)


def forward_kernel(span, qkv, out, logsum, rows_out, highest, summed, total, send, recv, local_sem):
    heads = logsum.shape[0]
    width, slots = out.shape
    dim = width // heads
    here = Place()
    pair_barrier(here)
    quarter = here.quarter()

    def into(q):
        return rows_out.at[pl.ds(pl.multiple_of(q * width, width), width)]

    def columns(i):
        return out.at[:, pl.ds(pl.multiple_of(i * TILE, TILE), TILE)]

    def copy(i):
        return remote(columns(i), into(quarter), send.at[i], recv.at[quarter], (here.base + here.g, i))

    keep = pltpu.make_async_copy(columns(here.t), into(here.t), local_sem)

    @pl.loop(0, slots // TILE)
    def _(s):
        i = slots // TILE - 1 - s
        qs = pl.ds(pl.multiple_of(i * TILE, TILE), TILE)
        highest[...] = jnp.full_like(highest, MASKED)
        summed[...] = jnp.zeros_like(summed)
        total[...] = jnp.zeros_like(total)

        def tile(j, diagonal):
            ks = pl.ds(pl.multiple_of(j * TILE, TILE), TILE)
            if diagonal:
                allowed = readable(span, j * TILE, i * TILE)
            else:
                bias = key_bias(span, j * TILE)
            for h in range(heads):
                hs = pl.ds(h * dim, dim)
                scores = dg(qkv[pl.ds(width + h * dim, dim), ks], qkv[hs, qs], 0, 0)
                scores = jnp.where(allowed, scores, MASKED) if diagonal else scores + bias
                before = highest[h : h + 1]
                after = jnp.maximum(before, jnp.max(scores, axis=0, keepdims=True))
                expo = jnp.exp(scores - after)
                scale = jnp.exp(before - after)
                summed[h : h + 1] = summed[h : h + 1] * scale + jnp.sum(expo, axis=0, keepdims=True)
                highest[h : h + 1] = after
                total[hs] = total[hs] * scale + dg(
                    qkv[pl.ds(2 * width + h * dim, dim), ks], expo.astype(qkv.dtype), 1, 0
                )

        @pl.loop(0, i)
        def _(j):
            tile(j, False)

        tile(i, True)
        for h in range(heads):
            hs = pl.ds(h * dim, dim)
            out[hs, qs] = (total[hs] / summed[h : h + 1]).astype(out.dtype)
            logsum[h : h + 1, qs] = highest[h : h + 1] + jnp.log(summed[h : h + 1])
        stays = here.main & (here.t == i)

        @pl.when(stays)
        def _():
            keep.start()

        @pl.when(jnp.logical_not(stays))
        def _():
            copy(i).start()

    for block in range(4):
        stays = here.main & (here.t == block)

        @pl.when(stays)
        def _():
            keep.wait()

        @pl.when(jnp.logical_not(stays))
        def _(block=block):
            copy(block).wait_send()
            remote(columns(0), into(block), send.at[0], recv.at[block], here.partner()).wait_recv()


def attention_forward(span, qkv, heads):
    width, slots = qkv.shape[0] // 3, qkv.shape[1]
    vmem = pl.BlockSpec(memory_space=pltpu.VMEM)
    return pl.pallas_call(
        forward_kernel,
        out_shape=(
            jax.ShapeDtypeStruct((width, slots), qkv.dtype),
            jax.ShapeDtypeStruct((heads, slots), jnp.float32),
            jax.ShapeDtypeStruct((4 * width, slots // 4), qkv.dtype),
        ),
        in_specs=[pl.BlockSpec(memory_space=pltpu.SMEM), vmem],
        out_specs=(vmem, vmem, pl.BlockSpec(memory_space=pl.ANY)),
        scratch_shapes=[
            pltpu.VMEM((heads, TILE), jnp.float32),
            pltpu.VMEM((heads, TILE), jnp.float32),
            pltpu.VMEM((width, TILE), jnp.float32),
            pltpu.SemaphoreType.DMA((4,)),
            pltpu.SemaphoreType.DMA((4,)),
            pltpu.SemaphoreType.DMA,
        ],
        compiler_params=pltpu.CompilerParams(
            collective_id=1, has_side_effects=True, vmem_limit_bytes=50 * 1024 * 1024
        ),
        name="attention_forward",
    )(span, qkv)


def backward_kernel(
    span, qkv, out, logsum, factor, weights, small, split, grad_out, grad_up, grad_down, gathered,
    rows_grad, mlp_all, qkv_all, small_all,
    result, grad, query_sum, key_sum, value_sum, term,
    partial, from_core, from_line, keep_in, chip_sum, plane_in,
    normed, weight_grad, qkv_in, qkv_swap, mlp_in, mlp_sum,
    small_own, small_pair, small_plane, small_line,
    split_sent, split_got, local_sem, keep_sem,
    give_sent, give_got, plane_sent, plane_got,
    send_c, send_z, recv_c, recv_z,
    out_sem, normed_sem, qkv_sent, qkv_got, cross_sent, cross_got, qkv_spread, qkv_share, qkv_have, qkv_local,
    line_sent, line_got, mlp_spread, mlp_share, mlp_have, mlp_local,
    small_sems, small_across_sent, small_across_got, small_along_sent, small_along_got,
):
    heads = logsum.shape[0]
    width, slots = out.shape
    dim = width // heads
    low, f32 = qkv.dtype, jnp.float32
    here = Place()
    pairs = here.pairs
    rows = split.shape[1]
    part = rows // CHUNKS
    partner = here.partner()
    pair_barrier(here, plane=True)
    blocks = slots // TILE

    def of(q):
        return split.at[pl.ds(pl.multiple_of(q * width, width), width)]

    def into(block):
        return grad.at[:, pl.ds(pl.multiple_of(block * rows, rows), rows)]

    def split_copy(q):
        native = (q // 2) == here.c
        seq = jnp.where(native, here.c, 1 - here.c)
        line = jnp.where(native, q, (q + 2) % 4)
        return remote(of(q), into(here.t), split_sent.at[q], split_got.at[here.t], (here.base + seq, line))

    keep = pltpu.make_async_copy(of(here.t), into(here.t), local_sem)
    for q in range(4):
        stays = here.main & (here.t == q)

        @pl.when(stays)
        def _():
            keep.start()

        @pl.when(jnp.logical_not(stays))
        def _(q=q):
            split_copy(q).start()

    sources = (grad_out, grad_up, grad_down)
    columns = chip_sum.shape[-1]

    def half(core):
        return pl.ds(pl.multiple_of(core * columns, columns), columns)

    def give(w):
        return remote(
            sources[w].at[:, :, :, half(1 - here.c)], chip_sum.at[w], give_sent.at[w], give_got.at[w], partner
        )

    def own_half(w, q):
        slot = (4 * w + q) % 2
        return pltpu.make_async_copy(
            sources[w].at[q, :, :, half(here.c)], keep_in.at[slot], keep_sem.at[slot]
        )

    def plane_copy(w, step):
        return remote(
            chip_sum.at[w, :, lax.rem(here.pair + step, pairs)],
            plane_in.at[step - 1, w],
            plane_sent.at[w, step - 1],
            plane_got.at[w, step - 1],
            here.across(step),
        )

    for w in range(3):
        give(w).start()
    own_half(0, 0).start()
    out_copy = pltpu.make_async_copy(out, result.at[pl.ds(0, width)], out_sem)
    out_copy.start()
    query_sum[...] = jnp.zeros_like(query_sum)
    key_sum[...] = jnp.zeros_like(key_sum)
    value_sum[...] = jnp.zeros_like(value_sum)
    for w in range(3):
        give(w).wait_recv()
        for q in range(4):
            own_half(w, q).wait()
            if q < 3:
                own_half(w, q + 1).start()
            elif w < 2:
                own_half(w + 1, 0).start()

            @pl.loop(0, pairs)
            def _(p, w=w, q=q):
                chip_sum[w, q, p] = (chip_sum[w, q, p].astype(f32) + keep_in[q % 2, p].astype(f32)).astype(low)

        for step in range(1, pairs):
            plane_copy(w, step).start()

    for block in range(4):
        stays = here.main & (here.t == block)

        @pl.when(stays)
        def _():
            keep.wait()

        @pl.when(jnp.logical_not(stays))
        def _(block=block):
            remote(of(0), into(block), split_sent.at[0], split_got.at[block], partner).wait_recv()

    out_copy.wait()
    for h in range(heads):
        hs = pl.ds(h * dim, dim)
        term[h : h + 1] = jnp.sum(grad[hs].astype(f32) * result[hs].astype(f32), axis=0, keepdims=True)

    def span_of(seq, k, ch):
        block = jnp.where(seq == 0, k, 3 - k)
        return pl.ds(pl.multiple_of(block * rows + ch * part, part), part)

    def piece(k, ch):
        return pl.ds(pl.multiple_of(k * rows + ch * part, part), part)

    def line_piece(k, ch):
        return piece(k % 3 if isinstance(k, int) else lax.rem(k, 3), ch)

    def line_rows(ch):
        return pl.ds(ch * part, part)

    def core_copy(k, ch):
        at = span_of(here.g, k, ch)
        return remote(partial.at[at], from_core.at[piece(k, ch)], send_c.at[k, ch], recv_c.at[k, ch], partner)

    def line_copy(k, ch):
        at = span_of(here.g, k, ch)
        return remote(
            partial.at[at],
            from_line.at[line_piece(k, ch)],
            send_z.at[k, ch],
            recv_z.at[k, ch],
            here.device(here.c, jnp.where(here.pos == 0, 1, 0)),
        )

    def home_copy(k, ch):
        at = span_of(here.g, k, ch)
        return remote(
            partial.at[at], rows_grad.at[line_rows(ch)], send_z.at[k, ch], recv_z.at[k, ch], here.device(here.c, k)
        )

    def core_sum(k, ch):
        core_copy(k, ch).wait_recv()
        return partial[span_of(here.g, k, ch)].astype(f32) + from_core[piece(k, ch)].astype(f32)

    def with_line(k, ch):
        line_copy(k, ch).wait_recv()
        return core_sum(k, ch) + from_line[line_piece(k, ch)].astype(f32)

    def pass_on(k):
        for ch in range(CHUNKS):
            partial[span_of(here.g, k, ch)] = core_sum(k, ch).astype(low)
            line_copy(k, ch).start()

    def send_home(k):
        for ch in range(CHUNKS):
            partial[span_of(here.g, k, ch)] = with_line(k, ch).astype(low)
            home_copy(k, ch).start()

    @pl.loop(0, blocks)
    def _(s):
        b = jnp.where(here.g == 0, blocks - 1 - s, s)
        k = blocks - 1 - s

        def tile(i, j, diagonal):
            qs = pl.ds(pl.multiple_of(i * TILE, TILE), TILE)
            ks = pl.ds(pl.multiple_of(j * TILE, TILE), TILE)
            if diagonal:
                allowed = readable(span, j * TILE, i * TILE)
            else:
                bias = key_bias(span, j * TILE)
            for h in range(heads):
                hs = pl.ds(h * dim, dim)
                ke = pl.ds(width + h * dim, dim)
                va = pl.ds(2 * width + h * dim, dim)
                scores = dg(qkv[ke, ks], qkv[hs, qs], 0, 0)
                scores = jnp.where(allowed, scores, MASKED) if diagonal else scores + bias
                probs = jnp.exp(scores - logsum[h : h + 1, qs])
                grad_probs = dg(qkv[va, ks], grad[hs, qs], 0, 0)
                grad_scores = (probs * (grad_probs - term[h : h + 1, qs])).astype(low)
                value_sum[hs, ks] += dg(grad[hs, qs], probs.astype(low), 1, 1)
                key_sum[hs, ks] += dg(qkv[hs, qs], grad_scores, 1, 1)
                query_sum[hs, qs] += dg(qkv[ke, ks], grad_scores, 1, 0)

        tile(b, b, True)

        @pl.when((here.pos == 0) & (s >= 1))
        def _():
            pass_on(k + 1)

        @pl.loop(0, blocks - 1 - s)
        def _(n):
            tile(jnp.where(here.g == 0, b, b + 1 + n), jnp.where(here.g == 0, n, b), False)

        bs = pl.ds(pl.multiple_of(b * TILE, TILE), TILE)
        result[pl.ds(0, width), bs] = (query_sum[:, bs] * factor[...]).astype(low)
        result[pl.ds(width, width), bs] = key_sum[:, bs].astype(low)
        result[pl.ds(2 * width, width), bs] = value_sum[:, bs].astype(low)
        partial[bs] = dg(result[:, bs], weights[...], 0, 1).astype(low)

        @pl.when(jnp.logical_not(here.main))
        def _():
            for ch in range(CHUNKS):
                core_copy(k, ch).start()

    @pl.when(here.pos == 1)
    def _():
        send_home(3)

    chunks, _, share, _ = weight_grad.shape
    depth = pairs * share

    half_slots = slots // 2

    def load(i, part_of):
        return pltpu.make_async_copy(
            gathered.at[
                pl.ds(part_of * half_slots, half_slots), pl.ds(pl.multiple_of(i * depth, depth), depth)
            ],
            normed.at[part_of],
            normed_sem.at[part_of],
        )

    def qkv_send(i, step):
        return remote(
            weight_grad.at[i, lax.rem(here.pair + step, pairs)],
            qkv_in.at[i, step - 1],
            qkv_sent.at[i, step - 1],
            qkv_got.at[i, step - 1],
            here.across(step),
        )

    small_own[...] = small[...]
    load(0, 0).start()
    load(0, 1).start()

    @pl.loop(0, chunks)
    def _(i):
        at = pl.ds(pl.multiple_of(i * depth, depth), depth)
        load(i, 0).wait()
        grads = dg(normed[0], result[:, :half_slots], 0, 1)

        @pl.when(i + 1 < chunks)
        def _():
            load(i + 1, 0).start()

        load(i, 1).wait()
        grads += dg(normed[1], result[:, half_slots:], 0, 1)

        @pl.when(i + 1 < chunks)
        def _():
            load(i + 1, 1).start()

        for p in range(pairs):
            weight_grad[i, p] = grads[p * share : (p + 1) * share].astype(low)
        for step in range(1, pairs):
            qkv_send(i, step).start()
        weighted = grads * weights[at].astype(f32)
        by_row = jnp.sum(weighted, axis=1, keepdims=True)
        small_own[0:1, at] = jnp.transpose(jnp.broadcast_to(by_row, (depth, 128)))[0:1]
        small_own[2:3, pl.ds(0, 3 * width)] += jnp.sum(weighted, axis=0, keepdims=True)

    small_copy = remote(small_own, small_pair, small_sems.at[0], small_sems.at[1], partner)
    small_copy.start()

    def mlp_line(step):
        line = lax.rem(here.t + step, 4)
        return remote(
            chip_sum.at[:, line, here.pair], mlp_in.at[step - 1], line_sent.at[step - 1], line_got.at[step - 1],
            (here.d, line),
        )

    for w in range(3):
        for step in range(1, pairs):
            plane_copy(w, step).wait_recv()

        @pl.loop(0, 4)
        def _(q, w=w):
            total = chip_sum[w, q, here.pair].astype(f32)
            for step in range(1, pairs):
                total += plane_in[step - 1, w, q].astype(f32)
            chip_sum[w, q, here.pair] = total.astype(low)

    for step in range(1, 4):
        mlp_line(step).start()

    @pl.when(here.pos == 1)
    def _():
        pass_on(0)
        send_home(2)

    line = lax.rem(here.t + 2, 4)

    def cross(i):
        return remote(
            qkv_swap.at[0, i], qkv_swap.at[1, i], cross_sent.at[i], cross_got.at[i],
            (here.base + line // 2, line),
        )

    def qkv_out(i, step):
        return remote(
            qkv_swap.at[0, i], qkv_all.at[i, here.pair], qkv_spread.at[i, step], qkv_have.at[i, here.pair],
            here.across(step),
        )

    def qkv_own(i):
        return remote(
            qkv_swap.at[0, i], qkv_all.at[i, here.pair], qkv_share.at[i, 0], qkv_have.at[i, here.pair], partner
        )

    def qkv_keep(i):
        return pltpu.make_async_copy(qkv_swap.at[0, i], qkv_all.at[i, here.pair], qkv_local.at[i])

    def qkv_core(i, step):
        pair = lax.rem(here.pair + step, pairs)
        return remote(
            qkv_all.at[i, pair], qkv_all.at[i, pair], qkv_share.at[i, step], qkv_have.at[i, pair], partner
        )

    def finish(i):
        @pl.when(here.main)
        def _():
            cross(i).wait_recv()
            qkv_swap[0, i] = (qkv_swap[0, i].astype(f32) + qkv_swap[1, i].astype(f32)).astype(low)
            qkv_keep(i).start()
            for step in range(1, pairs):
                qkv_out(i, step).start()
            qkv_own(i).start()

    @pl.loop(0, chunks)
    def _(i):
        total = weight_grad[i, here.pair].astype(f32)
        for step in range(1, pairs):
            qkv_send(i, step).wait_recv()
            total += qkv_in[i, step - 1].astype(f32)
        qkv_swap[0, i] = total.astype(low)

        @pl.when(jnp.logical_not(here.main))
        def _():
            cross(i).start()

        @pl.when(i >= 1)
        def _():
            finish(i - 1)

    finish(chunks - 1)

    small_copy.wait_recv()
    small_plane[here.pair] = small_own[...] + small_pair[...]

    def small_across(step):
        return remote(
            small_plane.at[here.pair], small_plane.at[here.pair], small_across_sent.at[step],
            small_across_got.at[here.pair], here.across(step),
        )

    def small_along(step):
        return remote(
            small_line.at[here.t], small_line.at[here.t], small_along_sent.at[step], small_along_got.at[here.t],
            (here.d, lax.rem(here.t + step, 4)),
        )

    for step in range(1, pairs):
        small_across(step).start()

    for step in range(1, 4):
        mlp_line(step).wait_recv()
    mlp_total = chip_sum[:, here.t, here.pair].astype(f32)
    for step in range(1, 4):
        mlp_total += mlp_in[step - 1].astype(f32)
    mlp_sum[...] = mlp_total.astype(low)

    def mlp_out(step):
        return remote(
            mlp_sum, mlp_all.at[here.d], mlp_spread.at[step], mlp_have.at[here.d], here.across(step)
        )

    mlp_own = remote(mlp_sum, mlp_all.at[here.d], mlp_share.at[0], mlp_have.at[here.d], partner)
    mlp_keep = pltpu.make_async_copy(mlp_sum, mlp_all.at[here.d], mlp_local)

    def mlp_core(step):
        member = 2 * lax.rem(here.pair + step, pairs) + here.c
        return remote(
            mlp_all.at[member], mlp_all.at[member], mlp_share.at[step], mlp_have.at[member], partner
        )

    def mlp_arrived(member):
        remote(mlp_sum, mlp_all.at[member], mlp_share.at[0], mlp_have.at[member], partner).wait_recv()

    for step in range(1, pairs):
        mlp_out(step).start()
    mlp_own.start()
    mlp_keep.start()

    for step in range(1, pairs):
        pair = lax.rem(here.pair + step, pairs)
        remote(
            small_own, small_plane.at[pair], small_across_sent.at[0], small_across_got.at[pair], partner
        ).wait_recv()
    plane_total = small_plane[0]
    for pair in range(1, pairs):
        plane_total += small_plane[pair]
    small_line[here.t] = plane_total
    for step in range(1, 4):
        small_along(step).start()

    @pl.when(here.pos == 0)
    def _():
        for ch in range(CHUNKS):
            rows_grad[line_rows(ch)] = with_line(0, ch).astype(low)
        for k in (1, 2, 3):
            for ch in range(CHUNKS):
                line_copy(k, ch).wait_send()

    @pl.when(here.pos == 1)
    def _():
        for ch in range(CHUNKS):
            rows_grad[line_rows(ch)] = with_line(1, ch).astype(low)
        for ch in range(CHUNKS):
            line_copy(0, ch).wait_send()
            for k in (2, 3):
                home_copy(k, ch).wait_send()

    for k in (2, 3):
        @pl.when(here.pos == k)
        def _(k=k):
            for ch in range(CHUNKS):
                remote(
                    partial.at[piece(0, ch)], rows_grad.at[line_rows(ch)], send_z.at[0, ch], recv_z.at[k, ch], partner
                ).wait_recv()

    for step in range(1, 4):
        other = lax.rem(here.t + step, 4)
        remote(
            small_own, small_line.at[other], small_along_sent.at[0], small_along_got.at[other], partner
        ).wait_recv()
    small_all[...] = (small_line[0] + small_line[1]) + (small_line[2] + small_line[3])

    @pl.when(here.main)
    def _():
        @pl.loop(0, chunks)
        def _(i):
            for step in range(1, pairs):
                qkv_core(i, step).wait_recv()
                qkv_core(i, step).start()

    for step in range(1, pairs):
        mlp_arrived(2 * lax.rem(here.pair + step, pairs) + here.c)
        mlp_core(step).start()

    @pl.when(here.main)
    def _():
        @pl.loop(0, chunks)
        def _(i):
            qkv_keep(i).wait()
            qkv_own(i).wait_send()
            for step in range(1, pairs):
                qkv_out(i, step).wait_send()
                qkv_core(i, step).wait_send()

    @pl.when(jnp.logical_not(here.main))
    def _():
        @pl.loop(0, chunks)
        def _(i):
            cross(i).wait_send()
            for step in range(pairs):
                qkv_core(i, step).wait_recv()

        for k in range(4):
            for ch in range(CHUNKS):
                core_copy(k, ch).wait_send()

    for step in range(pairs):
        mlp_arrived(2 * lax.rem(here.pair + step, pairs) + 1 - here.c)
    mlp_keep.wait()
    mlp_own.wait_send()

    for q in range(4):
        @pl.when(jnp.logical_not(here.main & (here.t == q)))
        def _(q=q):
            split_copy(q).wait_send()

    for w in range(3):
        give(w).wait_send()
        for step in range(1, pairs):
            plane_copy(w, step).wait_send()

    @pl.loop(0, chunks)
    def _(i):
        for step in range(1, pairs):
            qkv_send(i, step).wait_send()

    for step in range(1, pairs):
        mlp_out(step).wait_send()
        mlp_core(step).wait_send()
        small_across(step).wait_send()
    for step in range(1, 4):
        mlp_line(step).wait_send()
        small_along(step).wait_send()
    small_copy.wait_send()


DEPTH = 256


def attention_backward(
    span, qkv, out, logsum, factor, weights, small, split, grad_out, grad_up, grad_down, gathered
):
    width, slots = out.shape
    heads = logsum.shape[0]
    rows, model = split.shape[1], weights.shape[0]
    low, f32 = qkv.dtype, jnp.float32
    pairs, slice_rows = grad_out.shape[1], grad_out.shape[2]
    columns = model // 2
    chunks, share = model // DEPTH, DEPTH // pairs
    vmem = pl.BlockSpec(memory_space=pltpu.VMEM)
    hbm = pl.BlockSpec(memory_space=pl.ANY)
    dma = pltpu.SemaphoreType.DMA
    buffer = pltpu.VMEM
    return pl.pallas_call(
        backward_kernel,
        out_shape=(
            jax.ShapeDtypeStruct((rows, model), low),
            jax.ShapeDtypeStruct((2 * pairs, 3, slice_rows, columns), low),
            jax.ShapeDtypeStruct((chunks, pairs, share, 3 * width), low),
            jax.ShapeDtypeStruct(small.shape, f32),
        ),
        in_specs=[pl.BlockSpec(memory_space=pltpu.SMEM), vmem, hbm] + [vmem] * 4 + [hbm] * 5,
        out_specs=(vmem, hbm, hbm, vmem),
        scratch_shapes=[
            buffer(qkv.shape, low),
            buffer((width, slots), low),
            buffer((width, slots), f32),
            buffer((width, slots), f32),
            buffer((width, slots), f32),
            buffer((heads, slots), f32),
            buffer((slots, model), low),
            buffer((slots, model), low),
            buffer((3 * rows, model), low),
            buffer((2, pairs, slice_rows, columns), low),
            buffer((3, 4, pairs, slice_rows, columns), low),
            buffer((pairs - 1, 3, 4, slice_rows, columns), low),
            buffer((2, slots // 2, DEPTH), low),
            buffer((chunks, pairs, share, 3 * width), low),
            buffer((chunks, pairs - 1, share, 3 * width), low),
            buffer((2, chunks, share, 3 * width), low),
            buffer((3, 3, slice_rows, columns), low),
            buffer((3, slice_rows, columns), low),
            buffer(small.shape, f32),
            buffer(small.shape, f32),
            buffer((pairs,) + small.shape, f32),
            buffer((4,) + small.shape, f32),
            dma((4,)),
            dma((4,)),
            dma,
            dma((2,)),
            dma((3,)),
            dma((3,)),
            dma((3, pairs - 1)),
            dma((3, pairs - 1)),
            dma((4, CHUNKS)),
            dma((4, CHUNKS)),
            dma((4, CHUNKS)),
            dma((4, CHUNKS)),
            dma,
            dma((2,)),
            dma((chunks, pairs - 1)),
            dma((chunks, pairs - 1)),
            dma((chunks,)),
            dma((chunks,)),
            dma((chunks, pairs)),
            dma((chunks, pairs)),
            dma((chunks, pairs)),
            dma((chunks,)),
            dma((3,)),
            dma((3,)),
            dma((pairs,)),
            dma((pairs,)),
            dma((2 * pairs,)),
            dma,
            dma((2,)),
            dma((pairs,)),
            dma((pairs,)),
            dma((4,)),
            dma((4,)),
        ],
        compiler_params=pltpu.CompilerParams(
            collective_id=2, has_side_effects=True, vmem_limit_bytes=65_500_000
        ),
        name="attention_backward",
    )(span, qkv, out, logsum, factor, weights, small, split, grad_out, grad_up, grad_down, gathered)


def per_device(
    inputs,
    cotangent,
    gain_attn,
    gain_mlp,
    query_scale,
    w_query,
    w_key,
    w_value,
    w_out,
    w_up,
    w_down,
    lengths,
    offsets,
):
    low = jnp.bfloat16
    f32 = jnp.float32
    here = Place()
    n_dp = lax.axis_size("dp")
    local_rows, model = inputs.shape
    seq_slots = local_rows * 4
    width_local = w_query.shape[1]
    head_dim = query_scale.shape[0]
    heads_local = width_local // head_dim
    pairs = n_dp // 2
    swap_core = [(i, i ^ 1) for i in range(n_dp)]

    slice_rows = w_out.shape[0] // n_dp
    own_slice = jnp.stack(
        [
            lax.dynamic_slice_in_dim(w_out, here.d * slice_rows, slice_rows, 0),
            jnp.transpose(lax.dynamic_slice_in_dim(w_up, here.d * slice_rows, slice_rows, 1)),
            lax.dynamic_slice_in_dim(w_down, here.d * slice_rows, slice_rows, 0),
        ]
    )
    line_w = lax.all_gather(own_slice, "tensor", axis=0, tiled=False)
    mlp_w = lax.all_gather(line_w, "dp", axis=0, tiled=False)

    def whole_weight(w):
        return jnp.transpose(mlp_w[:, :, w], (1, 0, 2, 3)).reshape(model, model)

    w_out_all, w_up_all, w_down_all = whole_weight(0), whole_weight(1), whole_weight(2)

    own_span = jnp.concatenate([lengths, offsets])
    other_span = lax.ppermute(own_span, "dp", swap_core)
    group_span = jnp.where(here.main, own_span, other_span)
    own_rows = here.t * local_rows + jnp.arange(local_rows, dtype=jnp.int32)
    row_valid = ((own_rows >= offsets[0]) & (own_rows < offsets[0] + lengths[0])).astype(f32)

    residual = inputs.astype(f32)
    normed, inverse_one = rms_forward(residual, gain_attn)
    native_w = jnp.concatenate([w_query, w_key, w_value], axis=1)
    gathered, foreign_w = gather_rows(
        normed.astype(low), native_w.reshape(n_dp, model // n_dp, 3 * width_local)
    )
    stacked_w = jnp.where(here.main, native_w, foreign_w.reshape(model, 3 * width_local))

    scale_const = LOG_TWO_E / math.sqrt(head_dim)
    soft = jax.nn.softplus(query_scale)
    factor = jnp.tile(soft * scale_const, heads_local)[:, None]
    projected = dg(stacked_w, gathered, 0, 1)
    qkv = (projected * jnp.concatenate([factor, jnp.ones((2 * width_local, 1), f32)])).astype(low)
    attended, logsum, attended_rows = attention_forward(group_span, qkv, heads_local)

    hidden_one = residual + contract_rows(attended_rows, w_out_all)
    second, inverse_two = rms_forward(hidden_one, gain_mlp)
    second_low = second.astype(low)
    before_act = contract_cols(second_low, w_up_all)
    activated = jax.nn.silu(before_act).astype(low)
    output = hidden_one + jnp.dot(activated, w_down_all, preferred_element_type=f32)
    grad_hidden_out = cotangent.astype(f32) * row_valid[:, None]
    grad_low = grad_hidden_out.astype(low)
    grad_act = contract_cols(grad_low, w_down_all)
    grad_pre = (grad_act * silu_slope(before_act)).astype(low)
    grad_second = jnp.dot(grad_pre, w_up_all, preferred_element_type=f32)
    grad_hidden = grad_hidden_out + rms_backward(hidden_one, inverse_two, gain_mlp, grad_second)
    branch_low = grad_hidden.astype(low)
    grad_att_rows = contract_cols(w_out_all, branch_low).astype(low)

    grad_w_down = contract_rows(activated, grad_low)
    grad_w_up_t = contract_rows(grad_pre, second_low)
    grad_w_out = jnp.dot(attended_rows, branch_low, preferred_element_type=f32)
    gain_two_part = jnp.sum(grad_w_up_t * w_up_all.astype(f32), axis=0)

    def by_member(grad):
        return grad.astype(low).reshape(4, pairs, width_local // pairs, model)

    small = jnp.concatenate(
        [jnp.zeros((1, model), f32), gain_two_part[None], jnp.zeros((6, model), f32)]
    )
    grad_first, mlp_all, qkv_all, small = attention_backward(
        group_span, qkv, attended, logsum, factor, stacked_w, small, grad_att_rows,
        by_member(grad_w_out), by_member(grad_w_up_t), by_member(grad_w_down), gathered,
    )
    grad_input = grad_hidden + rms_backward(
        residual, inverse_one, gain_attn, grad_first.astype(f32)
    )
    grad_gain_one = small[0] / gain_attn
    grad_gain_two = small[1] / gain_mlp
    scale_sum = jnp.sum(small[2, :width_local].reshape(heads_local, head_dim), axis=0)
    grad_scale = scale_sum * jax.nn.sigmoid(query_scale) / soft
    mlp_all = mlp_all.astype(f32).reshape(pairs, 2, 3, width_local // pairs, model // 2)

    def final_weight(w):
        return jnp.transpose(mlp_all[:, :, w], (0, 2, 1, 3)).reshape(width_local, model)

    grad_out_final = final_weight(0)
    grad_up_final = jnp.transpose(final_weight(1))
    grad_down_final = final_weight(2)
    qkv_all = qkv_all.astype(f32).reshape(model, 3 * width_local)
    return (
        output.astype(low),
        grad_input,
        grad_gain_one,
        grad_gain_two,
        grad_scale,
        qkv_all[:, :width_local],
        qkv_all[:, width_local : 2 * width_local],
        qkv_all[:, 2 * width_local :],
        grad_out_final,
        grad_up_final,
        grad_down_final,
    )


def solution(mesh):
    rows = P(("dp", "tensor"), None)
    cols_t = P(None, "tensor")
    rows_t = P("tensor", None)
    return jax.shard_map(
        per_device,
        mesh=mesh,
        in_specs=(
            rows, rows, P(), P(), P(), cols_t, cols_t, cols_t, rows_t, cols_t, rows_t, P("dp"), P("dp"),
        ),
        out_specs=(
            rows, rows, P(), P(), P(), cols_t, cols_t, cols_t, rows_t, cols_t, rows_t,
        ),
        check_vma=False,
    )
```

```python
import functools
import math

import jax
import jax.numpy as jnp
from jax import lax
from jax.experimental import pallas as pl
from jax.experimental.pallas import tpu as pltpu
from jax.sharding import PartitionSpec as P

EPSILON = 1e-06
LOG_TWO_E = 1.4426950408889634
MESH_ID = pl.DeviceIdType.MESH
CHUNKS = 4


def rms_forward(values, gain):
    inverse = lax.rsqrt(jnp.mean(values * values, axis=-1, keepdims=True) + EPSILON)
    return (values * inverse * gain, inverse)


def rms_backward(values, inverse, gain, grad_normed):
    scaled = values * inverse
    grad_scaled = grad_normed * gain
    return inverse * (
        grad_scaled - scaled * jnp.mean(grad_scaled * scaled, axis=-1, keepdims=True)
    )


def contract_rows(left, right):
    return lax.dot_general(
        left, right, (((0,), (0,)), ((), ())), preferred_element_type=jnp.float32
    )


def contract_cols(left, right):
    return lax.dot_general(
        left, right, (((1,), (1,)), ((), ())), preferred_element_type=jnp.float32
    )


def silu_slope(values):
    sigmoid_v = jax.nn.sigmoid(values)
    return sigmoid_v * (1.0 + values * (1.0 - sigmoid_v))


class Place:
    def __init__(self):
        self.d = lax.axis_index("dp")
        self.t = lax.axis_index("tensor")
        self.c = lax.rem(self.d, 2)
        self.g = self.t // 2
        self.base = self.d - self.c
        self.pairs = lax.axis_size("dp") // 2
        self.pair = self.d // 2
        self.main = self.c == self.g
        self.pos = jnp.where(self.c == 0, self.t, 3 - self.t)

    def device(self, seq, pos):
        return (self.base + seq, jnp.where(seq == 0, pos, 3 - pos))

    def across(self, step):
        return (2 * lax.rem(self.pair + step, self.pairs) + self.c, self.t)

    def partner(self):
        return (self.base + 1 - self.c, self.t)

    def quarter(self):
        return jnp.where(self.main, self.t, lax.rem(self.t + 2, 4))


def pair_barrier(here, plane=False):
    barrier = pltpu.get_barrier_semaphore()
    others = []
    for step in range(1, 8):
        code = lax.rem(here.c * 4 + here.t + step, 8)
        others.append((here.base + code // 4, lax.rem(code, 4)))
    if plane:
        others += [here.across(step) for step in range(1, here.pairs)]
    for device in others:
        pl.semaphore_signal(barrier, inc=1, device_id=device, device_id_type=MESH_ID)
    pl.semaphore_wait(barrier, len(others))


def remote(src, dst, send, recv, device):
    return pltpu.make_async_remote_copy(
        src_ref=src, dst_ref=dst, send_sem=send, recv_sem=recv, device_id=device, device_id_type=MESH_ID
    )


def dg(left, right, left_dim, right_dim):
    return lax.dot_general(
        left, right, (((left_dim,), (right_dim,)), ((), ())), preferred_element_type=jnp.float32
    )


TILE = 512
MASKED = -1e30


def readable(span, first_key, first_query):
    shape = (TILE, TILE)
    key = first_key + lax.broadcasted_iota(jnp.int32, shape, 0)
    query = first_query + lax.broadcasted_iota(jnp.int32, shape, 1)
    valid = (key >= span[1]) & (key < span[1] + span[0])
    return (valid & (key <= query)) | (key == query)


def key_bias(span, first_key):
    key = first_key + lax.broadcasted_iota(jnp.int32, (TILE, 1), 0)
    return jnp.where((key >= span[1]) & (key < span[1] + span[0]), 0.0, MASKED)


def forward_kernel(
    span, own, native, factor, mlp_native,
    gathered, weights, qkv, out, logsum, rows_out, mlp_all,
    highest, summed, total,
    keep_sem, send_z, send_c, recv,
    native_sem, weight_sent, spread_sent, weight_got,
    rows_sent, rows_got, rows_local,
    mlp_local, line_sent, line_got, plane_sent, share_sent, mlp_have,
):
    heads = logsum.shape[0]
    width, slots = out.shape
    dim = width // heads
    low, f32 = qkv.dtype, jnp.float32
    here = Place()
    pairs = here.pairs
    split = mlp_native.shape[1]
    rows = own.shape[0]
    part = rows // CHUNKS
    columns = own.shape[1] // 2
    tall = native.shape[0] // split
    blocks = slots // TILE
    partner = here.partner()
    pair_barrier(here, plane=True)

    def half(core):
        return pl.ds(pl.multiple_of(core * columns, columns), columns)

    def weight_piece(ref, pair, core):
        return ref.at[pl.ds(pl.multiple_of(pair * tall, tall), tall), half(core)]

    line = lax.rem(here.t + 2, 4)
    weight_copy = remote(
        weight_piece(native, here.pair, here.c),
        weight_piece(weights, here.pair, here.c),
        weight_sent,
        weight_got.at[here.pair, here.c],
        (here.base + 1 - line // 2, line),
    )
    sends = here.pair < split

    @pl.when(sends)
    def _():
        weight_copy.start()

    native_copy = pltpu.make_async_copy(native, weights, native_sem)

    @pl.when(here.main)
    def _():
        native_copy.start()

    def place(seq, k, ch):
        block = jnp.where(seq == 0, k, 3 - k)
        return gathered.at[pl.ds(pl.multiple_of(block * rows + ch * part, part), part)]

    def copy(src, k, ch, seq, device, send):
        return remote(src, place(seq, k, ch), send.at[k, ch], recv.at[k, ch], device)

    def own_copy(k, ch, device, send):
        return copy(own.at[pl.ds(ch * part, part)], k, ch, here.c, device, send)

    def pass_copy(k, ch, device, send):
        return copy(place(here.g, k, ch), k, ch, here.g, device, send)

    def arrived(k, ch):
        pass_copy(k, ch, partner, send_z).wait_recv()

    keep = pltpu.make_async_copy(
        own, gathered.at[pl.ds(pl.multiple_of(here.t * rows, rows), rows)], keep_sem
    )
    near = here.device(here.c, jnp.where(here.pos == 1, 0, 1))

    @pl.when(here.main)
    def _():
        keep.start()
        for ch in range(CHUNKS):
            own_copy(here.pos, ch, near, send_z).start()
            own_copy(here.pos, ch, partner, send_c).start()

    @pl.when(jnp.logical_not(here.main))
    def _():
        for ch in range(CHUNKS):
            own_copy(here.pos, ch, near, send_z).start()

    def mlp_piece(quarter, pair, core):
        return mlp_all.at[:, quarter, pair, :, half(core)]

    def mlp_line(step):
        return remote(
            mlp_native.at[:, here.pair, :, half(here.c)],
            mlp_piece(here.t, here.pair, here.c),
            line_sent.at[step - 1],
            line_got.at[here.t],
            (here.d, lax.rem(here.t + step, 4)),
        )

    def mlp_plane(n, step):
        quarter = lax.rem(here.t + n, 4)
        piece = mlp_piece(quarter, here.pair, here.c)
        return remote(
            piece, piece, plane_sent.at[n - 1, step], mlp_have.at[quarter, here.pair, here.c], here.across(step)
        )

    def mlp_core(n, pair):
        quarter = lax.rem(here.t + n, 4)
        piece = mlp_piece(quarter, pair, here.c)
        return remote(
            piece, piece, share_sent.at[n - 1, pair], mlp_have.at[quarter, pair, here.c], partner
        )

    def mlp_arrived(n, pair, core):
        quarter = lax.rem(here.t + n, 4)
        piece = mlp_piece(quarter, pair, core)
        remote(piece, piece, share_sent.at[0, 0], mlp_have.at[quarter, pair, core], partner).wait_recv()

    mlp_keep = pltpu.make_async_copy(mlp_native, mlp_all.at[:, here.t], mlp_local)

    @pl.when(sends)
    def _():
        for step in range(1, 4):
            mlp_line(step).start()

    mlp_keep.start()

    def from_line():
        @pl.when(sends)
        def _():
            for n in (1, 3, 2):
                quarter = lax.rem(here.t + n, 4)
                piece = mlp_piece(quarter, here.pair, here.c)
                remote(piece, piece, share_sent.at[0, 0], line_got.at[quarter], partner).wait_recv()
                for step in range(1, pairs):
                    mlp_plane(n, step).start()
                mlp_core(n, here.pair).start()

    def spread(core, step):
        piece = weight_piece(weights, here.pair, core)
        return remote(
            piece, piece, spread_sent.at[core, step - 1], weight_got.at[here.pair, core], here.across(step)
        )

    def weight_arrived(pair, core):
        piece = weight_piece(weights, pair, core)
        remote(piece, piece, weight_sent, weight_got.at[pair, core], partner).wait_recv()

    @pl.when(jnp.logical_not(here.main))
    def _():
        @pl.when(sends)
        def _():
            for core in range(2):
                weight_arrived(here.pair, core)
                for step in range(1, pairs):
                    spread(core, step).start()

        for pair in range(split):
            @pl.when(here.pair != pair)
            def _(pair=pair):
                for core in range(2):
                    weight_arrived(pair, core)

    @pl.when(here.main)
    def _():
        native_copy.wait()
        keep.wait()

    @pl.when(here.pos == 1)
    def _():
        for ch in range(CHUNKS):
            arrived(2, ch)
            pass_copy(2, ch, near, send_z).start()
            pass_copy(2, ch, partner, send_c).start()
            arrived(0, ch)
            pass_copy(0, ch, partner, send_c).start()
        for ch in range(CHUNKS):
            arrived(3, ch)
            pass_copy(3, ch, near, send_z).start()
            pass_copy(3, ch, partner, send_c).start()

    quarter = here.quarter()

    def into(q):
        return rows_out.at[pl.ds(pl.multiple_of(q * width, width), width)]

    def done_columns(i):
        return out.at[:, pl.ds(pl.multiple_of(i * TILE, TILE), TILE)]

    def rows_copy(i):
        return remote(
            done_columns(i), into(quarter), rows_sent.at[i], rows_got.at[quarter], (here.base + here.g, i)
        )

    rows_keep = pltpu.make_async_copy(done_columns(here.t), into(here.t), rows_local)

    def finish(i):
        qs = pl.ds(pl.multiple_of(i * TILE, TILE), TILE)
        for h in range(heads):
            hs = pl.ds(h * dim, dim)
            sums = summed[h : h + 1, qs]
            out[hs, qs] = (total[hs, qs] / sums).astype(out.dtype)
            logsum[h : h + 1, qs] = highest[h : h + 1, qs] + jnp.log(sums)
        stays = here.main & (here.t == i)

        @pl.when(stays)
        def _():
            rows_keep.start()

        @pl.when(jnp.logical_not(stays))
        def _():
            rows_copy(i).start()

    highest[...] = jnp.full_like(highest, MASKED)
    summed[...] = jnp.zeros_like(summed)
    total[...] = jnp.zeros_like(total)

    @pl.loop(0, blocks)
    def _(s):
        b = jnp.where(here.g == 0, s, blocks - 1 - s)
        last = (here.g == 1) & (s == blocks - 1)

        @pl.when((here.pos == 0) & (s >= 1))
        def _():
            for ch in range(CHUNKS):
                arrived(s, ch)
                pass_copy(s, ch, partner, send_c).start()

        @pl.when(jnp.logical_not(here.main))
        def _():
            for ch in range(CHUNKS):
                arrived(s, ch)

        bs = pl.ds(pl.multiple_of(b * TILE, TILE), TILE)
        for w in range(3):
            at = pl.ds(w * width, width)
            qkv[at, bs] = (dg(weights[at], gathered[bs], 1, 1) * factor[at]).astype(low)

        def tile(i, j, diagonal):
            qs = pl.ds(pl.multiple_of(i * TILE, TILE), TILE)
            ks = pl.ds(pl.multiple_of(j * TILE, TILE), TILE)
            if diagonal:
                allowed = readable(span, j * TILE, i * TILE)
            else:
                bias = key_bias(span, j * TILE)
            for h in range(heads):
                hs = pl.ds(h * dim, dim)
                scores = dg(qkv[pl.ds(width + h * dim, dim), ks], qkv[hs, qs], 0, 0)
                scores = jnp.where(allowed, scores, MASKED) if diagonal else scores + bias
                before = highest[h : h + 1, qs]
                after = jnp.maximum(before, jnp.max(scores, axis=0, keepdims=True))
                expo = jnp.exp(scores - after)
                scale = jnp.exp(before - after)
                summed[h : h + 1, qs] = summed[h : h + 1, qs] * scale + jnp.sum(expo, axis=0, keepdims=True)
                highest[h : h + 1, qs] = after
                total[hs, qs] = total[hs, qs] * scale + dg(
                    qkv[pl.ds(2 * width + h * dim, dim), ks], expo.astype(low), 1, 0
                )

        tile(b, b, True)

        @pl.when(last)
        def _():
            finish(b)

        @pl.loop(0, s)
        def _(n):
            i = jnp.where(here.g == 0, b, b + 1 + n)
            tile(i, jnp.where(here.g == 0, n, b), False)

            @pl.when(last)
            def _():
                finish(i)

        @pl.when(here.g == 0)
        def _():
            finish(b)

        @pl.when(s == 2)
        def _():
            from_line()

    for n in (1, 3, 2):
        for pair in range(split):
            @pl.when(here.pair != pair)
            def _(n=n, pair=pair):
                mlp_arrived(n, pair, here.c)
                mlp_core(n, pair).start()

    for block in range(4):
        stays = here.main & (here.t == block)

        @pl.when(stays)
        def _():
            rows_keep.wait()

        @pl.when(jnp.logical_not(stays))
        def _(block=block):
            rows_copy(block).wait_send()
            remote(
                done_columns(0), into(block), rows_sent.at[0], rows_got.at[block], partner
            ).wait_recv()

    for n in range(1, 4):
        for pair in range(split):
            mlp_arrived(n, pair, 1 - here.c)
            mlp_core(n, pair).wait_send()
    mlp_keep.wait()

    @pl.when(sends)
    def _():
        weight_copy.wait_send()
        for step in range(1, 4):
            mlp_line(step).wait_send()
            for across in range(1, pairs):
                mlp_plane(step, across).wait_send()

    @pl.when(sends & jnp.logical_not(here.main))
    def _():
        for core in range(2):
            for step in range(1, pairs):
                spread(core, step).wait_send()

    for ch in range(CHUNKS):
        own_copy(here.pos, ch, near, send_z).wait_send()

    @pl.when(here.main)
    def _():
        for ch in range(CHUNKS):
            own_copy(here.pos, ch, partner, send_c).wait_send()

    @pl.when(here.pos == 0)
    def _():
        for k in (1, 2, 3):
            for ch in range(CHUNKS):
                pass_copy(k, ch, partner, send_c).wait_send()

    @pl.when(here.pos == 1)
    def _():
        for ch in range(CHUNKS):
            pass_copy(0, ch, partner, send_c).wait_send()
            for k in (2, 3):
                pass_copy(k, ch, near, send_z).wait_send()
                pass_copy(k, ch, partner, send_c).wait_send()


def attention_forward(span, own, native, factor, mlp_native, heads):
    rows, model = own.shape
    slots = 4 * rows
    width = native.shape[0] // 3
    _, split, tall, _ = mlp_native.shape
    pairs = lax.axis_size("dp") // 2
    low, f32 = own.dtype, jnp.float32
    vmem = pl.BlockSpec(memory_space=pltpu.VMEM)
    hbm = pl.BlockSpec(memory_space=pl.ANY)
    dma = pltpu.SemaphoreType.DMA
    return pl.pallas_call(
        forward_kernel,
        out_shape=(
            jax.ShapeDtypeStruct((slots, model), low),
            jax.ShapeDtypeStruct(native.shape, low),
            jax.ShapeDtypeStruct((3 * width, slots), low),
            jax.ShapeDtypeStruct((width, slots), low),
            jax.ShapeDtypeStruct((heads, slots), f32),
            jax.ShapeDtypeStruct((4 * width, rows), low),
            jax.ShapeDtypeStruct((3, 4, split, tall, model), low),
        ),
        in_specs=[pl.BlockSpec(memory_space=pltpu.SMEM), hbm, hbm, vmem, hbm],
        out_specs=(vmem,) * 5 + (hbm, hbm),
        scratch_shapes=[
            pltpu.VMEM((heads, slots), f32),
            pltpu.VMEM((heads, slots), f32),
            pltpu.VMEM((width, slots), f32),
            dma,
            dma((4, CHUNKS)),
            dma((4, CHUNKS)),
            dma((4, CHUNKS)),
            dma,
            dma,
            dma((2, pairs - 1)),
            dma((split, 2)),
            dma((4,)),
            dma((4,)),
            dma,
            dma,
            dma((3,)),
            dma((4,)),
            dma((3, pairs)),
            dma((3, split)),
            dma((4, split, 2)),
        ],
        compiler_params=pltpu.CompilerParams(
            collective_id=1, has_side_effects=True, vmem_limit_bytes=50 * 1024 * 1024
        ),
        name="attention_forward",
    )(span, own, native, factor, mlp_native)


def backward_kernel(
    span, qkv, out, logsum, factor, weights, small, split, grad_out, grad_up, grad_down, gathered,
    rows_grad, mlp_all, qkv_all, small_all,
    result, grad, query_sum, key_sum, value_sum, term,
    partial, from_core, from_line, keep_in, chip_sum, plane_in,
    normed, weight_grad, qkv_in, qkv_swap, mlp_in, mlp_sum,
    small_own, small_pair, small_plane, small_line,
    split_sent, split_got, local_sem, keep_sem,
    give_sent, give_got, plane_sent, plane_got,
    send_c, send_z, recv_c, recv_z,
    out_sem, normed_sem, qkv_sent, qkv_got, cross_sent, cross_got, qkv_spread, qkv_share, qkv_have, qkv_local,
    line_sent, line_got, mlp_spread, mlp_share, mlp_have, mlp_local,
    small_sems, small_across_sent, small_across_got, small_along_sent, small_along_got,
):
    heads = logsum.shape[0]
    width, slots = out.shape
    dim = width // heads
    low, f32 = qkv.dtype, jnp.float32
    here = Place()
    pairs = here.pairs
    rows = split.shape[1]
    part = rows // CHUNKS
    partner = here.partner()
    pair_barrier(here, plane=True)
    blocks = slots // TILE

    def of(q):
        return split.at[pl.ds(pl.multiple_of(q * width, width), width)]

    def into(block):
        return grad.at[:, pl.ds(pl.multiple_of(block * rows, rows), rows)]

    def split_copy(q):
        native = (q // 2) == here.c
        seq = jnp.where(native, here.c, 1 - here.c)
        line = jnp.where(native, q, (q + 2) % 4)
        return remote(of(q), into(here.t), split_sent.at[q], split_got.at[here.t], (here.base + seq, line))

    keep = pltpu.make_async_copy(of(here.t), into(here.t), local_sem)
    for q in range(4):
        stays = here.main & (here.t == q)

        @pl.when(stays)
        def _():
            keep.start()

        @pl.when(jnp.logical_not(stays))
        def _(q=q):
            split_copy(q).start()

    sources = (grad_out, grad_up, grad_down)
    columns = chip_sum.shape[-1]

    def half(core):
        return pl.ds(pl.multiple_of(core * columns, columns), columns)

    def give(w):
        return remote(
            sources[w].at[:, :, :, half(1 - here.c)], chip_sum.at[w], give_sent.at[w], give_got.at[w], partner
        )

    def own_half(w, q):
        slot = (4 * w + q) % 2
        return pltpu.make_async_copy(
            sources[w].at[q, :, :, half(here.c)], keep_in.at[slot], keep_sem.at[slot]
        )

    def plane_copy(w, step):
        return remote(
            chip_sum.at[w, :, lax.rem(here.pair + step, pairs)],
            plane_in.at[step - 1, w],
            plane_sent.at[w, step - 1],
            plane_got.at[w, step - 1],
            here.across(step),
        )

    for w in range(3):
        give(w).start()
    own_half(0, 0).start()
    out_copy = pltpu.make_async_copy(out, result.at[pl.ds(0, width)], out_sem)
    out_copy.start()
    query_sum[...] = jnp.zeros_like(query_sum)
    key_sum[...] = jnp.zeros_like(key_sum)
    value_sum[...] = jnp.zeros_like(value_sum)
    for w in range(3):
        give(w).wait_recv()
        for q in range(4):
            own_half(w, q).wait()
            if q < 3:
                own_half(w, q + 1).start()
            elif w < 2:
                own_half(w + 1, 0).start()

            @pl.loop(0, pairs)
            def _(p, w=w, q=q):
                chip_sum[w, q, p] = (chip_sum[w, q, p].astype(f32) + keep_in[q % 2, p].astype(f32)).astype(low)

        for step in range(1, pairs):
            plane_copy(w, step).start()

    for block in range(4):
        stays = here.main & (here.t == block)

        @pl.when(stays)
        def _():
            keep.wait()

        @pl.when(jnp.logical_not(stays))
        def _(block=block):
            remote(of(0), into(block), split_sent.at[0], split_got.at[block], partner).wait_recv()

    out_copy.wait()
    for h in range(heads):
        hs = pl.ds(h * dim, dim)
        term[h : h + 1] = jnp.sum(grad[hs].astype(f32) * result[hs].astype(f32), axis=0, keepdims=True)

    def span_of(seq, k, ch):
        block = jnp.where(seq == 0, k, 3 - k)
        return pl.ds(pl.multiple_of(block * rows + ch * part, part), part)

    def piece(k, ch):
        return pl.ds(pl.multiple_of(k * rows + ch * part, part), part)

    def line_piece(k, ch):
        return piece(k % 3 if isinstance(k, int) else lax.rem(k, 3), ch)

    def line_rows(ch):
        return pl.ds(ch * part, part)

    def core_copy(k, ch):
        at = span_of(here.g, k, ch)
        return remote(partial.at[at], from_core.at[piece(k, ch)], send_c.at[k, ch], recv_c.at[k, ch], partner)

    def line_copy(k, ch):
        at = span_of(here.g, k, ch)
        return remote(
            partial.at[at],
            from_line.at[line_piece(k, ch)],
            send_z.at[k, ch],
            recv_z.at[k, ch],
            here.device(here.c, jnp.where(here.pos == 0, 1, 0)),
        )

    def home_copy(k, ch):
        at = span_of(here.g, k, ch)
        return remote(
            partial.at[at], rows_grad.at[line_rows(ch)], send_z.at[k, ch], recv_z.at[k, ch], here.device(here.c, k)
        )

    def core_sum(k, ch):
        core_copy(k, ch).wait_recv()
        return partial[span_of(here.g, k, ch)].astype(f32) + from_core[piece(k, ch)].astype(f32)

    def with_line(k, ch):
        line_copy(k, ch).wait_recv()
        return core_sum(k, ch) + from_line[line_piece(k, ch)].astype(f32)

    def pass_on(k):
        for ch in range(CHUNKS):
            partial[span_of(here.g, k, ch)] = core_sum(k, ch).astype(low)
            line_copy(k, ch).start()

    def send_home(k):
        for ch in range(CHUNKS):
            partial[span_of(here.g, k, ch)] = with_line(k, ch).astype(low)
            home_copy(k, ch).start()

    @pl.loop(0, blocks)
    def _(s):
        b = jnp.where(here.g == 0, blocks - 1 - s, s)
        k = blocks - 1 - s

        def tile(i, j, diagonal):
            qs = pl.ds(pl.multiple_of(i * TILE, TILE), TILE)
            ks = pl.ds(pl.multiple_of(j * TILE, TILE), TILE)
            if diagonal:
                allowed = readable(span, j * TILE, i * TILE)
            else:
                bias = key_bias(span, j * TILE)
            for h in range(heads):
                hs = pl.ds(h * dim, dim)
                ke = pl.ds(width + h * dim, dim)
                va = pl.ds(2 * width + h * dim, dim)
                scores = dg(qkv[ke, ks], qkv[hs, qs], 0, 0)
                scores = jnp.where(allowed, scores, MASKED) if diagonal else scores + bias
                probs = jnp.exp(scores - logsum[h : h + 1, qs])
                grad_probs = dg(qkv[va, ks], grad[hs, qs], 0, 0)
                grad_scores = (probs * (grad_probs - term[h : h + 1, qs])).astype(low)
                value_sum[hs, ks] += dg(grad[hs, qs], probs.astype(low), 1, 1)
                key_sum[hs, ks] += dg(qkv[hs, qs], grad_scores, 1, 1)
                query_sum[hs, qs] += dg(qkv[ke, ks], grad_scores, 1, 0)

        tile(b, b, True)

        @pl.when((here.pos == 0) & (s >= 1))
        def _():
            pass_on(k + 1)

        @pl.loop(0, blocks - 1 - s)
        def _(n):
            tile(jnp.where(here.g == 0, b, b + 1 + n), jnp.where(here.g == 0, n, b), False)

        bs = pl.ds(pl.multiple_of(b * TILE, TILE), TILE)
        result[pl.ds(0, width), bs] = (query_sum[:, bs] * factor[...]).astype(low)
        result[pl.ds(width, width), bs] = key_sum[:, bs].astype(low)
        result[pl.ds(2 * width, width), bs] = value_sum[:, bs].astype(low)
        partial[bs] = dg(result[:, bs], weights[...], 0, 0).astype(low)

        @pl.when(jnp.logical_not(here.main))
        def _():
            for ch in range(CHUNKS):
                core_copy(k, ch).start()

    @pl.when(here.pos == 1)
    def _():
        send_home(3)

    chunks, _, share, _ = weight_grad.shape
    depth = pairs * share

    half_slots = slots // 2

    def load(i, part_of):
        return pltpu.make_async_copy(
            gathered.at[
                pl.ds(part_of * half_slots, half_slots), pl.ds(pl.multiple_of(i * depth, depth), depth)
            ],
            normed.at[part_of],
            normed_sem.at[part_of],
        )

    def qkv_send(i, step):
        return remote(
            weight_grad.at[i, lax.rem(here.pair + step, pairs)],
            qkv_in.at[i, step - 1],
            qkv_sent.at[i, step - 1],
            qkv_got.at[i, step - 1],
            here.across(step),
        )

    small_own[...] = small[...]
    load(0, 0).start()
    load(0, 1).start()

    @pl.loop(0, chunks)
    def _(i):
        at = pl.ds(pl.multiple_of(i * depth, depth), depth)
        load(i, 0).wait()
        grads = dg(normed[0], result[:, :half_slots], 0, 1)

        @pl.when(i + 1 < chunks)
        def _():
            load(i + 1, 0).start()

        load(i, 1).wait()
        grads += dg(normed[1], result[:, half_slots:], 0, 1)

        @pl.when(i + 1 < chunks)
        def _():
            load(i + 1, 1).start()

        for p in range(pairs):
            weight_grad[i, p] = grads[p * share : (p + 1) * share].astype(low)
        for step in range(1, pairs):
            qkv_send(i, step).start()
        weighted = grads * jnp.transpose(weights[:, at]).astype(f32)
        by_row = jnp.sum(weighted, axis=1, keepdims=True)
        small_own[0:1, at] = jnp.transpose(jnp.broadcast_to(by_row, (depth, 128)))[0:1]
        small_own[2:3, pl.ds(0, 3 * width)] += jnp.sum(weighted, axis=0, keepdims=True)

    small_copy = remote(small_own, small_pair, small_sems.at[0], small_sems.at[1], partner)
    small_copy.start()

    def mlp_line(step):
        line = lax.rem(here.t + step, 4)
        return remote(
            chip_sum.at[:, line, here.pair], mlp_in.at[step - 1], line_sent.at[step - 1], line_got.at[step - 1],
            (here.d, line),
        )

    for w in range(3):
        for step in range(1, pairs):
            plane_copy(w, step).wait_recv()

        @pl.loop(0, 4)
        def _(q, w=w):
            total = chip_sum[w, q, here.pair].astype(f32)
            for step in range(1, pairs):
                total += plane_in[step - 1, w, q].astype(f32)
            chip_sum[w, q, here.pair] = total.astype(low)

    for step in range(1, 4):
        mlp_line(step).start()

    @pl.when(here.pos == 1)
    def _():
        pass_on(0)
        send_home(2)

    line = lax.rem(here.t + 2, 4)

    def cross(i):
        return remote(
            qkv_swap.at[0, i], qkv_swap.at[1, i], cross_sent.at[i], cross_got.at[i],
            (here.base + line // 2, line),
        )

    def qkv_out(i, step):
        return remote(
            qkv_swap.at[0, i], qkv_all.at[i, here.pair], qkv_spread.at[i, step], qkv_have.at[i, here.pair],
            here.across(step),
        )

    def qkv_own(i):
        return remote(
            qkv_swap.at[0, i], qkv_all.at[i, here.pair], qkv_share.at[i, 0], qkv_have.at[i, here.pair], partner
        )

    def qkv_keep(i):
        return pltpu.make_async_copy(qkv_swap.at[0, i], qkv_all.at[i, here.pair], qkv_local.at[i])

    def qkv_core(i, step):
        pair = lax.rem(here.pair + step, pairs)
        return remote(
            qkv_all.at[i, pair], qkv_all.at[i, pair], qkv_share.at[i, step], qkv_have.at[i, pair], partner
        )

    def finish(i):
        @pl.when(here.main)
        def _():
            cross(i).wait_recv()
            qkv_swap[0, i] = (qkv_swap[0, i].astype(f32) + qkv_swap[1, i].astype(f32)).astype(low)
            qkv_keep(i).start()
            for step in range(1, pairs):
                qkv_out(i, step).start()
            qkv_own(i).start()

    @pl.loop(0, chunks)
    def _(i):
        total = weight_grad[i, here.pair].astype(f32)
        for step in range(1, pairs):
            qkv_send(i, step).wait_recv()
            total += qkv_in[i, step - 1].astype(f32)
        qkv_swap[0, i] = total.astype(low)

        @pl.when(jnp.logical_not(here.main))
        def _():
            cross(i).start()

        @pl.when(i >= 1)
        def _():
            finish(i - 1)

    finish(chunks - 1)

    small_copy.wait_recv()
    small_plane[here.pair] = small_own[...] + small_pair[...]

    def small_across(step):
        return remote(
            small_plane.at[here.pair], small_plane.at[here.pair], small_across_sent.at[step],
            small_across_got.at[here.pair], here.across(step),
        )

    def small_along(step):
        return remote(
            small_line.at[here.t], small_line.at[here.t], small_along_sent.at[step], small_along_got.at[here.t],
            (here.d, lax.rem(here.t + step, 4)),
        )

    for step in range(1, pairs):
        small_across(step).start()

    for step in range(1, 4):
        mlp_line(step).wait_recv()
    mlp_total = chip_sum[:, here.t, here.pair].astype(f32)
    for step in range(1, 4):
        mlp_total += mlp_in[step - 1].astype(f32)
    mlp_sum[...] = mlp_total.astype(low)

    def mlp_out(step):
        return remote(
            mlp_sum, mlp_all.at[here.d], mlp_spread.at[step], mlp_have.at[here.d], here.across(step)
        )

    mlp_own = remote(mlp_sum, mlp_all.at[here.d], mlp_share.at[0], mlp_have.at[here.d], partner)
    mlp_keep = pltpu.make_async_copy(mlp_sum, mlp_all.at[here.d], mlp_local)

    def mlp_core(step):
        member = 2 * lax.rem(here.pair + step, pairs) + here.c
        return remote(
            mlp_all.at[member], mlp_all.at[member], mlp_share.at[step], mlp_have.at[member], partner
        )

    def mlp_arrived(member):
        remote(mlp_sum, mlp_all.at[member], mlp_share.at[0], mlp_have.at[member], partner).wait_recv()

    for step in range(1, pairs):
        mlp_out(step).start()
    mlp_own.start()
    mlp_keep.start()

    for step in range(1, pairs):
        pair = lax.rem(here.pair + step, pairs)
        remote(
            small_own, small_plane.at[pair], small_across_sent.at[0], small_across_got.at[pair], partner
        ).wait_recv()
    plane_total = small_plane[0]
    for pair in range(1, pairs):
        plane_total += small_plane[pair]
    small_line[here.t] = plane_total
    for step in range(1, 4):
        small_along(step).start()

    @pl.when(here.pos == 0)
    def _():
        for ch in range(CHUNKS):
            rows_grad[line_rows(ch)] = with_line(0, ch).astype(low)
        for k in (1, 2, 3):
            for ch in range(CHUNKS):
                line_copy(k, ch).wait_send()

    @pl.when(here.pos == 1)
    def _():
        for ch in range(CHUNKS):
            rows_grad[line_rows(ch)] = with_line(1, ch).astype(low)
        for ch in range(CHUNKS):
            line_copy(0, ch).wait_send()
            for k in (2, 3):
                home_copy(k, ch).wait_send()

    for k in (2, 3):
        @pl.when(here.pos == k)
        def _(k=k):
            for ch in range(CHUNKS):
                remote(
                    partial.at[piece(0, ch)], rows_grad.at[line_rows(ch)], send_z.at[0, ch], recv_z.at[k, ch], partner
                ).wait_recv()

    for step in range(1, 4):
        other = lax.rem(here.t + step, 4)
        remote(
            small_own, small_line.at[other], small_along_sent.at[0], small_along_got.at[other], partner
        ).wait_recv()
    small_all[...] = (small_line[0] + small_line[1]) + (small_line[2] + small_line[3])

    @pl.when(here.main)
    def _():
        @pl.loop(0, chunks)
        def _(i):
            for step in range(1, pairs):
                qkv_core(i, step).wait_recv()
                qkv_core(i, step).start()

    for step in range(1, pairs):
        mlp_arrived(2 * lax.rem(here.pair + step, pairs) + here.c)
        mlp_core(step).start()

    @pl.when(here.main)
    def _():
        @pl.loop(0, chunks)
        def _(i):
            qkv_keep(i).wait()
            qkv_own(i).wait_send()
            for step in range(1, pairs):
                qkv_out(i, step).wait_send()
                qkv_core(i, step).wait_send()

    @pl.when(jnp.logical_not(here.main))
    def _():
        @pl.loop(0, chunks)
        def _(i):
            cross(i).wait_send()
            for step in range(pairs):
                qkv_core(i, step).wait_recv()

        for k in range(4):
            for ch in range(CHUNKS):
                core_copy(k, ch).wait_send()

    for step in range(pairs):
        mlp_arrived(2 * lax.rem(here.pair + step, pairs) + 1 - here.c)
    mlp_keep.wait()
    mlp_own.wait_send()

    for q in range(4):
        @pl.when(jnp.logical_not(here.main & (here.t == q)))
        def _(q=q):
            split_copy(q).wait_send()

    for w in range(3):
        give(w).wait_send()
        for step in range(1, pairs):
            plane_copy(w, step).wait_send()

    @pl.loop(0, chunks)
    def _(i):
        for step in range(1, pairs):
            qkv_send(i, step).wait_send()

    for step in range(1, pairs):
        mlp_out(step).wait_send()
        mlp_core(step).wait_send()
        small_across(step).wait_send()
    for step in range(1, 4):
        mlp_line(step).wait_send()
        small_along(step).wait_send()
    small_copy.wait_send()


DEPTH = 256


def attention_backward(
    span, qkv, out, logsum, factor, weights, small, split, grad_out, grad_up, grad_down, gathered
):
    width, slots = out.shape
    heads = logsum.shape[0]
    rows, model = split.shape[1], weights.shape[1]
    low, f32 = qkv.dtype, jnp.float32
    pairs, slice_rows = grad_out.shape[1], grad_out.shape[2]
    columns = model // 2
    chunks, share = model // DEPTH, DEPTH // pairs
    vmem = pl.BlockSpec(memory_space=pltpu.VMEM)
    hbm = pl.BlockSpec(memory_space=pl.ANY)
    dma = pltpu.SemaphoreType.DMA
    buffer = pltpu.VMEM
    return pl.pallas_call(
        backward_kernel,
        out_shape=(
            jax.ShapeDtypeStruct((rows, model), low),
            jax.ShapeDtypeStruct((2 * pairs, 3, slice_rows, columns), low),
            jax.ShapeDtypeStruct((chunks, pairs, share, 3 * width), low),
            jax.ShapeDtypeStruct(small.shape, f32),
        ),
        in_specs=[pl.BlockSpec(memory_space=pltpu.SMEM), vmem, hbm] + [vmem] * 4 + [hbm] * 5,
        out_specs=(vmem, hbm, hbm, vmem),
        scratch_shapes=[
            buffer(qkv.shape, low),
            buffer((width, slots), low),
            buffer((width, slots), f32),
            buffer((width, slots), f32),
            buffer((width, slots), f32),
            buffer((heads, slots), f32),
            buffer((slots, model), low),
            buffer((slots, model), low),
            buffer((3 * rows, model), low),
            buffer((2, pairs, slice_rows, columns), low),
            buffer((3, 4, pairs, slice_rows, columns), low),
            buffer((pairs - 1, 3, 4, slice_rows, columns), low),
            buffer((2, slots // 2, DEPTH), low),
            buffer((chunks, pairs, share, 3 * width), low),
            buffer((chunks, pairs - 1, share, 3 * width), low),
            buffer((2, chunks, share, 3 * width), low),
            buffer((3, 3, slice_rows, columns), low),
            buffer((3, slice_rows, columns), low),
            buffer(small.shape, f32),
            buffer(small.shape, f32),
            buffer((pairs,) + small.shape, f32),
            buffer((4,) + small.shape, f32),
            dma((4,)),
            dma((4,)),
            dma,
            dma((2,)),
            dma((3,)),
            dma((3,)),
            dma((3, pairs - 1)),
            dma((3, pairs - 1)),
            dma((4, CHUNKS)),
            dma((4, CHUNKS)),
            dma((4, CHUNKS)),
            dma((4, CHUNKS)),
            dma,
            dma((2,)),
            dma((chunks, pairs - 1)),
            dma((chunks, pairs - 1)),
            dma((chunks,)),
            dma((chunks,)),
            dma((chunks, pairs)),
            dma((chunks, pairs)),
            dma((chunks, pairs)),
            dma((chunks,)),
            dma((3,)),
            dma((3,)),
            dma((pairs,)),
            dma((pairs,)),
            dma((2 * pairs,)),
            dma,
            dma((2,)),
            dma((pairs,)),
            dma((pairs,)),
            dma((4,)),
            dma((4,)),
        ],
        compiler_params=pltpu.CompilerParams(
            collective_id=2, has_side_effects=True, vmem_limit_bytes=65_500_000
        ),
        name="attention_backward",
    )(span, qkv, out, logsum, factor, weights, small, split, grad_out, grad_up, grad_down, gathered)


def per_device(
    inputs,
    cotangent,
    gain_attn,
    gain_mlp,
    query_scale,
    w_query,
    w_key,
    w_value,
    w_out,
    w_up,
    w_down,
    lengths,
    offsets,
):
    low = jnp.bfloat16
    f32 = jnp.float32
    here = Place()
    n_dp = lax.axis_size("dp")
    local_rows, model = inputs.shape
    seq_slots = local_rows * 4
    width_local = w_query.shape[1]
    head_dim = query_scale.shape[0]
    heads_local = width_local // head_dim
    pairs = n_dp // 2
    swap_core = [(i, i ^ 1) for i in range(n_dp)]

    split = min(pairs, 4)
    mlp_native = jnp.stack([w_out, jnp.transpose(w_up), w_down])
    mlp_native = mlp_native.reshape(3, split, width_local // split, model)
    native = jnp.concatenate(
        [jnp.transpose(w_query), jnp.transpose(w_key), jnp.transpose(w_value)]
    )
    own_span = jnp.concatenate([lengths, offsets])
    other_span = lax.ppermute(own_span, "dp", swap_core)
    group_span = jnp.where(here.main, own_span, other_span)
    own_rows = here.t * local_rows + jnp.arange(local_rows, dtype=jnp.int32)
    row_valid = ((own_rows >= offsets[0]) & (own_rows < offsets[0] + lengths[0])).astype(f32)

    residual = inputs.astype(f32)
    normed, inverse_one = rms_forward(residual, gain_attn)
    scale_const = LOG_TWO_E / math.sqrt(head_dim)
    soft = jax.nn.softplus(query_scale)
    factor = jnp.tile(soft * scale_const, heads_local)[:, None]
    gathered, stacked_w, qkv, attended, logsum, attended_rows, mlp_w = attention_forward(
        group_span,
        normed.astype(low),
        native,
        jnp.concatenate([factor, jnp.ones((2 * width_local, 1), f32)]),
        mlp_native,
        heads_local,
    )
    mlp_w = mlp_w.reshape(3, model, model)
    w_out_all, w_up_all, w_down_all = mlp_w[0], mlp_w[1], mlp_w[2]

    hidden_one = residual + contract_rows(attended_rows, w_out_all)
    second, inverse_two = rms_forward(hidden_one, gain_mlp)
    second_low = second.astype(low)
    before_act = contract_cols(second_low, w_up_all)
    activated = jax.nn.silu(before_act).astype(low)
    output = hidden_one + jnp.dot(activated, w_down_all, preferred_element_type=f32)
    grad_hidden_out = cotangent.astype(f32) * row_valid[:, None]
    grad_low = grad_hidden_out.astype(low)
    grad_act = contract_cols(grad_low, w_down_all)
    grad_pre = (grad_act * silu_slope(before_act)).astype(low)
    grad_second = jnp.dot(grad_pre, w_up_all, preferred_element_type=f32)
    grad_hidden = grad_hidden_out + rms_backward(hidden_one, inverse_two, gain_mlp, grad_second)
    branch_low = grad_hidden.astype(low)
    grad_att_rows = contract_cols(w_out_all, branch_low).astype(low)

    grad_w_down = contract_rows(activated, grad_low)
    grad_w_up_t = contract_rows(grad_pre, second_low)
    grad_w_out = jnp.dot(attended_rows, branch_low, preferred_element_type=f32)
    gain_two_part = jnp.sum(grad_w_up_t * w_up_all.astype(f32), axis=0)

    def by_member(grad):
        return grad.astype(low).reshape(4, pairs, width_local // pairs, model)

    small = jnp.concatenate(
        [jnp.zeros((1, model), f32), gain_two_part[None], jnp.zeros((6, model), f32)]
    )
    grad_first, mlp_all, qkv_all, small = attention_backward(
        group_span, qkv, attended, logsum, factor, stacked_w, small, grad_att_rows,
        by_member(grad_w_out), by_member(grad_w_up_t), by_member(grad_w_down), gathered,
    )
    grad_input = grad_hidden + rms_backward(
        residual, inverse_one, gain_attn, grad_first.astype(f32)
    )
    grad_gain_one = small[0] / gain_attn
    grad_gain_two = small[1] / gain_mlp
    scale_sum = jnp.sum(small[2, :width_local].reshape(heads_local, head_dim), axis=0)
    grad_scale = scale_sum * jax.nn.sigmoid(query_scale) / soft
    mlp_all = mlp_all.astype(f32).reshape(pairs, 2, 3, width_local // pairs, model // 2)

    def final_weight(w):
        return jnp.transpose(mlp_all[:, :, w], (0, 2, 1, 3)).reshape(width_local, model)

    grad_out_final = final_weight(0)
    grad_up_final = jnp.transpose(final_weight(1))
    grad_down_final = final_weight(2)
    qkv_all = qkv_all.astype(f32).reshape(model, 3 * width_local)
    return (
        output.astype(low),
        grad_input,
        grad_gain_one,
        grad_gain_two,
        grad_scale,
        qkv_all[:, :width_local],
        qkv_all[:, width_local : 2 * width_local],
        qkv_all[:, 2 * width_local :],
        grad_out_final,
        grad_up_final,
        grad_down_final,
    )


def solution(mesh):
    rows = P(("dp", "tensor"), None)
    cols_t = P(None, "tensor")
    rows_t = P("tensor", None)
    return jax.shard_map(
        per_device,
        mesh=mesh,
        in_specs=(
            rows, rows, P(), P(), P(), cols_t, cols_t, cols_t, rows_t, cols_t, rows_t, P("dp"), P("dp"),
        ),
        out_specs=(
            rows, rows, P(), P(), P(), cols_t, cols_t, cols_t, rows_t, cols_t, rows_t,
        ),
        check_vma=False,
    )
```

```python
import functools
import math

import jax
import jax.numpy as jnp
from jax import lax
from jax.experimental import pallas as pl
from jax.experimental.pallas import tpu as pltpu
from jax.sharding import PartitionSpec as P

EPSILON = 1e-06
LOG_TWO_E = 1.4426950408889634
MESH_ID = pl.DeviceIdType.MESH
CHUNKS = 4


def rms_forward(values, gain):
    inverse = lax.rsqrt(jnp.mean(values * values, axis=-1, keepdims=True) + EPSILON)
    return (values * inverse * gain, inverse)


def rms_backward(values, inverse, gain, grad_normed):
    scaled = values * inverse
    grad_scaled = grad_normed * gain
    return inverse * (
        grad_scaled - scaled * jnp.mean(grad_scaled * scaled, axis=-1, keepdims=True)
    )


class Place:
    def __init__(self):
        self.d = lax.axis_index("dp")
        self.t = lax.axis_index("tensor")
        self.c = lax.rem(self.d, 2)
        self.g = self.t // 2
        self.base = self.d - self.c
        self.pairs = lax.axis_size("dp") // 2
        self.pair = self.d // 2
        self.main = self.c == self.g
        self.pos = jnp.where(self.c == 0, self.t, 3 - self.t)

    def device(self, seq, pos):
        return (self.base + seq, jnp.where(seq == 0, pos, 3 - pos))

    def across(self, step):
        return (2 * lax.rem(self.pair + step, self.pairs) + self.c, self.t)

    def partner(self):
        return (self.base + 1 - self.c, self.t)

    def quarter(self):
        return jnp.where(self.main, self.t, lax.rem(self.t + 2, 4))


def pair_barrier(here, plane=False):
    barrier = pltpu.get_barrier_semaphore()
    others = []
    for step in range(1, 8):
        code = lax.rem(here.c * 4 + here.t + step, 8)
        others.append((here.base + code // 4, lax.rem(code, 4)))
    if plane:
        others += [here.across(step) for step in range(1, here.pairs)]
    for device in others:
        pl.semaphore_signal(barrier, inc=1, device_id=device, device_id_type=MESH_ID)
    pl.semaphore_wait(barrier, len(others))


def remote(src, dst, send, recv, device):
    return pltpu.make_async_remote_copy(
        src_ref=src, dst_ref=dst, send_sem=send, recv_sem=recv, device_id=device, device_id_type=MESH_ID
    )


def dg(left, right, left_dim, right_dim):
    return lax.dot_general(
        left, right, (((left_dim,), (right_dim,)), ((), ())), preferred_element_type=jnp.float32
    )


TILE = 512
MASKED = -1e30


def readable(span, first_key, first_query):
    shape = (TILE, TILE)
    key = first_key + lax.broadcasted_iota(jnp.int32, shape, 0)
    query = first_query + lax.broadcasted_iota(jnp.int32, shape, 1)
    valid = (key >= span[1]) & (key < span[1] + span[0])
    return (valid & (key <= query)) | (key == query)


def key_bias(span, first_key):
    key = first_key + lax.broadcasted_iota(jnp.int32, (TILE, 1), 0)
    return jnp.where((key >= span[1]) & (key < span[1] + span[0]), 0.0, MASKED)


def forward_kernel(
    span, own, native, factor, mlp_native,
    gathered, weights, qkv, out, logsum, rows_out, mlp_out, mlp_up, mlp_down,
    highest, summed, total,
    keep_sem, send_z, send_c, recv,
    native_sem, weight_sent, spread_sent, weight_got,
    rows_sent, rows_got, rows_local,
    mlp_local, line_sent, line_got, plane_sent, share_sent, mlp_have,
):
    heads = logsum.shape[0]
    width, slots = out.shape
    dim = width // heads
    low, f32 = qkv.dtype, jnp.float32
    here = Place()
    pairs = here.pairs
    split = mlp_native.shape[1]
    rows = own.shape[0]
    part = rows // CHUNKS
    columns = own.shape[1] // 2
    tall = native.shape[0] // split
    blocks = slots // TILE
    partner = here.partner()
    pair_barrier(here, plane=True)

    def half(core):
        return pl.ds(pl.multiple_of(core * columns, columns), columns)

    def weight_piece(ref, pair, core):
        return ref.at[pl.ds(pl.multiple_of(pair * tall, tall), tall), half(core)]

    line = lax.rem(here.t + 2, 4)
    weight_copy = remote(
        weight_piece(native, here.pair, here.c),
        weight_piece(weights, here.pair, here.c),
        weight_sent,
        weight_got.at[here.pair, here.c],
        (here.base + 1 - line // 2, line),
    )
    sends = here.pair < split

    @pl.when(sends)
    def _():
        weight_copy.start()

    native_copy = pltpu.make_async_copy(native, weights, native_sem)

    @pl.when(here.main)
    def _():
        native_copy.start()

    def place(seq, k, ch):
        block = jnp.where(seq == 0, k, 3 - k)
        return gathered.at[pl.ds(pl.multiple_of(block * rows + ch * part, part), part)]

    def copy(src, k, ch, seq, device, send):
        return remote(src, place(seq, k, ch), send.at[k, ch], recv.at[k, ch], device)

    def own_copy(k, ch, device, send):
        return copy(own.at[pl.ds(ch * part, part)], k, ch, here.c, device, send)

    def pass_copy(k, ch, device, send):
        return copy(place(here.g, k, ch), k, ch, here.g, device, send)

    def arrived(k, ch):
        pass_copy(k, ch, partner, send_z).wait_recv()

    keep = pltpu.make_async_copy(
        own, gathered.at[pl.ds(pl.multiple_of(here.t * rows, rows), rows)], keep_sem
    )
    near = here.device(here.c, jnp.where(here.pos == 1, 0, 1))

    @pl.when(here.main)
    def _():
        keep.start()
        for ch in range(CHUNKS):
            own_copy(here.pos, ch, near, send_z).start()
            own_copy(here.pos, ch, partner, send_c).start()

    @pl.when(jnp.logical_not(here.main))
    def _():
        for ch in range(CHUNKS):
            own_copy(here.pos, ch, near, send_z).start()

    kept = (mlp_out, mlp_up, mlp_down)

    def mlp_piece(w, quarter, pair, core):
        return kept[w].at[quarter, pair, :, half(core)]

    def mlp_line(w, step):
        return remote(
            mlp_native.at[w, here.pair, :, half(here.c)],
            mlp_piece(w, here.t, here.pair, here.c),
            line_sent.at[w, step - 1],
            line_got.at[w, here.t],
            (here.d, lax.rem(here.t + step, 4)),
        )

    def mlp_plane(w, n, step):
        quarter = lax.rem(here.t + n, 4)
        piece = mlp_piece(w, quarter, here.pair, here.c)
        return remote(
            piece, piece, plane_sent.at[w, n - 1, step], mlp_have.at[w, quarter, here.pair, here.c],
            here.across(step),
        )

    def mlp_core(w, n, pair):
        quarter = lax.rem(here.t + n, 4)
        piece = mlp_piece(w, quarter, pair, here.c)
        return remote(
            piece, piece, share_sent.at[w, n - 1, pair], mlp_have.at[w, quarter, pair, here.c], partner
        )

    def mlp_arrived(w, n, pair, core):
        quarter = lax.rem(here.t + n, 4)
        piece = mlp_piece(w, quarter, pair, core)
        remote(
            piece, piece, share_sent.at[0, 0, 0], mlp_have.at[w, quarter, pair, core], partner
        ).wait_recv()

    def mlp_keep(w):
        return pltpu.make_async_copy(mlp_native.at[w], kept[w].at[here.t], mlp_local.at[w])

    @pl.when(sends)
    def _():
        for w in range(3):
            for step in range(1, 4):
                mlp_line(w, step).start()

    for w in range(3):
        mlp_keep(w).start()

    def from_line():
        @pl.when(sends)
        def _():
            for w in range(3):
                for n in (1, 3, 2):
                    quarter = lax.rem(here.t + n, 4)
                    piece = mlp_piece(w, quarter, here.pair, here.c)
                    remote(
                        piece, piece, share_sent.at[0, 0, 0], line_got.at[w, quarter], partner
                    ).wait_recv()
                    for step in range(1, pairs):
                        mlp_plane(w, n, step).start()
                    mlp_core(w, n, here.pair).start()

    def spread(core, step):
        piece = weight_piece(weights, here.pair, core)
        return remote(
            piece, piece, spread_sent.at[core, step - 1], weight_got.at[here.pair, core], here.across(step)
        )

    def weight_arrived(pair, core):
        piece = weight_piece(weights, pair, core)
        remote(piece, piece, weight_sent, weight_got.at[pair, core], partner).wait_recv()

    @pl.when(jnp.logical_not(here.main))
    def _():
        @pl.when(sends)
        def _():
            for core in range(2):
                weight_arrived(here.pair, core)
                for step in range(1, pairs):
                    spread(core, step).start()

        for pair in range(split):
            @pl.when(here.pair != pair)
            def _(pair=pair):
                for core in range(2):
                    weight_arrived(pair, core)

    @pl.when(here.main)
    def _():
        native_copy.wait()
        keep.wait()

    @pl.when(here.pos == 1)
    def _():
        for ch in range(CHUNKS):
            arrived(2, ch)
            pass_copy(2, ch, near, send_z).start()
            pass_copy(2, ch, partner, send_c).start()
            arrived(0, ch)
            pass_copy(0, ch, partner, send_c).start()
        for ch in range(CHUNKS):
            arrived(3, ch)
            pass_copy(3, ch, near, send_z).start()
            pass_copy(3, ch, partner, send_c).start()

    quarter = here.quarter()

    def into(q):
        return rows_out.at[pl.ds(pl.multiple_of(q * width, width), width)]

    def done_columns(i):
        return out.at[:, pl.ds(pl.multiple_of(i * TILE, TILE), TILE)]

    def rows_copy(i):
        return remote(
            done_columns(i), into(quarter), rows_sent.at[i], rows_got.at[quarter], (here.base + here.g, i)
        )

    rows_keep = pltpu.make_async_copy(done_columns(here.t), into(here.t), rows_local)

    def finish(i):
        qs = pl.ds(pl.multiple_of(i * TILE, TILE), TILE)
        for h in range(heads):
            hs = pl.ds(h * dim, dim)
            sums = summed[h : h + 1, qs]
            out[hs, qs] = (total[hs, qs] / sums).astype(out.dtype)
            logsum[h : h + 1, qs] = highest[h : h + 1, qs] + jnp.log(sums)
        stays = here.main & (here.t == i)

        @pl.when(stays)
        def _():
            rows_keep.start()

        @pl.when(jnp.logical_not(stays))
        def _():
            rows_copy(i).start()

    highest[...] = jnp.full_like(highest, MASKED)
    summed[...] = jnp.zeros_like(summed)
    total[...] = jnp.zeros_like(total)

    @pl.loop(0, blocks)
    def _(s):
        b = jnp.where(here.g == 0, s, blocks - 1 - s)
        last = (here.g == 1) & (s == blocks - 1)

        @pl.when((here.pos == 0) & (s >= 1))
        def _():
            for ch in range(CHUNKS):
                arrived(s, ch)
                pass_copy(s, ch, partner, send_c).start()

        @pl.when(jnp.logical_not(here.main))
        def _():
            for ch in range(CHUNKS):
                arrived(s, ch)

        bs = pl.ds(pl.multiple_of(b * TILE, TILE), TILE)
        for w in range(3):
            at = pl.ds(w * width, width)
            qkv[at, bs] = (dg(weights[at], gathered[bs], 1, 1) * factor[at]).astype(low)

        def tile(i, j, diagonal):
            qs = pl.ds(pl.multiple_of(i * TILE, TILE), TILE)
            ks = pl.ds(pl.multiple_of(j * TILE, TILE), TILE)
            if diagonal:
                allowed = readable(span, j * TILE, i * TILE)
            else:
                bias = key_bias(span, j * TILE)
            for h in range(heads):
                hs = pl.ds(h * dim, dim)
                scores = dg(qkv[pl.ds(width + h * dim, dim), ks], qkv[hs, qs], 0, 0)
                scores = jnp.where(allowed, scores, MASKED) if diagonal else scores + bias
                before = highest[h : h + 1, qs]
                after = jnp.maximum(before, jnp.max(scores, axis=0, keepdims=True))
                expo = jnp.exp(scores - after)
                scale = jnp.exp(before - after)
                summed[h : h + 1, qs] = summed[h : h + 1, qs] * scale + jnp.sum(expo, axis=0, keepdims=True)
                highest[h : h + 1, qs] = after
                total[hs, qs] = total[hs, qs] * scale + dg(
                    qkv[pl.ds(2 * width + h * dim, dim), ks], expo.astype(low), 1, 0
                )

        tile(b, b, True)

        @pl.when(last)
        def _():
            finish(b)

        @pl.loop(0, s)
        def _(n):
            i = jnp.where(here.g == 0, b, b + 1 + n)
            tile(i, jnp.where(here.g == 0, n, b), False)

            @pl.when(last)
            def _():
                finish(i)

        @pl.when(here.g == 0)
        def _():
            finish(b)

        @pl.when(s == 2)
        def _():
            from_line()

    for w in range(3):
        for n in (1, 3, 2):
            for pair in range(split):
                @pl.when(here.pair != pair)
                def _(w=w, n=n, pair=pair):
                    mlp_arrived(w, n, pair, here.c)
                    mlp_core(w, n, pair).start()

    for block in range(4):
        stays = here.main & (here.t == block)

        @pl.when(stays)
        def _():
            rows_keep.wait()

        @pl.when(jnp.logical_not(stays))
        def _(block=block):
            rows_copy(block).wait_send()
            remote(
                done_columns(0), into(block), rows_sent.at[0], rows_got.at[block], partner
            ).wait_recv()

    for w in range(3):
        for n in range(1, 4):
            for pair in range(split):
                mlp_arrived(w, n, pair, 1 - here.c)
                mlp_core(w, n, pair).wait_send()
        mlp_keep(w).wait()

    @pl.when(sends)
    def _():
        weight_copy.wait_send()
        for w in range(3):
            for step in range(1, 4):
                mlp_line(w, step).wait_send()
                for across in range(1, pairs):
                    mlp_plane(w, step, across).wait_send()

    @pl.when(sends & jnp.logical_not(here.main))
    def _():
        for core in range(2):
            for step in range(1, pairs):
                spread(core, step).wait_send()

    for ch in range(CHUNKS):
        own_copy(here.pos, ch, near, send_z).wait_send()

    @pl.when(here.main)
    def _():
        for ch in range(CHUNKS):
            own_copy(here.pos, ch, partner, send_c).wait_send()

    @pl.when(here.pos == 0)
    def _():
        for k in (1, 2, 3):
            for ch in range(CHUNKS):
                pass_copy(k, ch, partner, send_c).wait_send()

    @pl.when(here.pos == 1)
    def _():
        for ch in range(CHUNKS):
            pass_copy(0, ch, partner, send_c).wait_send()
            for k in (2, 3):
                pass_copy(k, ch, near, send_z).wait_send()
                pass_copy(k, ch, partner, send_c).wait_send()


def attention_forward(span, own, native, factor, mlp_native, heads):
    rows, model = own.shape
    slots = 4 * rows
    width = native.shape[0] // 3
    _, split, tall, _ = mlp_native.shape
    pairs = lax.axis_size("dp") // 2
    low, f32 = own.dtype, jnp.float32
    vmem = pl.BlockSpec(memory_space=pltpu.VMEM)
    hbm = pl.BlockSpec(memory_space=pl.ANY)
    dma = pltpu.SemaphoreType.DMA
    return pl.pallas_call(
        forward_kernel,
        out_shape=(
            jax.ShapeDtypeStruct((slots, model), low),
            jax.ShapeDtypeStruct(native.shape, low),
            jax.ShapeDtypeStruct((3 * width, slots), low),
            jax.ShapeDtypeStruct((width, slots), low),
            jax.ShapeDtypeStruct((heads, slots), f32),
            jax.ShapeDtypeStruct((4 * width, rows), low),
        )
        + (jax.ShapeDtypeStruct((4, split, tall, model), low),) * 3,
        in_specs=[pl.BlockSpec(memory_space=pltpu.SMEM), hbm, hbm, vmem, hbm],
        out_specs=(vmem,) * 5 + (hbm,) * 4,
        scratch_shapes=[
            pltpu.VMEM((heads, slots), f32),
            pltpu.VMEM((heads, slots), f32),
            pltpu.VMEM((width, slots), f32),
            dma,
            dma((4, CHUNKS)),
            dma((4, CHUNKS)),
            dma((4, CHUNKS)),
            dma,
            dma,
            dma((2, pairs - 1)),
            dma((split, 2)),
            dma((4,)),
            dma((4,)),
            dma,
            dma((3,)),
            dma((3, 3)),
            dma((3, 4)),
            dma((3, 3, pairs)),
            dma((3, 3, split)),
            dma((3, 4, split, 2)),
        ],
        compiler_params=pltpu.CompilerParams(
            collective_id=1, has_side_effects=True, vmem_limit_bytes=50 * 1024 * 1024
        ),
        name="attention_forward",
    )(span, own, native, factor, mlp_native)


def middle_kernel(
    span, gain, attended, residual, cotangent, w_out_in, w_up_in, w_down_in,
    output, grad_hidden, chip_sum, small, grad,
    w_out, w_up, w_down, second, activated, grad_low, grad_pre, branch, grad_att, weight_grad,
    load_sem, split_sent, split_got, local_sem, give_sent, give_got,
):
    here = Place()
    low, f32 = output.dtype, jnp.float32
    rows, model = output.shape
    width = grad.shape[0]
    pairs, tall = weight_grad.shape[2], weight_grad.shape[3]
    half_rows = rows // 2
    partner = here.partner()
    loads = [
        pltpu.make_async_copy(src, dst, load_sem.at[w])
        for w, (src, dst) in enumerate(((w_out_in, w_out), (w_up_in, w_up), (w_down_in, w_down)))
    ]
    for load in loads:
        load.start()
    pair_barrier(here)

    def of(q, r):
        return grad_att.at[
            pl.ds(pl.multiple_of(q * width, width), width), pl.ds(pl.multiple_of(r * half_rows, half_rows), half_rows)
        ]

    def into(block, r):
        return grad.at[:, pl.ds(pl.multiple_of(block * rows + r * half_rows, half_rows), half_rows)]

    def split_copy(q, r):
        native = (q // 2) == here.c
        seq = jnp.where(native, here.c, 1 - here.c)
        line = jnp.where(native, q, (q + 2) % 4)
        return remote(
            of(q, r), into(here.t, r), split_sent.at[q, r], split_got.at[here.t, r], (here.base + seq, line)
        )

    def keep(r):
        return pltpu.make_async_copy(of(here.t, r), into(here.t, r), local_sem.at[r])

    loads[0].wait()

    @pl.loop(0, 2)
    def _(r):
        at = pl.ds(pl.multiple_of(r * half_rows, half_rows), half_rows)
        hidden = residual[at].astype(f32) + dg(attended[:, at], w_out[...], 0, 0)
        inverse = lax.rsqrt(jnp.mean(hidden * hidden, axis=-1, keepdims=True) + EPSILON)
        scaled = hidden * inverse
        second[at] = (scaled * gain[...]).astype(low)

        @pl.when(r == 0)
        def _():
            loads[1].wait()

        before = dg(second[at], w_up[...], 1, 1)
        sigmoid = jax.nn.sigmoid(before)
        activated[at] = (before * sigmoid).astype(low)

        @pl.when(r == 0)
        def _():
            loads[2].wait()

        position = here.t * rows + r * half_rows + lax.broadcasted_iota(jnp.int32, (half_rows, 1), 0)
        valid = (position >= span[1]) & (position < span[1] + span[0])
        grad_out = jnp.where(valid, cotangent[at].astype(f32), 0.0)
        grad_low[at] = grad_out.astype(low)
        grad_act = dg(grad_low[at], w_down[...], 1, 1)
        grad_pre[at] = (grad_act * (sigmoid * (1.0 + before * (1.0 - sigmoid)))).astype(low)
        grad_scaled = dg(grad_pre[at], w_up[...], 1, 0) * gain[...]
        grad_rows = grad_out + inverse * (
            grad_scaled - scaled * jnp.mean(grad_scaled * scaled, axis=-1, keepdims=True)
        )
        grad_hidden[at] = grad_rows
        branch[at] = grad_rows.astype(low)
        grad_att[:, at] = dg(w_out[...], branch[at], 1, 1).astype(low)
        for q in range(4):
            stays = here.main & (here.t == q)

            @pl.when(stays)
            def _():
                keep(r).start()

            @pl.when(jnp.logical_not(stays))
            def _(q=q):
                split_copy(q, r).start()

        output[at] = (hidden + dg(activated[at], w_down[...], 1, 0)).astype(low)

    columns = chip_sum.shape[-1]
    two = 2 * width

    def half(core):
        return pl.ds(pl.multiple_of(core * columns, columns), columns)

    def give(w):
        return remote(
            weight_grad.at[w, :, :, :, half(1 - here.c)], chip_sum.at[w], give_sent.at[w], give_got.at[w], partner
        )

    small[...] = jnp.zeros_like(small)
    for w in range(3):
        for quarters in range(2):
            at = pl.ds(quarters * two, two)
            if w == 0:
                grads = dg(attended[at], branch[...], 1, 0)
            elif w == 1:
                grads = dg(grad_pre[:, at], second[...], 0, 0)
                small[1:2] += jnp.sum(grads * w_up[at].astype(f32), axis=0, keepdims=True)
            else:
                grads = dg(activated[:, at], grad_low[...], 0, 0)
            for q in range(2):
                for p in range(pairs):
                    first = q * width + p * tall
                    weight_grad[w, 2 * quarters + q, p] = grads[first : first + tall].astype(low)
        give(w).start()

    for w in range(3):
        give(w).wait_recv()

        @pl.loop(0, 4)
        def _(q, w=w):
            @pl.loop(0, pairs)
            def _(p):
                mine = weight_grad[w, q, p, :, half(here.c)]
                chip_sum[w, q, p] = (chip_sum[w, q, p].astype(f32) + mine.astype(f32)).astype(low)

    for r in range(2):
        for q in range(4):
            stays = here.main & (here.t == q)

            @pl.when(stays)
            def _(r=r):
                keep(r).wait()

            @pl.when(jnp.logical_not(stays))
            def _(q=q, r=r):
                remote(of(0, r), into(q, r), split_sent.at[0, r], split_got.at[q, r], partner).wait_recv()
                split_copy(q, r).wait_send()

    for w in range(3):
        give(w).wait_send()


def feed_forward(span, gain, attended, residual, cotangent, w_out, w_up, w_down, width, pairs):
    rows, model = residual.shape
    low, f32 = residual.dtype, jnp.float32
    vmem = pl.BlockSpec(memory_space=pltpu.VMEM)
    hbm = pl.BlockSpec(memory_space=pl.ANY)
    dma = pltpu.SemaphoreType.DMA
    tall = width // pairs
    return pl.pallas_call(
        middle_kernel,
        out_shape=(
            jax.ShapeDtypeStruct((rows, model), low),
            jax.ShapeDtypeStruct((rows, model), f32),
            jax.ShapeDtypeStruct((3, 4, pairs, tall, model // 2), low),
            jax.ShapeDtypeStruct((8, model), f32),
            jax.ShapeDtypeStruct((width, 4 * rows), low),
        ),
        in_specs=[pl.BlockSpec(memory_space=pltpu.SMEM)] + [vmem] * 4 + [hbm] * 3,
        out_specs=(vmem,) * 4 + (hbm,),
        scratch_shapes=[pltpu.VMEM((model, model), low)] * 3
        + [pltpu.VMEM((rows, model), low)] * 5
        + [
            pltpu.VMEM((model, rows), low),
            pltpu.VMEM((3, 4, pairs, tall, model), low),
            dma((3,)),
            dma((4, 2)),
            dma((4, 2)),
            dma((2,)),
            dma((3,)),
            dma((3,)),
        ],
        compiler_params=pltpu.CompilerParams(
            collective_id=3, has_side_effects=True, vmem_limit_bytes=65_000_000
        ),
        name="feed_forward",
    )(span, gain, attended, residual, cotangent, w_out, w_up, w_down)


def backward_kernel(
    span, qkv, out, logsum, factor, weights, small, grad, chip_sum, gathered,
    rows_grad, mlp_all, qkv_all, small_all,
    result, query_sum, key_sum, value_sum, term,
    partial, from_core, from_line, own_sum, pass_sum, plane_in,
    normed, weight_grad, qkv_in, qkv_swap, mlp_in, mlp_sum,
    small_own, small_pair, small_plane, small_line,
    own_sem, pass_sem, plane_sent, plane_got,
    send_c, send_z, recv_c, recv_z,
    out_sem, normed_sem, qkv_sent, qkv_got, cross_sent, cross_got, qkv_spread, qkv_share, qkv_have, qkv_local,
    line_sent, line_got, mlp_spread, mlp_share, mlp_have, mlp_local,
    small_sems, small_across_sent, small_across_got, small_along_sent, small_along_got,
):
    heads = logsum.shape[0]
    width, slots = out.shape
    dim = width // heads
    low, f32 = qkv.dtype, jnp.float32
    here = Place()
    pairs = here.pairs
    rows = rows_grad.shape[0]
    part = rows // CHUNKS
    partner = here.partner()
    pair_barrier(here, plane=True)
    blocks = slots // TILE

    columns = chip_sum.shape[-1]

    def half(core):
        return pl.ds(pl.multiple_of(core * columns, columns), columns)

    square = pairs == 4
    by_x = here.pair + 1 - 2 * lax.rem(here.pair, 2)
    by_y = lax.rem(here.pair + 2, 4)
    corner = 3 - here.pair

    def at_pair(pair):
        return (2 * pair + here.c, here.t)

    def plane_first(w, side, kind):
        to, pair = (by_x, by_y)[side], ((by_x, by_y)[side], corner)[kind]
        return remote(
            chip_sum.at[w, pl.ds(2 * side, 2), pair], plane_in.at[w, side, kind],
            plane_sent.at[w, 2 * side + kind], plane_got.at[w, 2 * side + kind], at_pair(to),
        )

    def plane_second(w, side):
        return remote(
            pass_sum.at[w, side], plane_in.at[w, side, 2], plane_sent.at[w, 4 + side], plane_got.at[w, 4 + side],
            at_pair((by_y, by_x)[side]),
        )

    def plane_copy(w, step):
        return remote(
            chip_sum.at[w, :, lax.rem(here.pair + step, pairs)],
            plane_in.at[step - 1, w],
            plane_sent.at[w, step - 1],
            plane_got.at[w, step - 1],
            here.across(step),
        )

    def plane_start(w):
        if square:
            for kind in (1, 0):
                for side in range(2):
                    plane_first(w, side, kind).start()
        else:
            for step in range(1, pairs):
                plane_copy(w, step).start()

    def plane_pass(w):
        if square:
            for side in range(2):
                plane_first(w, side, 1).wait_recv()
                for q in range(2):
                    pass_sum[w, side, q] = (
                        pass_sum[w, side, q].astype(f32) + plane_in[w, side, 1, q].astype(f32)
                    ).astype(low)
                plane_second(w, side).start()

    def plane_sent_all(w):
        if square:
            for side in range(2):
                plane_first(w, side, 0).wait_send()
                plane_first(w, side, 1).wait_send()
                plane_second(w, side).wait_send()
        else:
            for step in range(1, pairs):
                plane_copy(w, step).wait_send()

    pass_loads = []
    if square:
        pass_loads = [
            pltpu.make_async_copy(
                chip_sum.at[:, pl.ds(2 * side, 2), (by_y, by_x)[side]], pass_sum.at[:, side], pass_sem.at[side]
            )
            for side in range(2)
        ]
    for load in pass_loads:
        load.start()
    own_load = pltpu.make_async_copy(chip_sum.at[:, :, here.pair], own_sum, own_sem)
    own_load.start()
    for w in range(3):
        plane_start(w)
    out_copy = pltpu.make_async_copy(out, result.at[pl.ds(0, width)], out_sem)
    out_copy.start()
    query_sum[...] = jnp.zeros_like(query_sum)
    key_sum[...] = jnp.zeros_like(key_sum)
    value_sum[...] = jnp.zeros_like(value_sum)
    out_copy.wait()
    own_load.wait()
    for load in pass_loads:
        load.wait()
    for h in range(heads):
        hs = pl.ds(h * dim, dim)
        term[h : h + 1] = jnp.sum(grad[hs].astype(f32) * result[hs].astype(f32), axis=0, keepdims=True)

    def span_of(seq, k, ch):
        block = jnp.where(seq == 0, k, 3 - k)
        return pl.ds(pl.multiple_of(block * rows + ch * part, part), part)

    def piece(k, ch):
        return pl.ds(pl.multiple_of(k * rows + ch * part, part), part)

    def line_piece(k, ch):
        return piece(k % 3 if isinstance(k, int) else lax.rem(k, 3), ch)

    def line_rows(ch):
        return pl.ds(ch * part, part)

    def core_copy(k, ch):
        at = span_of(here.g, k, ch)
        return remote(partial.at[at], from_core.at[piece(k, ch)], send_c.at[k, ch], recv_c.at[k, ch], partner)

    def line_copy(k, ch):
        at = span_of(here.g, k, ch)
        return remote(
            partial.at[at],
            from_line.at[line_piece(k, ch)],
            send_z.at[k, ch],
            recv_z.at[k, ch],
            here.device(here.c, jnp.where(here.pos == 0, 1, 0)),
        )

    def home_copy(k, ch):
        at = span_of(here.g, k, ch)
        return remote(
            partial.at[at], rows_grad.at[line_rows(ch)], send_z.at[k, ch], recv_z.at[k, ch], here.device(here.c, k)
        )

    def core_sum(k, ch):
        core_copy(k, ch).wait_recv()
        return partial[span_of(here.g, k, ch)].astype(f32) + from_core[piece(k, ch)].astype(f32)

    def with_line(k, ch):
        line_copy(k, ch).wait_recv()
        return core_sum(k, ch) + from_line[line_piece(k, ch)].astype(f32)

    def pass_on(k):
        for ch in range(CHUNKS):
            partial[span_of(here.g, k, ch)] = core_sum(k, ch).astype(low)
            line_copy(k, ch).start()

    def send_home(k):
        for ch in range(CHUNKS):
            partial[span_of(here.g, k, ch)] = with_line(k, ch).astype(low)
            home_copy(k, ch).start()

    def mlp_line(w, step):
        line = lax.rem(here.t + step, 4)
        return remote(
            own_sum.at[w, line], mlp_in.at[w, step - 1], line_sent.at[w, step - 1],
            line_got.at[w, step - 1], (here.d, line),
        )

    def plane_total(w):
        if square:
            for side in range(2):
                plane_first(w, side, 0).wait_recv()
                plane_second(w, side).wait_recv()
                for q in range(2):
                    own_sum[w, 2 * side + q] = (
                        own_sum[w, 2 * side + q].astype(f32)
                        + plane_in[w, side, 0, q].astype(f32)
                        + plane_in[w, side, 2, q].astype(f32)
                    ).astype(low)
        else:
            for step in range(1, pairs):
                plane_copy(w, step).wait_recv()

            @pl.loop(0, 4)
            def _(q):
                total = own_sum[w, q].astype(f32)
                for step in range(1, pairs):
                    total += plane_in[step - 1, w, q].astype(f32)
                own_sum[w, q] = total.astype(low)

        for step in range(1, 4):
            mlp_line(w, step).start()

    @pl.loop(0, blocks)
    def _(s):
        b = jnp.where(here.g == 0, blocks - 1 - s, s)
        k = blocks - 1 - s

        def tile(i, j, diagonal):
            qs = pl.ds(pl.multiple_of(i * TILE, TILE), TILE)
            ks = pl.ds(pl.multiple_of(j * TILE, TILE), TILE)
            if diagonal:
                allowed = readable(span, j * TILE, i * TILE)
            else:
                bias = key_bias(span, j * TILE)
            for h in range(heads):
                hs = pl.ds(h * dim, dim)
                ke = pl.ds(width + h * dim, dim)
                va = pl.ds(2 * width + h * dim, dim)
                scores = dg(qkv[ke, ks], qkv[hs, qs], 0, 0)
                scores = jnp.where(allowed, scores, MASKED) if diagonal else scores + bias
                probs = jnp.exp(scores - logsum[h : h + 1, qs])
                grad_probs = dg(qkv[va, ks], grad[hs, qs], 0, 0)
                grad_scores = (probs * (grad_probs - term[h : h + 1, qs])).astype(low)
                value_sum[hs, ks] += dg(grad[hs, qs], probs.astype(low), 1, 1)
                key_sum[hs, ks] += dg(qkv[hs, qs], grad_scores, 1, 1)
                query_sum[hs, qs] += dg(qkv[ke, ks], grad_scores, 1, 0)

        tile(b, b, True)

        @pl.when((here.pos == 0) & (s >= 1))
        def _():
            pass_on(k + 1)

        @pl.when(s >= 1)
        def _():
            plane_pass(s - 1)

        @pl.when(s >= 2)
        def _():
            plane_total(s - 2)

        @pl.loop(0, blocks - 1 - s)
        def _(n):
            tile(jnp.where(here.g == 0, b, b + 1 + n), jnp.where(here.g == 0, n, b), False)

        bs = pl.ds(pl.multiple_of(b * TILE, TILE), TILE)
        result[pl.ds(0, width), bs] = (query_sum[:, bs] * factor[...]).astype(low)
        result[pl.ds(width, width), bs] = key_sum[:, bs].astype(low)
        result[pl.ds(2 * width, width), bs] = value_sum[:, bs].astype(low)
        partial[bs] = dg(result[:, bs], weights[...], 0, 0).astype(low)

        @pl.when(jnp.logical_not(here.main))
        def _():
            for ch in range(CHUNKS):
                core_copy(k, ch).start()

    plane_total(2)

    @pl.when(here.pos == 1)
    def _():
        send_home(3)

    chunks, _, _, share, _ = weight_grad.shape
    depth = pairs * share

    half_slots = slots // 2

    def load(i, part_of):
        return pltpu.make_async_copy(
            gathered.at[
                pl.ds(part_of * half_slots, half_slots), pl.ds(pl.multiple_of(i * depth, depth), depth)
            ],
            normed.at[part_of],
            normed_sem.at[part_of],
        )

    def turn(i):
        even = lax.rem(i, 2) == 0
        return jnp.where(even, by_x, by_y), jnp.where(even, by_y, by_x)

    def qkv_send(i, step):
        if square:
            first, second = turn(i)
            to = (first, first, second)[step - 1]
            pair = (first, corner, second)[step - 1]
            device = at_pair(to)
        else:
            pair, device = lax.rem(here.pair + step, pairs), here.across(step)
        return remote(
            weight_grad.at[i, pair], qkv_in.at[i, step - 1], qkv_sent.at[i, step - 1], qkv_got.at[i, step - 1], device
        )

    first_steps = (2, 1) if square else range(1, pairs)

    small_own[...] = small[...]
    load(0, 0).start()
    load(0, 1).start()

    @pl.loop(0, chunks)
    def _(i):
        at = pl.ds(pl.multiple_of(i * depth, depth), depth)
        load(i, 0).wait()
        grads = dg(normed[0], result[:, :half_slots], 0, 1)

        @pl.when(i + 1 < chunks)
        def _():
            load(i + 1, 0).start()

        load(i, 1).wait()
        grads += dg(normed[1], result[:, half_slots:], 0, 1)

        @pl.when(i + 1 < chunks)
        def _():
            load(i + 1, 1).start()

        for p in range(pairs):
            for w in range(3):
                weight_grad[i, p, w] = grads[
                    p * share : (p + 1) * share, w * width : (w + 1) * width
                ].astype(low)
        for step in first_steps:
            qkv_send(i, step).start()
        weighted = grads * jnp.transpose(weights[:, at]).astype(f32)
        by_row = jnp.sum(weighted, axis=1, keepdims=True)
        small_own[0:1, at] = jnp.transpose(jnp.broadcast_to(by_row, (depth, 128)))[0:1]
        small_own[2:3, pl.ds(0, 3 * width)] += jnp.sum(weighted, axis=0, keepdims=True)

    small_copy = remote(small_own, small_pair, small_sems.at[0], small_sems.at[1], partner)
    small_copy.start()

    @pl.when(here.pos == 1)
    def _():
        pass_on(0)

    def mlp_piece(w, pair, core):
        return mlp_all.at[w, pair, :, half(core)]

    def mlp_out(w, step):
        return remote(
            mlp_sum.at[w], mlp_piece(w, here.pair, here.c), mlp_spread.at[w, step], mlp_have.at[w, here.d],
            here.across(step),
        )

    def mlp_own(w):
        return remote(
            mlp_sum.at[w], mlp_piece(w, here.pair, here.c), mlp_share.at[w, 0], mlp_have.at[w, here.d], partner
        )

    def mlp_keep(w):
        return pltpu.make_async_copy(mlp_sum.at[w], mlp_piece(w, here.pair, here.c), mlp_local.at[w])

    def mlp_core(w, step):
        pair = lax.rem(here.pair + step, pairs)
        piece = mlp_piece(w, pair, here.c)
        return remote(piece, piece, mlp_share.at[w, step], mlp_have.at[w, 2 * pair + here.c], partner)

    def mlp_arrived(w, pair, core):
        remote(
            mlp_sum.at[w], mlp_piece(w, pair, core), mlp_share.at[w, 0], mlp_have.at[w, 2 * pair + core], partner
        ).wait_recv()

    @pl.when(here.pos == 1)
    def _():
        send_home(2)

    line = lax.rem(here.t + 2, 4)

    def cross(i):
        return remote(
            qkv_swap.at[0, i], qkv_swap.at[1, i], cross_sent.at[i], cross_got.at[i],
            (here.base + line // 2, line),
        )

    def qkv_out(i, step):
        return remote(
            qkv_swap.at[0, i], qkv_all.at[:, i, here.pair], qkv_spread.at[i, step], qkv_have.at[i, here.pair],
            here.across(step),
        )

    def qkv_own(i):
        return remote(
            qkv_swap.at[0, i], qkv_all.at[:, i, here.pair], qkv_share.at[i, 0], qkv_have.at[i, here.pair], partner
        )

    def qkv_keep(i):
        return pltpu.make_async_copy(qkv_swap.at[0, i], qkv_all.at[:, i, here.pair], qkv_local.at[i])

    def qkv_core(i, step):
        pair = lax.rem(here.pair + step, pairs)
        return remote(
            qkv_all.at[:, i, pair], qkv_all.at[:, i, pair], qkv_share.at[i, step], qkv_have.at[i, pair], partner
        )

    def finish(i):
        @pl.when(here.main)
        def _():
            cross(i).wait_recv()
            qkv_swap[0, i] = (qkv_swap[0, i].astype(f32) + qkv_swap[1, i].astype(f32)).astype(low)
            qkv_keep(i).start()
            for step in range(1, pairs):
                qkv_out(i, step).start()
            qkv_own(i).start()

    def qkv_pass(i):
        if square:
            qkv_send(i, 2).wait_recv()
            _, second = turn(i)
            weight_grad[i, second] = (weight_grad[i, second].astype(f32) + qkv_in[i, 1].astype(f32)).astype(low)
            qkv_send(i, 3).start()

    def qkv_total(i):
        total = weight_grad[i, here.pair].astype(f32)
        for step in (1, 3) if square else range(1, pairs):
            qkv_send(i, step).wait_recv()
            total += qkv_in[i, step - 1].astype(f32)
        qkv_swap[0, i] = total.astype(low)

        @pl.when(jnp.logical_not(here.main))
        def _():
            cross(i).start()

    @pl.loop(0, chunks + 2)
    def _(n):
        @pl.when(n < chunks)
        def _():
            qkv_pass(n)

        @pl.when((n >= 1) & (n <= chunks))
        def _():
            qkv_total(n - 1)

        @pl.when(n >= 2)
        def _():
            finish(n - 2)

    @pl.loop(0, 3)
    def _(w):
        total = own_sum[w, here.t].astype(f32)
        for step in range(1, 4):
            mlp_line(w, step).wait_recv()
            total += mlp_in[w, step - 1].astype(f32)
        mlp_sum[w] = total.astype(low)
        for step in range(1, pairs):
            mlp_out(w, step).start()
        mlp_own(w).start()
        mlp_keep(w).start()

    small_copy.wait_recv()
    small_plane[here.pair] = small_own[...] + small_pair[...]

    def small_across(step):
        return remote(
            small_plane.at[here.pair], small_plane.at[here.pair], small_across_sent.at[step],
            small_across_got.at[here.pair], here.across(step),
        )

    def small_along(step):
        return remote(
            small_line.at[here.t], small_line.at[here.t], small_along_sent.at[step], small_along_got.at[here.t],
            (here.d, lax.rem(here.t + step, 4)),
        )

    for step in range(1, pairs):
        small_across(step).start()

    for step in range(1, pairs):
        pair = lax.rem(here.pair + step, pairs)
        remote(
            small_own, small_plane.at[pair], small_across_sent.at[0], small_across_got.at[pair], partner
        ).wait_recv()
    plane_total = small_plane[0]
    for pair in range(1, pairs):
        plane_total += small_plane[pair]
    small_line[here.t] = plane_total
    for step in range(1, 4):
        small_along(step).start()

    @pl.when(here.pos == 0)
    def _():
        for ch in range(CHUNKS):
            rows_grad[line_rows(ch)] = with_line(0, ch).astype(low)
        for k in (1, 2, 3):
            for ch in range(CHUNKS):
                line_copy(k, ch).wait_send()

    @pl.when(here.pos == 1)
    def _():
        for ch in range(CHUNKS):
            rows_grad[line_rows(ch)] = with_line(1, ch).astype(low)
        for ch in range(CHUNKS):
            line_copy(0, ch).wait_send()
            for k in (2, 3):
                home_copy(k, ch).wait_send()

    for k in (2, 3):
        @pl.when(here.pos == k)
        def _(k=k):
            for ch in range(CHUNKS):
                remote(
                    partial.at[piece(0, ch)], rows_grad.at[line_rows(ch)], send_z.at[0, ch], recv_z.at[k, ch], partner
                ).wait_recv()

    for step in range(1, 4):
        other = lax.rem(here.t + step, 4)
        remote(
            small_own, small_line.at[other], small_along_sent.at[0], small_along_got.at[other], partner
        ).wait_recv()
    small_all[...] = (small_line[0] + small_line[1]) + (small_line[2] + small_line[3])

    @pl.when(here.main)
    def _():
        @pl.loop(0, chunks)
        def _(i):
            for step in range(1, pairs):
                qkv_core(i, step).wait_recv()
                qkv_core(i, step).start()

    @pl.loop(0, 3)
    def _(w):
        for step in range(1, pairs):
            mlp_arrived(w, lax.rem(here.pair + step, pairs), here.c)
            mlp_core(w, step).start()

    @pl.when(here.main)
    def _():
        @pl.loop(0, chunks)
        def _(i):
            qkv_keep(i).wait()
            qkv_own(i).wait_send()
            for step in range(1, pairs):
                qkv_out(i, step).wait_send()
                qkv_core(i, step).wait_send()

    @pl.when(jnp.logical_not(here.main))
    def _():
        @pl.loop(0, chunks)
        def _(i):
            cross(i).wait_send()
            for step in range(pairs):
                qkv_core(i, step).wait_recv()

        for k in range(4):
            for ch in range(CHUNKS):
                core_copy(k, ch).wait_send()

    @pl.loop(0, 3)
    def _(w):
        for step in range(pairs):
            mlp_arrived(w, lax.rem(here.pair + step, pairs), 1 - here.c)
        mlp_keep(w).wait()
        mlp_own(w).wait_send()
        for step in range(1, pairs):
            mlp_out(w, step).wait_send()
            mlp_core(w, step).wait_send()
        for step in range(1, 4):
            mlp_line(w, step).wait_send()

    for w in range(3):
        plane_sent_all(w)

    @pl.loop(0, chunks)
    def _(i):
        for step in range(1, pairs):
            qkv_send(i, step).wait_send()

    for step in range(1, pairs):
        small_across(step).wait_send()
    for step in range(1, 4):
        small_along(step).wait_send()
    small_copy.wait_send()


DEPTH = 256


def attention_backward(
    span, qkv, out, logsum, factor, weights, small, grad, chip_sum, gathered
):
    width, slots = out.shape
    heads = logsum.shape[0]
    rows, model = slots // 4, weights.shape[1]
    low, f32 = qkv.dtype, jnp.float32
    _, _, pairs, slice_rows, columns = chip_sum.shape
    chunks, share = model // DEPTH, DEPTH // pairs
    vmem = pl.BlockSpec(memory_space=pltpu.VMEM)
    hbm = pl.BlockSpec(memory_space=pl.ANY)
    dma = pltpu.SemaphoreType.DMA
    buffer = pltpu.VMEM
    return pl.pallas_call(
        backward_kernel,
        out_shape=(
            jax.ShapeDtypeStruct((rows, model), low),
            jax.ShapeDtypeStruct((3, pairs, slice_rows, model), low),
            jax.ShapeDtypeStruct((3, chunks, pairs, share, width), low),
            jax.ShapeDtypeStruct(small.shape, f32),
        ),
        in_specs=[pl.BlockSpec(memory_space=pltpu.SMEM), vmem, hbm] + [vmem] * 5 + [hbm] * 2,
        out_specs=(vmem, hbm, hbm, vmem),
        scratch_shapes=[
            buffer(qkv.shape, low),
            buffer((width, slots), f32),
            buffer((width, slots), f32),
            buffer((width, slots), f32),
            buffer((heads, slots), f32),
            buffer((slots, model), low),
            buffer((slots, model), low),
            buffer((3 * rows, model), low),
            buffer((3, 4, slice_rows, columns), low),
            buffer((3, 2, 2, slice_rows, columns) if pairs == 4 else (8, 128), low),
            buffer(
                (3, 2, 3, 2, slice_rows, columns) if pairs == 4 else (pairs - 1, 3, 4, slice_rows, columns), low
            ),
            buffer((2, slots // 2, DEPTH), low),
            buffer((chunks, pairs, 3, share, width), low),
            buffer((chunks, pairs - 1, 3, share, width), low),
            buffer((2, chunks, 3, share, width), low),
            buffer((3, 3, slice_rows, columns), low),
            buffer((3, slice_rows, columns), low),
            buffer(small.shape, f32),
            buffer(small.shape, f32),
            buffer((pairs,) + small.shape, f32),
            buffer((4,) + small.shape, f32),
            dma,
            dma((2,)),
            dma((3, max(6, pairs - 1))),
            dma((3, max(6, pairs - 1))),
            dma((4, CHUNKS)),
            dma((4, CHUNKS)),
            dma((4, CHUNKS)),
            dma((4, CHUNKS)),
            dma,
            dma((2,)),
            dma((chunks, pairs - 1)),
            dma((chunks, pairs - 1)),
            dma((chunks,)),
            dma((chunks,)),
            dma((chunks, pairs)),
            dma((chunks, pairs)),
            dma((chunks, pairs)),
            dma((chunks,)),
            dma((3, 3)),
            dma((3, 3)),
            dma((3, pairs)),
            dma((3, pairs)),
            dma((3, 2 * pairs)),
            dma((3,)),
            dma((2,)),
            dma((pairs,)),
            dma((pairs,)),
            dma((4,)),
            dma((4,)),
        ],
        compiler_params=pltpu.CompilerParams(
            collective_id=2, has_side_effects=True, vmem_limit_bytes=65_500_000
        ),
        name="attention_backward",
    )(span, qkv, out, logsum, factor, weights, small, grad, chip_sum, gathered)


def per_device(
    inputs,
    cotangent,
    gain_attn,
    gain_mlp,
    query_scale,
    w_query,
    w_key,
    w_value,
    w_out,
    w_up,
    w_down,
    lengths,
    offsets,
):
    low = jnp.bfloat16
    f32 = jnp.float32
    here = Place()
    n_dp = lax.axis_size("dp")
    local_rows, model = inputs.shape
    seq_slots = local_rows * 4
    width_local = w_query.shape[1]
    head_dim = query_scale.shape[0]
    heads_local = width_local // head_dim
    pairs = n_dp // 2
    swap_core = [(i, i ^ 1) for i in range(n_dp)]

    split = min(pairs, 4)
    mlp_native = jnp.stack([w_out, jnp.transpose(w_up), w_down])
    mlp_native = mlp_native.reshape(3, split, width_local // split, model)
    native = jnp.concatenate(
        [jnp.transpose(w_query), jnp.transpose(w_key), jnp.transpose(w_value)]
    )
    own_span = jnp.concatenate([lengths, offsets])
    other_span = lax.ppermute(own_span, "dp", swap_core)
    group_span = jnp.where(here.main, own_span, other_span)
    residual = inputs.astype(f32)
    normed, inverse_one = rms_forward(residual, gain_attn)
    scale_const = LOG_TWO_E / math.sqrt(head_dim)
    soft = jax.nn.softplus(query_scale)
    factor = jnp.tile(soft * scale_const, heads_local)[:, None]
    gathered, stacked_w, qkv, attended, logsum, attended_rows, *mlp_w = attention_forward(
        group_span,
        normed.astype(low),
        native,
        jnp.concatenate([factor, jnp.ones((2 * width_local, 1), f32)]),
        mlp_native,
        heads_local,
    )
    w_out_all, w_up_all, w_down_all = (weight.reshape(model, model) for weight in mlp_w)
    output, grad_hidden, chip_sum, small, grad_attended = feed_forward(
        own_span, gain_mlp[None], attended_rows, inputs, cotangent, w_out_all, w_up_all, w_down_all,
        width_local, pairs,
    )
    grad_first, mlp_all, qkv_all, small = attention_backward(
        group_span, qkv, attended, logsum, factor, stacked_w, small, grad_attended, chip_sum, gathered
    )
    grad_input = grad_hidden + rms_backward(
        residual, inverse_one, gain_attn, grad_first.astype(f32)
    )
    grad_gain_one = small[0] / gain_attn
    grad_gain_two = small[1] / gain_mlp
    scale_sum = jnp.sum(small[2, :width_local].reshape(heads_local, head_dim), axis=0)
    grad_scale = scale_sum * jax.nn.sigmoid(query_scale) / soft
    mlp_all = mlp_all.reshape(3, width_local, model)
    qkv_all = qkv_all.reshape(3, model, width_local)

    return (
        output,
        grad_input,
        grad_gain_one,
        grad_gain_two,
        grad_scale,
        qkv_all[0].astype(f32),
        qkv_all[1].astype(f32),
        qkv_all[2].astype(f32),
        mlp_all[0].astype(f32),
        jnp.transpose(mlp_all[1].astype(f32)),
        mlp_all[2].astype(f32),
    )


def solution(mesh):
    rows = P(("dp", "tensor"), None)
    cols_t = P(None, "tensor")
    rows_t = P("tensor", None)
    return jax.shard_map(
        per_device,
        mesh=mesh,
        in_specs=(
            rows, rows, P(), P(), P(), cols_t, cols_t, cols_t, rows_t, cols_t, rows_t, P("dp"), P("dp"),
        ),
        out_specs=(
            rows, rows, P(), P(), P(), cols_t, cols_t, cols_t, rows_t, cols_t, rows_t,
        ),
        check_vma=False,
    )
```

```python
import functools
import math

import jax
import jax.numpy as jnp
from jax import lax
from jax.experimental import pallas as pl
from jax.experimental.pallas import tpu as pltpu
from jax.sharding import PartitionSpec as P

EPSILON = 1e-06
LOG_TWO_E = 1.4426950408889634
MESH_ID = pl.DeviceIdType.MESH
CHUNKS = 4


def rms_forward(values, gain):
    inverse = lax.rsqrt(jnp.mean(values * values, axis=-1, keepdims=True) + EPSILON)
    return (values * inverse * gain, inverse)


def rms_backward(values, inverse, gain, grad_normed):
    scaled = values * inverse
    grad_scaled = grad_normed * gain
    return inverse * (
        grad_scaled - scaled * jnp.mean(grad_scaled * scaled, axis=-1, keepdims=True)
    )


class Place:
    def __init__(self):
        self.d = lax.axis_index("dp")
        self.t = lax.axis_index("tensor")
        self.c = lax.rem(self.d, 2)
        self.g = self.t // 2
        self.base = self.d - self.c
        self.pairs = lax.axis_size("dp") // 2
        self.pair = self.d // 2
        self.main = self.c == self.g
        self.pos = jnp.where(self.c == 0, self.t, 3 - self.t)

    def device(self, seq, pos):
        return (self.base + seq, jnp.where(seq == 0, pos, 3 - pos))

    def across(self, step):
        return (2 * lax.rem(self.pair + step, self.pairs) + self.c, self.t)

    def partner(self):
        return (self.base + 1 - self.c, self.t)

    def quarter(self):
        return jnp.where(self.main, self.t, lax.rem(self.t + 2, 4))


def pair_barrier(here, plane=False):
    barrier = pltpu.get_barrier_semaphore()
    others = []
    for step in range(1, 8):
        code = lax.rem(here.c * 4 + here.t + step, 8)
        others.append((here.base + code // 4, lax.rem(code, 4)))
    if plane:
        others += [here.across(step) for step in range(1, here.pairs)]
    for device in others:
        pl.semaphore_signal(barrier, inc=1, device_id=device, device_id_type=MESH_ID)
    pl.semaphore_wait(barrier, len(others))


def remote(src, dst, send, recv, device):
    return pltpu.make_async_remote_copy(
        src_ref=src, dst_ref=dst, send_sem=send, recv_sem=recv, device_id=device, device_id_type=MESH_ID
    )


def dg(left, right, left_dim, right_dim):
    return lax.dot_general(
        left, right, (((left_dim,), (right_dim,)), ((), ())), preferred_element_type=jnp.float32
    )


TILE = 512
MASKED = -1e30


def readable(span, first_key, first_query):
    shape = (TILE, TILE)
    key = first_key + lax.broadcasted_iota(jnp.int32, shape, 0)
    query = first_query + lax.broadcasted_iota(jnp.int32, shape, 1)
    valid = (key >= span[1]) & (key < span[1] + span[0])
    return (valid & (key <= query)) | (key == query)


def key_bias(span, first_key):
    key = first_key + lax.broadcasted_iota(jnp.int32, (TILE, 1), 0)
    return jnp.where((key >= span[1]) & (key < span[1] + span[0]), 0.0, MASKED)


def forward_kernel(
    span, own, native, factor, mlp_native,
    gathered, weights, qkv, out, logsum, rows_out, mlp_out, mlp_up, mlp_down,
    highest, summed, total,
    keep_sem, send_z, send_c, recv,
    native_sem, weight_sent, spread_sent, weight_got,
    rows_sent, rows_got, rows_local,
    mlp_local, line_sent, line_got, plane_sent, share_sent, mlp_have,
):
    heads = logsum.shape[0]
    width, slots = out.shape
    dim = width // heads
    low, f32 = qkv.dtype, jnp.float32
    here = Place()
    pairs = here.pairs
    split = mlp_native.shape[1]
    rows = own.shape[0]
    part = rows // CHUNKS
    columns = own.shape[1] // 2
    tall = native.shape[0] // split
    blocks = slots // TILE
    partner = here.partner()
    pair_barrier(here, plane=True)

    def half(core):
        return pl.ds(pl.multiple_of(core * columns, columns), columns)

    def weight_piece(ref, pair, core):
        return ref.at[pl.ds(pl.multiple_of(pair * tall, tall), tall), half(core)]

    line = lax.rem(here.t + 2, 4)
    weight_copy = remote(
        weight_piece(native, here.pair, here.c),
        weight_piece(weights, here.pair, here.c),
        weight_sent,
        weight_got.at[here.pair, here.c],
        (here.base + 1 - line // 2, line),
    )
    sends = here.pair < split

    @pl.when(sends)
    def _():
        weight_copy.start()

    native_copy = pltpu.make_async_copy(native, weights, native_sem)

    @pl.when(here.main)
    def _():
        native_copy.start()

    def place(seq, k, ch):
        block = jnp.where(seq == 0, k, 3 - k)
        return gathered.at[pl.ds(pl.multiple_of(block * rows + ch * part, part), part)]

    def copy(src, k, ch, seq, device, send):
        return remote(src, place(seq, k, ch), send.at[k, ch], recv.at[k, ch], device)

    def own_copy(k, ch, device, send):
        return copy(own.at[pl.ds(ch * part, part)], k, ch, here.c, device, send)

    def pass_copy(k, ch, device, send):
        return copy(place(here.g, k, ch), k, ch, here.g, device, send)

    def arrived(k, ch):
        pass_copy(k, ch, partner, send_z).wait_recv()

    keep = pltpu.make_async_copy(
        own, gathered.at[pl.ds(pl.multiple_of(here.t * rows, rows), rows)], keep_sem
    )
    near = here.device(here.c, jnp.where(here.pos == 1, 0, 1))

    @pl.when(here.main)
    def _():
        keep.start()
        for ch in range(CHUNKS):
            own_copy(here.pos, ch, near, send_z).start()
            own_copy(here.pos, ch, partner, send_c).start()

    @pl.when(jnp.logical_not(here.main))
    def _():
        for ch in range(CHUNKS):
            own_copy(here.pos, ch, near, send_z).start()

    kept = (mlp_out, mlp_up, mlp_down)

    def mlp_piece(w, quarter, pair, core):
        return kept[w].at[quarter, pair, :, half(core)]

    def mlp_line(w, step):
        return remote(
            mlp_native.at[w, here.pair, :, half(here.c)],
            mlp_piece(w, here.t, here.pair, here.c),
            line_sent.at[w, step - 1],
            line_got.at[w, here.t],
            (here.d, lax.rem(here.t + step, 4)),
        )

    def mlp_plane(w, n, step):
        quarter = lax.rem(here.t + n, 4)
        piece = mlp_piece(w, quarter, here.pair, here.c)
        return remote(
            piece, piece, plane_sent.at[w, n - 1, step], mlp_have.at[w, quarter, here.pair, here.c],
            here.across(step),
        )

    def mlp_core(w, n, pair):
        quarter = lax.rem(here.t + n, 4)
        piece = mlp_piece(w, quarter, pair, here.c)
        return remote(
            piece, piece, share_sent.at[w, n - 1, pair], mlp_have.at[w, quarter, pair, here.c], partner
        )

    def mlp_arrived(w, n, pair, core):
        quarter = lax.rem(here.t + n, 4)
        piece = mlp_piece(w, quarter, pair, core)
        remote(
            piece, piece, share_sent.at[0, 0, 0], mlp_have.at[w, quarter, pair, core], partner
        ).wait_recv()

    def mlp_keep(w):
        return pltpu.make_async_copy(mlp_native.at[w], kept[w].at[here.t], mlp_local.at[w])

    def to_line(w):
        @pl.when(sends)
        def _():
            for step in range(1, 4):
                mlp_line(w, step).start()

    to_line(0)
    to_line(1)
    to_line(2)
    for w in range(3):
        mlp_keep(w).start()

    def from_line(w):
        @pl.when(sends)
        def _():
            for n in (1, 3, 2):
                quarter = lax.rem(here.t + n, 4)
                piece = mlp_piece(w, quarter, here.pair, here.c)
                remote(
                    piece, piece, share_sent.at[0, 0, 0], line_got.at[w, quarter], partner
                ).wait_recv()
                for step in range(1, pairs):
                    mlp_plane(w, n, step).start()
                mlp_core(w, n, here.pair).start()

    def spread(core, step):
        piece = weight_piece(weights, here.pair, core)
        return remote(
            piece, piece, spread_sent.at[core, step - 1], weight_got.at[here.pair, core], here.across(step)
        )

    def weight_arrived(pair, core):
        piece = weight_piece(weights, pair, core)
        remote(piece, piece, weight_sent, weight_got.at[pair, core], partner).wait_recv()

    @pl.when(jnp.logical_not(here.main))
    def _():
        @pl.when(sends)
        def _():
            for core in range(2):
                weight_arrived(here.pair, core)
                for step in range(1, pairs):
                    spread(core, step).start()

        for pair in range(split):
            @pl.when(here.pair != pair)
            def _(pair=pair):
                for core in range(2):
                    weight_arrived(pair, core)

    @pl.when(here.main)
    def _():
        native_copy.wait()
        keep.wait()

    @pl.when(here.pos == 1)
    def _():
        for ch in range(CHUNKS):
            arrived(2, ch)
            pass_copy(2, ch, near, send_z).start()
            pass_copy(2, ch, partner, send_c).start()
            arrived(0, ch)
            pass_copy(0, ch, partner, send_c).start()
        for ch in range(CHUNKS):
            arrived(3, ch)
            pass_copy(3, ch, near, send_z).start()
            pass_copy(3, ch, partner, send_c).start()

    quarter = here.quarter()

    def into(q):
        return rows_out.at[pl.ds(pl.multiple_of(q * width, width), width)]

    def done_columns(i):
        return out.at[:, pl.ds(pl.multiple_of(i * TILE, TILE), TILE)]

    def rows_copy(i):
        return remote(
            done_columns(i), into(quarter), rows_sent.at[i], rows_got.at[quarter], (here.base + here.g, i)
        )

    rows_keep = pltpu.make_async_copy(done_columns(here.t), into(here.t), rows_local)

    def finish(i):
        qs = pl.ds(pl.multiple_of(i * TILE, TILE), TILE)
        for h in range(heads):
            hs = pl.ds(h * dim, dim)
            sums = summed[h : h + 1, qs]
            out[hs, qs] = (total[hs, qs] / sums).astype(out.dtype)
            logsum[h : h + 1, qs] = highest[h : h + 1, qs] + jnp.log(sums)
        stays = here.main & (here.t == i)

        @pl.when(stays)
        def _():
            rows_keep.start()

        @pl.when(jnp.logical_not(stays))
        def _():
            rows_copy(i).start()

    highest[...] = jnp.full_like(highest, MASKED)
    summed[...] = jnp.zeros_like(summed)
    total[...] = jnp.zeros_like(total)

    @pl.loop(0, blocks)
    def _(s):
        b = jnp.where(here.g == 0, s, blocks - 1 - s)
        last = (here.g == 1) & (s == blocks - 1)

        @pl.when((here.pos == 0) & (s >= 1))
        def _():
            for ch in range(CHUNKS):
                arrived(s, ch)
                pass_copy(s, ch, partner, send_c).start()

        @pl.when(jnp.logical_not(here.main))
        def _():
            for ch in range(CHUNKS):
                arrived(s, ch)

        @pl.when(s == 0)
        def _():
            from_line(0)

        @pl.when(s == 1)
        def _():
            from_line(1)

        @pl.when(s == 2)
        def _():
            from_line(2)

        bs = pl.ds(pl.multiple_of(b * TILE, TILE), TILE)
        for w in range(3):
            at = pl.ds(w * width, width)
            qkv[at, bs] = (dg(weights[at], gathered[bs], 1, 1) * factor[at]).astype(low)

        def tile(i, j, diagonal):
            qs = pl.ds(pl.multiple_of(i * TILE, TILE), TILE)
            ks = pl.ds(pl.multiple_of(j * TILE, TILE), TILE)
            if diagonal:
                allowed = readable(span, j * TILE, i * TILE)
            else:
                bias = key_bias(span, j * TILE)
            for h in range(heads):
                hs = pl.ds(h * dim, dim)
                scores = dg(qkv[pl.ds(width + h * dim, dim), ks], qkv[hs, qs], 0, 0)
                scores = jnp.where(allowed, scores, MASKED) if diagonal else scores + bias
                before = highest[h : h + 1, qs]
                after = jnp.maximum(before, jnp.max(scores, axis=0, keepdims=True))
                expo = jnp.exp(scores - after)
                scale = jnp.exp(before - after)
                summed[h : h + 1, qs] = summed[h : h + 1, qs] * scale + jnp.sum(expo, axis=0, keepdims=True)
                highest[h : h + 1, qs] = after
                total[hs, qs] = total[hs, qs] * scale + dg(
                    qkv[pl.ds(2 * width + h * dim, dim), ks], expo.astype(low), 1, 0
                )

        tile(b, b, True)

        @pl.when(last)
        def _():
            finish(b)

        @pl.loop(0, s)
        def _(n):
            i = jnp.where(here.g == 0, b, b + 1 + n)
            tile(i, jnp.where(here.g == 0, n, b), False)

            @pl.when(last)
            def _():
                finish(i)

        @pl.when(here.g == 0)
        def _():
            finish(b)


    for w in range(3):
        for n in (1, 3, 2):
            for pair in range(split):
                @pl.when(here.pair != pair)
                def _(w=w, n=n, pair=pair):
                    mlp_arrived(w, n, pair, here.c)
                    mlp_core(w, n, pair).start()

    for block in range(4):
        stays = here.main & (here.t == block)

        @pl.when(stays)
        def _():
            rows_keep.wait()

        @pl.when(jnp.logical_not(stays))
        def _(block=block):
            rows_copy(block).wait_send()
            remote(
                done_columns(0), into(block), rows_sent.at[0], rows_got.at[block], partner
            ).wait_recv()

    for w in range(3):
        for n in range(1, 4):
            for pair in range(split):
                mlp_arrived(w, n, pair, 1 - here.c)
                mlp_core(w, n, pair).wait_send()
        mlp_keep(w).wait()

    @pl.when(sends)
    def _():
        weight_copy.wait_send()
        for w in range(3):
            for step in range(1, 4):
                mlp_line(w, step).wait_send()
                for across in range(1, pairs):
                    mlp_plane(w, step, across).wait_send()

    @pl.when(sends & jnp.logical_not(here.main))
    def _():
        for core in range(2):
            for step in range(1, pairs):
                spread(core, step).wait_send()

    for ch in range(CHUNKS):
        own_copy(here.pos, ch, near, send_z).wait_send()

    @pl.when(here.main)
    def _():
        for ch in range(CHUNKS):
            own_copy(here.pos, ch, partner, send_c).wait_send()

    @pl.when(here.pos == 0)
    def _():
        for k in (1, 2, 3):
            for ch in range(CHUNKS):
                pass_copy(k, ch, partner, send_c).wait_send()

    @pl.when(here.pos == 1)
    def _():
        for ch in range(CHUNKS):
            pass_copy(0, ch, partner, send_c).wait_send()
            for k in (2, 3):
                pass_copy(k, ch, near, send_z).wait_send()
                pass_copy(k, ch, partner, send_c).wait_send()


def attention_forward(span, own, native, factor, mlp_native, heads):
    rows, model = own.shape
    slots = 4 * rows
    width = native.shape[0] // 3
    _, split, tall, _ = mlp_native.shape
    pairs = lax.axis_size("dp") // 2
    low, f32 = own.dtype, jnp.float32
    vmem = pl.BlockSpec(memory_space=pltpu.VMEM)
    hbm = pl.BlockSpec(memory_space=pl.ANY)
    dma = pltpu.SemaphoreType.DMA
    return pl.pallas_call(
        forward_kernel,
        out_shape=(
            jax.ShapeDtypeStruct((slots, model), low),
            jax.ShapeDtypeStruct(native.shape, low),
            jax.ShapeDtypeStruct((3 * width, slots), low),
            jax.ShapeDtypeStruct((width, slots), low),
            jax.ShapeDtypeStruct((heads, slots), f32),
            jax.ShapeDtypeStruct((4 * width, rows), low),
        )
        + (jax.ShapeDtypeStruct((4, split, tall, model), low),) * 3,
        in_specs=[pl.BlockSpec(memory_space=pltpu.SMEM), hbm, hbm, vmem, hbm],
        out_specs=(vmem,) * 5 + (hbm,) * 4,
        scratch_shapes=[
            pltpu.VMEM((heads, slots), f32),
            pltpu.VMEM((heads, slots), f32),
            pltpu.VMEM((width, slots), f32),
            dma,
            dma((4, CHUNKS)),
            dma((4, CHUNKS)),
            dma((4, CHUNKS)),
            dma,
            dma,
            dma((2, pairs - 1)),
            dma((split, 2)),
            dma((4,)),
            dma((4,)),
            dma,
            dma((3,)),
            dma((3, 3)),
            dma((3, 4)),
            dma((3, 3, pairs)),
            dma((3, 3, split)),
            dma((3, 4, split, 2)),
        ],
        compiler_params=pltpu.CompilerParams(
            collective_id=1, has_side_effects=True, vmem_limit_bytes=50 * 1024 * 1024
        ),
        name="attention_forward",
    )(span, own, native, factor, mlp_native)


def middle_kernel(
    span, gain, attended, residual, cotangent, w_out_in, w_up_in, w_down_in,
    output, grad_hidden, chip_sum, small, grad,
    w_out, w_up, w_down, second, activated, grad_low, grad_pre, branch, grad_att, weight_grad,
    load_sem, split_sent, split_got, local_sem, give_sent, give_got,
):
    here = Place()
    low, f32 = output.dtype, jnp.float32
    rows, model = output.shape
    width = grad.shape[0]
    pairs, tall = weight_grad.shape[2], weight_grad.shape[3]
    half_rows = rows // 2
    partner = here.partner()
    loads = [
        pltpu.make_async_copy(src, dst, load_sem.at[w])
        for w, (src, dst) in enumerate(((w_out_in, w_out), (w_up_in, w_up), (w_down_in, w_down)))
    ]
    for load in loads:
        load.start()
    pair_barrier(here)

    def of(q, r):
        return grad_att.at[
            pl.ds(pl.multiple_of(q * width, width), width), pl.ds(pl.multiple_of(r * half_rows, half_rows), half_rows)
        ]

    def into(block, r):
        return grad.at[:, pl.ds(pl.multiple_of(block * rows + r * half_rows, half_rows), half_rows)]

    def split_copy(q, r):
        native = (q // 2) == here.c
        seq = jnp.where(native, here.c, 1 - here.c)
        line = jnp.where(native, q, (q + 2) % 4)
        return remote(
            of(q, r), into(here.t, r), split_sent.at[q, r], split_got.at[here.t, r], (here.base + seq, line)
        )

    def keep(r):
        return pltpu.make_async_copy(of(here.t, r), into(here.t, r), local_sem.at[r])

    loads[0].wait()

    @pl.loop(0, 2)
    def _(r):
        at = pl.ds(pl.multiple_of(r * half_rows, half_rows), half_rows)
        hidden = residual[at].astype(f32) + dg(attended[:, at], w_out[...], 0, 0)
        inverse = lax.rsqrt(jnp.mean(hidden * hidden, axis=-1, keepdims=True) + EPSILON)
        scaled = hidden * inverse
        second[at] = (scaled * gain[...]).astype(low)

        @pl.when(r == 0)
        def _():
            loads[1].wait()

        before = dg(second[at], w_up[...], 1, 1)
        sigmoid = jax.nn.sigmoid(before)
        activated[at] = (before * sigmoid).astype(low)

        @pl.when(r == 0)
        def _():
            loads[2].wait()

        position = here.t * rows + r * half_rows + lax.broadcasted_iota(jnp.int32, (half_rows, 1), 0)
        valid = (position >= span[1]) & (position < span[1] + span[0])
        grad_out = jnp.where(valid, cotangent[at].astype(f32), 0.0)
        grad_low[at] = grad_out.astype(low)
        grad_act = dg(grad_low[at], w_down[...], 1, 1)
        grad_pre[at] = (grad_act * (sigmoid * (1.0 + before * (1.0 - sigmoid)))).astype(low)
        grad_scaled = dg(grad_pre[at], w_up[...], 1, 0) * gain[...]
        grad_rows = grad_out + inverse * (
            grad_scaled - scaled * jnp.mean(grad_scaled * scaled, axis=-1, keepdims=True)
        )
        grad_hidden[at] = grad_rows
        branch[at] = grad_rows.astype(low)
        grad_att[:, at] = dg(w_out[...], branch[at], 1, 1).astype(low)
        for q in range(4):
            stays = here.main & (here.t == q)

            @pl.when(stays)
            def _():
                keep(r).start()

            @pl.when(jnp.logical_not(stays))
            def _(q=q):
                split_copy(q, r).start()

        output[at] = (hidden + dg(activated[at], w_down[...], 1, 0)).astype(low)

    columns = chip_sum.shape[-1]
    two = 2 * width

    def half(core):
        return pl.ds(pl.multiple_of(core * columns, columns), columns)

    def give(w):
        return remote(
            weight_grad.at[w, :, :, :, half(1 - here.c)], chip_sum.at[w], give_sent.at[w], give_got.at[w], partner
        )

    small[...] = jnp.zeros_like(small)
    for w in range(3):
        for quarters in range(2):
            at = pl.ds(quarters * two, two)
            if w == 0:
                grads = dg(attended[at], branch[...], 1, 0)
            elif w == 1:
                grads = dg(grad_pre[:, at], second[...], 0, 0)
                small[1:2] += jnp.sum(grads * w_up[at].astype(f32), axis=0, keepdims=True)
            else:
                grads = dg(activated[:, at], grad_low[...], 0, 0)
            for q in range(2):
                for p in range(pairs):
                    first = q * width + p * tall
                    weight_grad[w, 2 * quarters + q, p] = grads[first : first + tall].astype(low)
        give(w).start()

    for w in range(3):
        give(w).wait_recv()

        @pl.loop(0, 4)
        def _(q, w=w):
            @pl.loop(0, pairs)
            def _(p):
                mine = weight_grad[w, q, p, :, half(here.c)]
                chip_sum[w, q, p] = (chip_sum[w, q, p].astype(f32) + mine.astype(f32)).astype(low)

    for r in range(2):
        for q in range(4):
            stays = here.main & (here.t == q)

            @pl.when(stays)
            def _(r=r):
                keep(r).wait()

            @pl.when(jnp.logical_not(stays))
            def _(q=q, r=r):
                remote(of(0, r), into(q, r), split_sent.at[0, r], split_got.at[q, r], partner).wait_recv()
                split_copy(q, r).wait_send()

    for w in range(3):
        give(w).wait_send()


def feed_forward(span, gain, attended, residual, cotangent, w_out, w_up, w_down, width, pairs):
    rows, model = residual.shape
    low, f32 = residual.dtype, jnp.float32
    vmem = pl.BlockSpec(memory_space=pltpu.VMEM)
    hbm = pl.BlockSpec(memory_space=pl.ANY)
    dma = pltpu.SemaphoreType.DMA
    tall = width // pairs
    return pl.pallas_call(
        middle_kernel,
        out_shape=(
            jax.ShapeDtypeStruct((rows, model), low),
            jax.ShapeDtypeStruct((rows, model), f32),
            jax.ShapeDtypeStruct((3, 4, pairs, tall, model // 2), low),
            jax.ShapeDtypeStruct((8, model), f32),
            jax.ShapeDtypeStruct((width, 4 * rows), low),
        ),
        in_specs=[pl.BlockSpec(memory_space=pltpu.SMEM)] + [vmem] * 4 + [hbm] * 3,
        out_specs=(vmem,) * 4 + (hbm,),
        scratch_shapes=[pltpu.VMEM((model, model), low)] * 3
        + [pltpu.VMEM((rows, model), low)] * 5
        + [
            pltpu.VMEM((model, rows), low),
            pltpu.VMEM((3, 4, pairs, tall, model), low),
            dma((3,)),
            dma((4, 2)),
            dma((4, 2)),
            dma((2,)),
            dma((3,)),
            dma((3,)),
        ],
        compiler_params=pltpu.CompilerParams(
            collective_id=3, has_side_effects=True, vmem_limit_bytes=65_000_000
        ),
        name="feed_forward",
    )(span, gain, attended, residual, cotangent, w_out, w_up, w_down)


def backward_kernel(
    span, qkv, out, logsum, factor, weights, small, grad, chip_sum, gathered,
    rows_grad, out_final, up_final, down_final, qkv_all, small_all,
    result, query_sum, key_sum, value_sum, term,
    partial, from_core, from_line, own_sum, pass_sum, plane_in,
    normed, scale_sum, weight_grad, qkv_in, qkv_swap, mlp_in, mlp_sum,
    small_own, small_pair, small_plane, small_line,
    own_sem, pass_sem, plane_sent, plane_got,
    send_c, send_z, recv_c, recv_z,
    out_sem, normed_sem, qkv_sent, qkv_got, cross_sent, cross_got, qkv_spread, qkv_share, qkv_have, qkv_local,
    line_sent, line_got, mlp_spread, mlp_share, mlp_have, mlp_local,
    small_sems, small_across_sent, small_across_got, small_along_sent, small_along_got,
):
    heads = logsum.shape[0]
    width, slots = out.shape
    dim = width // heads
    low, f32 = qkv.dtype, jnp.float32
    here = Place()
    pairs = here.pairs
    rows = rows_grad.shape[0]
    part = rows // CHUNKS
    partner = here.partner()
    pair_barrier(here, plane=True)
    blocks = slots // TILE

    columns = chip_sum.shape[-1]

    def half(core):
        return pl.ds(pl.multiple_of(core * columns, columns), columns)

    square = pairs == 4
    by_x = here.pair + 1 - 2 * lax.rem(here.pair, 2)
    by_y = lax.rem(here.pair + 2, 4)
    corner = 3 - here.pair

    def at_pair(pair):
        return (2 * pair + here.c, here.t)

    def plane_first(w, side, kind):
        to, pair = (by_x, by_y)[side], ((by_x, by_y)[side], corner)[kind]
        return remote(
            chip_sum.at[w, pl.ds(2 * side, 2), pair], plane_in.at[w, side, kind],
            plane_sent.at[w, 2 * side + kind], plane_got.at[w, 2 * side + kind], at_pair(to),
        )

    def plane_second(w, side):
        return remote(
            pass_sum.at[w, side], plane_in.at[w, side, 2], plane_sent.at[w, 4 + side], plane_got.at[w, 4 + side],
            at_pair((by_y, by_x)[side]),
        )

    def plane_copy(w, step):
        return remote(
            chip_sum.at[w, :, lax.rem(here.pair + step, pairs)],
            plane_in.at[step - 1, w],
            plane_sent.at[w, step - 1],
            plane_got.at[w, step - 1],
            here.across(step),
        )

    def plane_start(w):
        if square:
            for kind in (1, 0):
                for side in range(2):
                    plane_first(w, side, kind).start()
        else:
            for step in range(1, pairs):
                plane_copy(w, step).start()

    def plane_pass(w):
        if square:
            for side in range(2):
                plane_first(w, side, 1).wait_recv()
                for q in range(2):
                    pass_sum[w, side, q] = (
                        pass_sum[w, side, q].astype(f32) + plane_in[w, side, 1, q].astype(f32)
                    ).astype(low)
                plane_second(w, side).start()

    def plane_sent_all(w):
        if square:
            for side in range(2):
                plane_first(w, side, 0).wait_send()
                plane_first(w, side, 1).wait_send()
                plane_second(w, side).wait_send()
        else:
            for step in range(1, pairs):
                plane_copy(w, step).wait_send()

    pass_loads = []
    if square:
        pass_loads = [
            pltpu.make_async_copy(
                chip_sum.at[:, pl.ds(2 * side, 2), (by_y, by_x)[side]], pass_sum.at[:, side], pass_sem.at[side]
            )
            for side in range(2)
        ]
    for load in pass_loads:
        load.start()
    own_load = pltpu.make_async_copy(chip_sum.at[:, :, here.pair], own_sum, own_sem)
    own_load.start()
    for w in range(3):
        plane_start(w)
    out_copy = pltpu.make_async_copy(out, result.at[pl.ds(0, width)], out_sem)
    out_copy.start()
    query_sum[...] = jnp.zeros_like(query_sum)
    key_sum[...] = jnp.zeros_like(key_sum)
    value_sum[...] = jnp.zeros_like(value_sum)
    out_copy.wait()
    own_load.wait()
    for load in pass_loads:
        load.wait()
    for h in range(heads):
        hs = pl.ds(h * dim, dim)
        term[h : h + 1] = jnp.sum(grad[hs].astype(f32) * result[hs].astype(f32), axis=0, keepdims=True)

    def span_of(seq, k, ch):
        block = jnp.where(seq == 0, k, 3 - k)
        return pl.ds(pl.multiple_of(block * rows + ch * part, part), part)

    def piece(k, ch):
        return pl.ds(pl.multiple_of(k * rows + ch * part, part), part)

    def line_piece(k, ch):
        return piece(k % 3 if isinstance(k, int) else lax.rem(k, 3), ch)

    def line_rows(ch):
        return pl.ds(ch * part, part)

    def core_copy(k, ch):
        at = span_of(here.g, k, ch)
        return remote(partial.at[at], from_core.at[piece(k, ch)], send_c.at[k, ch], recv_c.at[k, ch], partner)

    def line_copy(k, ch):
        at = span_of(here.g, k, ch)
        return remote(
            partial.at[at],
            from_line.at[line_piece(k, ch)],
            send_z.at[k, ch],
            recv_z.at[k, ch],
            here.device(here.c, jnp.where(here.pos == 0, 1, 0)),
        )

    def home_copy(k, ch):
        at = span_of(here.g, k, ch)
        return remote(
            partial.at[at], rows_grad.at[line_rows(ch)], send_z.at[k, ch], recv_z.at[k, ch], here.device(here.c, k)
        )

    def core_sum(k, ch):
        core_copy(k, ch).wait_recv()
        return partial[span_of(here.g, k, ch)].astype(f32) + from_core[piece(k, ch)].astype(f32)

    def with_line(k, ch):
        line_copy(k, ch).wait_recv()
        return core_sum(k, ch) + from_line[line_piece(k, ch)].astype(f32)

    def pass_on(k):
        for ch in range(CHUNKS):
            partial[span_of(here.g, k, ch)] = core_sum(k, ch).astype(low)
            line_copy(k, ch).start()

    def send_home(k):
        for ch in range(CHUNKS):
            partial[span_of(here.g, k, ch)] = with_line(k, ch).astype(low)
            home_copy(k, ch).start()

    def mlp_line(w, step):
        line = lax.rem(here.t + step, 4)
        return remote(
            own_sum.at[w, line], mlp_in.at[w, step - 1], line_sent.at[w, step - 1],
            line_got.at[w, step - 1], (here.d, line),
        )

    def plane_total(w):
        if square:
            for side in range(2):
                plane_first(w, side, 0).wait_recv()
                plane_second(w, side).wait_recv()
                for q in range(2):
                    own_sum[w, 2 * side + q] = (
                        own_sum[w, 2 * side + q].astype(f32)
                        + plane_in[w, side, 0, q].astype(f32)
                        + plane_in[w, side, 2, q].astype(f32)
                    ).astype(low)
        else:
            for step in range(1, pairs):
                plane_copy(w, step).wait_recv()

            @pl.loop(0, 4)
            def _(q):
                total = own_sum[w, q].astype(f32)
                for step in range(1, pairs):
                    total += plane_in[step - 1, w, q].astype(f32)
                own_sum[w, q] = total.astype(low)

        for step in range(1, 4):
            mlp_line(w, step).start()

    @pl.loop(0, blocks)
    def _(s):
        b = jnp.where(here.g == 0, blocks - 1 - s, s)
        k = blocks - 1 - s

        def tile(i, j, diagonal):
            qs = pl.ds(pl.multiple_of(i * TILE, TILE), TILE)
            ks = pl.ds(pl.multiple_of(j * TILE, TILE), TILE)
            if diagonal:
                allowed = readable(span, j * TILE, i * TILE)
            else:
                bias = key_bias(span, j * TILE)
            for h in range(heads):
                hs = pl.ds(h * dim, dim)
                ke = pl.ds(width + h * dim, dim)
                va = pl.ds(2 * width + h * dim, dim)
                scores = dg(qkv[ke, ks], qkv[hs, qs], 0, 0)
                scores = jnp.where(allowed, scores, MASKED) if diagonal else scores + bias
                probs = jnp.exp(scores - logsum[h : h + 1, qs])
                grad_probs = dg(qkv[va, ks], grad[hs, qs], 0, 0)
                grad_scores = (probs * (grad_probs - term[h : h + 1, qs])).astype(low)
                value_sum[hs, ks] += dg(grad[hs, qs], probs.astype(low), 1, 1)
                key_sum[hs, ks] += dg(qkv[hs, qs], grad_scores, 1, 1)
                query_sum[hs, qs] += dg(qkv[ke, ks], grad_scores, 1, 0)

        tile(b, b, True)

        @pl.when((here.pos == 0) & (s >= 1))
        def _():
            pass_on(k + 1)

        @pl.when(s >= 1)
        def _():
            plane_pass(s - 1)

        @pl.when(s >= 2)
        def _():
            plane_total(s - 2)

        @pl.loop(0, blocks - 1 - s)
        def _(n):
            tile(jnp.where(here.g == 0, b, b + 1 + n), jnp.where(here.g == 0, n, b), False)

        bs = pl.ds(pl.multiple_of(b * TILE, TILE), TILE)
        result[pl.ds(0, width), bs] = (query_sum[:, bs] * factor[...]).astype(low)
        result[pl.ds(width, width), bs] = key_sum[:, bs].astype(low)
        result[pl.ds(2 * width, width), bs] = value_sum[:, bs].astype(low)
        partial[bs] = dg(result[:, bs], weights[...], 0, 0).astype(low)

        @pl.when(jnp.logical_not(here.main))
        def _():
            for ch in range(CHUNKS):
                core_copy(k, ch).start()

    plane_total(2)

    @pl.when(here.pos == 1)
    def _():
        send_home(3)

    chunks, _, share, depth = weight_grad.shape

    half_slots = slots // 2

    def load(i, part_of):
        return pltpu.make_async_copy(
            gathered.at[
                pl.ds(part_of * half_slots, half_slots), pl.ds(pl.multiple_of(i * depth, depth), depth)
            ],
            normed.at[part_of],
            normed_sem.at[part_of],
        )

    def turn(i):
        even = lax.rem(i, 2) == 0
        return jnp.where(even, by_x, by_y), jnp.where(even, by_y, by_x)

    def qkv_send(i, step):
        if square:
            first, second = turn(i)
            to = (first, first, second)[step - 1]
            pair = (first, corner, second)[step - 1]
            device = at_pair(to)
        else:
            pair, device = lax.rem(here.pair + step, pairs), here.across(step)
        return remote(
            weight_grad.at[i, pair], qkv_in.at[i, step - 1], qkv_sent.at[i, step - 1], qkv_got.at[i, step - 1], device
        )

    first_steps = (2, 1) if square else range(1, pairs)

    small_own[...] = small[...]
    scale_sum[...] = jnp.zeros_like(scale_sum)
    load(0, 0).start()
    load(0, 1).start()

    @pl.loop(0, chunks)
    def _(i):
        at = pl.ds(pl.multiple_of(i * depth, depth), depth)
        load(i, 0).wait()
        grads = dg(result[:, :half_slots], normed[0], 1, 0)

        @pl.when(i + 1 < chunks)
        def _():
            load(i + 1, 0).start()

        load(i, 1).wait()
        grads += dg(result[:, half_slots:], normed[1], 1, 0)

        @pl.when(i + 1 < chunks)
        def _():
            load(i + 1, 1).start()

        for p in range(pairs):
            weight_grad[i, p] = grads[p * share : (p + 1) * share].astype(low)
        for step in first_steps:
            qkv_send(i, step).start()
        weighted = grads * weights[:, at].astype(f32)
        small_own[0:1, at] = jnp.sum(weighted, axis=0, keepdims=True)
        scale_sum[pl.ds(0, width)] += jnp.broadcast_to(
            jnp.sum(weighted[:width], axis=1, keepdims=True), (width, 128)
        )

    padded = scale_sum.shape[0]
    small_own[2:3, pl.ds(0, padded)] = jnp.transpose(scale_sum[...])[0:1]
    small_copy = remote(small_own, small_pair, small_sems.at[0], small_sems.at[1], partner)
    small_copy.start()

    @pl.when(here.pos == 1)
    def _():
        pass_on(0)

    def mlp_piece(w, pair, core):
        return (out_final, up_final, down_final)[w].at[pair, :, half(core)]

    def mlp_out(w, step):
        return remote(
            mlp_sum.at[w], mlp_piece(w, here.pair, here.c), mlp_spread.at[w, step], mlp_have.at[w, here.d],
            here.across(step),
        )

    def mlp_own(w):
        return remote(
            mlp_sum.at[w], mlp_piece(w, here.pair, here.c), mlp_share.at[w, 0], mlp_have.at[w, here.d], partner
        )

    def mlp_keep(w):
        return pltpu.make_async_copy(mlp_sum.at[w], mlp_piece(w, here.pair, here.c), mlp_local.at[w])

    def mlp_core(w, step):
        pair = lax.rem(here.pair + step, pairs)
        piece = mlp_piece(w, pair, here.c)
        return remote(piece, piece, mlp_share.at[w, step], mlp_have.at[w, 2 * pair + here.c], partner)

    def mlp_arrived(w, pair, core):
        remote(
            mlp_sum.at[w], mlp_piece(w, pair, core), mlp_share.at[w, 0], mlp_have.at[w, 2 * pair + core], partner
        ).wait_recv()

    @pl.when(here.pos == 1)
    def _():
        send_home(2)

    line = lax.rem(here.t + 2, 4)

    def cross(i):
        return remote(
            qkv_swap.at[0, i], qkv_swap.at[1, i], cross_sent.at[i], cross_got.at[i],
            (here.base + line // 2, line),
        )

    def qkv_piece(i, pair):
        return qkv_all.at[pair, :, pl.ds(pl.multiple_of(i * depth, depth), depth)]

    def qkv_out(i, step):
        return remote(
            qkv_swap.at[0, i], qkv_piece(i, here.pair), qkv_spread.at[i, step], qkv_have.at[i, here.pair],
            here.across(step),
        )

    def qkv_own(i):
        return remote(
            qkv_swap.at[0, i], qkv_piece(i, here.pair), qkv_share.at[i, 0], qkv_have.at[i, here.pair], partner
        )

    def qkv_keep(i):
        return pltpu.make_async_copy(qkv_swap.at[0, i], qkv_piece(i, here.pair), qkv_local.at[i])

    def qkv_core(i, step):
        pair = lax.rem(here.pair + step, pairs)
        return remote(
            qkv_piece(i, pair), qkv_piece(i, pair), qkv_share.at[i, step], qkv_have.at[i, pair], partner
        )

    def finish(i):
        @pl.when(here.main)
        def _():
            cross(i).wait_recv()
            qkv_swap[0, i] = (qkv_swap[0, i].astype(f32) + qkv_swap[1, i].astype(f32)).astype(low)
            qkv_keep(i).start()
            for step in range(1, pairs):
                qkv_out(i, step).start()
            qkv_own(i).start()

    def qkv_pass(i):
        if square:
            qkv_send(i, 2).wait_recv()
            _, second = turn(i)
            weight_grad[i, second] = (weight_grad[i, second].astype(f32) + qkv_in[i, 1].astype(f32)).astype(low)
            qkv_send(i, 3).start()

    def qkv_total(i):
        total = weight_grad[i, here.pair].astype(f32)
        for step in (1, 3) if square else range(1, pairs):
            qkv_send(i, step).wait_recv()
            total += qkv_in[i, step - 1].astype(f32)
        qkv_swap[0, i] = total.astype(low)

        @pl.when(jnp.logical_not(here.main))
        def _():
            cross(i).start()

    @pl.loop(0, chunks + 2)
    def _(n):
        @pl.when(n < chunks)
        def _():
            qkv_pass(n)

        @pl.when((n >= 1) & (n <= chunks))
        def _():
            qkv_total(n - 1)

        @pl.when(n >= 2)
        def _():
            finish(n - 2)

    for w in range(3):
        total = own_sum[w, here.t].astype(f32)
        for step in range(1, 4):
            mlp_line(w, step).wait_recv()
            total += mlp_in[w, step - 1].astype(f32)
        mlp_sum[w] = total.astype(low)
        for step in range(1, pairs):
            mlp_out(w, step).start()
        mlp_own(w).start()
        mlp_keep(w).start()

    small_copy.wait_recv()
    small_plane[here.pair] = small_own[...] + small_pair[...]

    def small_across(step):
        return remote(
            small_plane.at[here.pair], small_plane.at[here.pair], small_across_sent.at[step],
            small_across_got.at[here.pair], here.across(step),
        )

    def small_along(step):
        return remote(
            small_line.at[here.t], small_line.at[here.t], small_along_sent.at[step], small_along_got.at[here.t],
            (here.d, lax.rem(here.t + step, 4)),
        )

    for step in range(1, pairs):
        small_across(step).start()

    for step in range(1, pairs):
        pair = lax.rem(here.pair + step, pairs)
        remote(
            small_own, small_plane.at[pair], small_across_sent.at[0], small_across_got.at[pair], partner
        ).wait_recv()
    plane_total = small_plane[0]
    for pair in range(1, pairs):
        plane_total += small_plane[pair]
    small_line[here.t] = plane_total
    for step in range(1, 4):
        small_along(step).start()

    @pl.when(here.pos == 0)
    def _():
        for ch in range(CHUNKS):
            rows_grad[line_rows(ch)] = with_line(0, ch).astype(low)
        for k in (1, 2, 3):
            for ch in range(CHUNKS):
                line_copy(k, ch).wait_send()

    @pl.when(here.pos == 1)
    def _():
        for ch in range(CHUNKS):
            rows_grad[line_rows(ch)] = with_line(1, ch).astype(low)
        for ch in range(CHUNKS):
            line_copy(0, ch).wait_send()
            for k in (2, 3):
                home_copy(k, ch).wait_send()

    for k in (2, 3):
        @pl.when(here.pos == k)
        def _(k=k):
            for ch in range(CHUNKS):
                remote(
                    partial.at[piece(0, ch)], rows_grad.at[line_rows(ch)], send_z.at[0, ch], recv_z.at[k, ch], partner
                ).wait_recv()

    for step in range(1, 4):
        other = lax.rem(here.t + step, 4)
        remote(
            small_own, small_line.at[other], small_along_sent.at[0], small_along_got.at[other], partner
        ).wait_recv()
    small_all[...] = (small_line[0] + small_line[1]) + (small_line[2] + small_line[3])

    @pl.when(here.main)
    def _():
        @pl.loop(0, chunks)
        def _(i):
            for step in range(1, pairs):
                qkv_core(i, step).wait_recv()
                qkv_core(i, step).start()

    for w in range(3):
        for step in range(1, pairs):
            mlp_arrived(w, lax.rem(here.pair + step, pairs), here.c)
            mlp_core(w, step).start()

    @pl.when(here.main)
    def _():
        @pl.loop(0, chunks)
        def _(i):
            qkv_keep(i).wait()
            qkv_own(i).wait_send()
            for step in range(1, pairs):
                qkv_out(i, step).wait_send()
                qkv_core(i, step).wait_send()

    @pl.when(jnp.logical_not(here.main))
    def _():
        @pl.loop(0, chunks)
        def _(i):
            cross(i).wait_send()
            for step in range(pairs):
                qkv_core(i, step).wait_recv()

        for k in range(4):
            for ch in range(CHUNKS):
                core_copy(k, ch).wait_send()

    for w in range(3):
        for step in range(pairs):
            mlp_arrived(w, lax.rem(here.pair + step, pairs), 1 - here.c)
        mlp_keep(w).wait()
        mlp_own(w).wait_send()
        for step in range(1, pairs):
            mlp_out(w, step).wait_send()
            mlp_core(w, step).wait_send()
        for step in range(1, 4):
            mlp_line(w, step).wait_send()

    for w in range(3):
        plane_sent_all(w)

    @pl.loop(0, chunks)
    def _(i):
        for step in range(1, pairs):
            qkv_send(i, step).wait_send()

    for step in range(1, pairs):
        small_across(step).wait_send()
    for step in range(1, 4):
        small_along(step).wait_send()
    small_copy.wait_send()


DEPTH = 256


def attention_backward(
    span, qkv, out, logsum, factor, weights, small, grad, chip_sum, gathered
):
    width, slots = out.shape
    heads = logsum.shape[0]
    rows, model = slots // 4, weights.shape[1]
    low, f32 = qkv.dtype, jnp.float32
    _, _, pairs, slice_rows, columns = chip_sum.shape
    chunks, share = model // DEPTH, 3 * width // pairs
    vmem = pl.BlockSpec(memory_space=pltpu.VMEM)
    hbm = pl.BlockSpec(memory_space=pl.ANY)
    dma = pltpu.SemaphoreType.DMA
    buffer = pltpu.VMEM
    return pl.pallas_call(
        backward_kernel,
        out_shape=(
            jax.ShapeDtypeStruct((rows, model), low),
            jax.ShapeDtypeStruct((pairs, slice_rows, model), low),
            jax.ShapeDtypeStruct((pairs, slice_rows, model), low),
            jax.ShapeDtypeStruct((pairs, slice_rows, model), low),
            jax.ShapeDtypeStruct((pairs, share, model), low),
            jax.ShapeDtypeStruct(small.shape, f32),
        ),
        in_specs=[pl.BlockSpec(memory_space=pltpu.SMEM), vmem, hbm] + [vmem] * 5 + [hbm] * 2,
        out_specs=(vmem, hbm, hbm, hbm, hbm, vmem),
        scratch_shapes=[
            buffer(qkv.shape, low),
            buffer((width, slots), f32),
            buffer((width, slots), f32),
            buffer((width, slots), f32),
            buffer((heads, slots), f32),
            buffer((slots, model), low),
            buffer((slots, model), low),
            buffer((3 * rows, model), low),
            buffer((3, 4, slice_rows, columns), low),
            buffer((3, 2, 2, slice_rows, columns) if pairs == 4 else (8, 128), low),
            buffer(
                (3, 2, 3, 2, slice_rows, columns) if pairs == 4 else (pairs - 1, 3, 4, slice_rows, columns), low
            ),
            buffer((2, slots // 2, DEPTH), low),
            buffer((width + -width % 128, 128), f32),
            buffer((chunks, pairs, share, DEPTH), low),
            buffer((chunks, pairs - 1, share, DEPTH), low),
            buffer((2, chunks, share, DEPTH), low),
            buffer((3, 3, slice_rows, columns), low),
            buffer((3, slice_rows, columns), low),
            buffer(small.shape, f32),
            buffer(small.shape, f32),
            buffer((pairs,) + small.shape, f32),
            buffer((4,) + small.shape, f32),
            dma,
            dma((2,)),
            dma((3, max(6, pairs - 1))),
            dma((3, max(6, pairs - 1))),
            dma((4, CHUNKS)),
            dma((4, CHUNKS)),
            dma((4, CHUNKS)),
            dma((4, CHUNKS)),
            dma,
            dma((2,)),
            dma((chunks, pairs - 1)),
            dma((chunks, pairs - 1)),
            dma((chunks,)),
            dma((chunks,)),
            dma((chunks, pairs)),
            dma((chunks, pairs)),
            dma((chunks, pairs)),
            dma((chunks,)),
            dma((3, 3)),
            dma((3, 3)),
            dma((3, pairs)),
            dma((3, pairs)),
            dma((3, 2 * pairs)),
            dma((3,)),
            dma((2,)),
            dma((pairs,)),
            dma((pairs,)),
            dma((4,)),
            dma((4,)),
        ],
        compiler_params=pltpu.CompilerParams(
            collective_id=2, has_side_effects=True, vmem_limit_bytes=65_500_000
        ),
        name="attention_backward",
    )(span, qkv, out, logsum, factor, weights, small, grad, chip_sum, gathered)


def per_device(
    inputs,
    cotangent,
    gain_attn,
    gain_mlp,
    query_scale,
    w_query,
    w_key,
    w_value,
    w_out,
    w_up,
    w_down,
    lengths,
    offsets,
):
    low = jnp.bfloat16
    f32 = jnp.float32
    here = Place()
    n_dp = lax.axis_size("dp")
    local_rows, model = inputs.shape
    seq_slots = local_rows * 4
    width_local = w_query.shape[1]
    head_dim = query_scale.shape[0]
    heads_local = width_local // head_dim
    pairs = n_dp // 2
    swap_core = [(i, i ^ 1) for i in range(n_dp)]

    split = min(pairs, 4)
    mlp_native = jnp.stack([w_out, jnp.transpose(w_up), w_down])
    mlp_native = mlp_native.reshape(3, split, width_local // split, model)
    native = jnp.concatenate(
        [jnp.transpose(w_query), jnp.transpose(w_key), jnp.transpose(w_value)]
    )
    own_span = jnp.concatenate([lengths, offsets])
    other_span = lax.ppermute(own_span, "dp", swap_core)
    group_span = jnp.where(here.main, own_span, other_span)
    residual = inputs.astype(f32)
    normed, inverse_one = rms_forward(residual, gain_attn)
    scale_const = LOG_TWO_E / math.sqrt(head_dim)
    soft = jax.nn.softplus(query_scale)
    factor = jnp.tile(soft * scale_const, heads_local)[:, None]
    gathered, stacked_w, qkv, attended, logsum, attended_rows, *mlp_w = attention_forward(
        group_span,
        normed.astype(low),
        native,
        jnp.concatenate([factor, jnp.ones((2 * width_local, 1), f32)]),
        mlp_native,
        heads_local,
    )
    w_out_all, w_up_all, w_down_all = (weight.reshape(model, model) for weight in mlp_w)
    output, grad_hidden, chip_sum, small, grad_attended = feed_forward(
        own_span, gain_mlp[None], attended_rows, inputs, cotangent, w_out_all, w_up_all, w_down_all,
        width_local, pairs,
    )
    grad_first, grad_out, grad_up, grad_down, qkv_all, small = attention_backward(
        group_span, qkv, attended, logsum, factor, stacked_w, small, grad_attended, chip_sum, gathered
    )
    grad_input = grad_hidden + rms_backward(
        residual, inverse_one, gain_attn, grad_first.astype(f32)
    )
    grad_gain_one = small[0] / gain_attn
    grad_gain_two = small[1] / gain_mlp
    scale_sum = jnp.sum(small[2, :width_local].reshape(heads_local, head_dim), axis=0)
    grad_scale = scale_sum * jax.nn.sigmoid(query_scale) / soft
    qkv_all = qkv_all.reshape(3 * width_local, model)

    def final(weight):
        return weight.reshape(width_local, model).astype(f32)

    return (
        output,
        grad_input,
        grad_gain_one,
        grad_gain_two,
        grad_scale,
        jnp.transpose(final(qkv_all[:width_local])),
        jnp.transpose(final(qkv_all[width_local:2 * width_local])),
        jnp.transpose(final(qkv_all[2 * width_local:3 * width_local])),
        final(grad_out),
        jnp.transpose(final(grad_up)),
        final(grad_down),
    )


def solution(mesh):
    rows = P(("dp", "tensor"), None)
    cols_t = P(None, "tensor")
    rows_t = P("tensor", None)
    return jax.shard_map(
        per_device,
        mesh=mesh,
        in_specs=(
            rows, rows, P(), P(), P(), cols_t, cols_t, cols_t, rows_t, cols_t, rows_t, P("dp"), P("dp"),
        ),
        out_specs=(
            rows, rows, P(), P(), P(), cols_t, cols_t, cols_t, rows_t, cols_t, rows_t,
        ),
        check_vma=False,
    )
```

```python
import functools
import math

import jax
import jax.numpy as jnp
from jax import lax
from jax.experimental import pallas as pl
from jax.experimental.pallas import tpu as pltpu
from jax.sharding import PartitionSpec as P

EPSILON = 1e-06
LOG_TWO_E = 1.4426950408889634
MESH_ID = pl.DeviceIdType.MESH
CHUNKS = 8
BACK_CHUNKS = 2


def rms_forward(values, gain):
    inverse = lax.rsqrt(jnp.mean(values * values, axis=-1, keepdims=True) + EPSILON)
    return (values * inverse * gain, inverse)


def rms_backward(values, inverse, gain, grad_normed):
    scaled = values * inverse
    grad_scaled = grad_normed * gain
    return inverse * (
        grad_scaled - scaled * jnp.mean(grad_scaled * scaled, axis=-1, keepdims=True)
    )


class Place:
    def __init__(self):
        self.d = lax.axis_index("dp")
        self.t = lax.axis_index("tensor")
        self.c = lax.rem(self.d, 2)
        self.g = self.t // 2
        self.base = self.d - self.c
        self.pairs = lax.axis_size("dp") // 2
        self.pair = self.d // 2
        self.main = self.c == self.g
        self.pos = jnp.where(self.c == 0, self.t, 3 - self.t)

    def device(self, seq, pos):
        return (self.base + seq, jnp.where(seq == 0, pos, 3 - pos))

    def across(self, step):
        return (2 * lax.rem(self.pair + step, self.pairs) + self.c, self.t)

    def partner(self):
        return (self.base + 1 - self.c, self.t)

    def quarter(self):
        return jnp.where(self.main, self.t, lax.rem(self.t + 2, 4))


def pair_barrier(here, plane=False):
    barrier = pltpu.get_barrier_semaphore()
    others = []
    for step in range(1, 8):
        code = lax.rem(here.c * 4 + here.t + step, 8)
        others.append((here.base + code // 4, lax.rem(code, 4)))
    if plane:
        others += [here.across(step) for step in range(1, here.pairs)]
    for device in others:
        pl.semaphore_signal(barrier, inc=1, device_id=device, device_id_type=MESH_ID)
    pl.semaphore_wait(barrier, len(others))


def remote(src, dst, send, recv, device):
    return pltpu.make_async_remote_copy(
        src_ref=src, dst_ref=dst, send_sem=send, recv_sem=recv, device_id=device, device_id_type=MESH_ID
    )


def dg(left, right, left_dim, right_dim):
    return lax.dot_general(
        left, right, (((left_dim,), (right_dim,)), ((), ())), preferred_element_type=jnp.float32
    )


TILE = 512
MASKED = -1e30


def readable(span, first_key, first_query):
    shape = (TILE, TILE)
    key = first_key + lax.broadcasted_iota(jnp.int32, shape, 0)
    query = first_query + lax.broadcasted_iota(jnp.int32, shape, 1)
    valid = (key >= span[1]) & (key < span[1] + span[0])
    return (valid & (key <= query)) | (key == query)


def key_bias(span, first_key):
    key = first_key + lax.broadcasted_iota(jnp.int32, (TILE, 1), 0)
    return jnp.where((key >= span[1]) & (key < span[1] + span[0]), 0.0, MASKED)


def forward_kernel(
    span, own, native, factor, mlp_native,
    gathered, weights, qkv, out, logsum, rows_out, mlp_out, mlp_up, mlp_down,
    highest, summed, total,
    keep_sem, send_z, send_c, recv,
    native_sem, weight_sent, spread_sent, weight_got,
    rows_sent, rows_got, rows_local,
    mlp_local, line_sent, line_got, plane_sent, share_sent, mlp_have,
):
    heads = logsum.shape[0]
    width, slots = out.shape
    dim = width // heads
    low, f32 = qkv.dtype, jnp.float32
    here = Place()
    pairs = here.pairs
    split = mlp_native.shape[1]
    rows = own.shape[0]
    part = rows // CHUNKS
    columns = own.shape[1] // 2
    tall = native.shape[0] // split
    blocks = slots // TILE
    partner = here.partner()
    pair_barrier(here, plane=True)

    def half(core):
        return pl.ds(pl.multiple_of(core * columns, columns), columns)

    def weight_piece(ref, pair, core):
        return ref.at[pl.ds(pl.multiple_of(pair * tall, tall), tall), half(core)]

    line = lax.rem(here.t + 2, 4)
    weight_copy = remote(
        weight_piece(native, here.pair, here.c),
        weight_piece(weights, here.pair, here.c),
        weight_sent,
        weight_got.at[here.pair, here.c],
        (here.base + 1 - line // 2, line),
    )
    sends = here.pair < split

    @pl.when(sends)
    def _():
        weight_copy.start()

    native_copy = pltpu.make_async_copy(native, weights, native_sem)

    @pl.when(here.main)
    def _():
        native_copy.start()

    def place(seq, k, ch):
        block = jnp.where(seq == 0, k, 3 - k)
        return gathered.at[pl.ds(pl.multiple_of(block * rows + ch * part, part), part)]

    def copy(src, k, ch, seq, device, send):
        return remote(src, place(seq, k, ch), send.at[k, ch], recv.at[k, ch], device)

    def own_copy(k, ch, device, send):
        return copy(own.at[pl.ds(ch * part, part)], k, ch, here.c, device, send)

    def pass_copy(k, ch, device, send):
        return copy(place(here.g, k, ch), k, ch, here.g, device, send)

    def arrived(k, ch):
        pass_copy(k, ch, partner, send_z).wait_recv()

    keep = pltpu.make_async_copy(
        own, gathered.at[pl.ds(pl.multiple_of(here.t * rows, rows), rows)], keep_sem
    )
    near = here.device(here.c, jnp.where(here.pos == 1, 0, 1))

    @pl.when(here.main)
    def _():
        keep.start()
        for ch in range(CHUNKS):
            own_copy(here.pos, ch, near, send_z).start()
            own_copy(here.pos, ch, partner, send_c).start()

    @pl.when(jnp.logical_not(here.main))
    def _():
        for ch in range(CHUNKS):
            own_copy(here.pos, ch, near, send_z).start()

    kept = (mlp_out, mlp_up, mlp_down)

    def mlp_piece(w, quarter, pair, core):
        return kept[w].at[quarter, pair, :, half(core)]

    def mlp_line(w, step):
        return remote(
            mlp_native.at[w, here.pair, :, half(here.c)],
            mlp_piece(w, here.t, here.pair, here.c),
            line_sent.at[w, step - 1],
            line_got.at[w, here.t],
            (here.d, lax.rem(here.t + step, 4)),
        )

    def mlp_plane(w, n, step):
        quarter = lax.rem(here.t + n, 4)
        piece = mlp_piece(w, quarter, here.pair, here.c)
        return remote(
            piece, piece, plane_sent.at[w, n - 1, step], mlp_have.at[w, quarter, here.pair, here.c],
            here.across(step),
        )

    def mlp_core(w, n, pair):
        quarter = lax.rem(here.t + n, 4)
        piece = mlp_piece(w, quarter, pair, here.c)
        return remote(
            piece, piece, share_sent.at[w, n - 1, pair], mlp_have.at[w, quarter, pair, here.c], partner
        )

    def mlp_arrived(w, n, pair, core):
        quarter = lax.rem(here.t + n, 4)
        piece = mlp_piece(w, quarter, pair, core)
        remote(
            piece, piece, share_sent.at[0, 0, 0], mlp_have.at[w, quarter, pair, core], partner
        ).wait_recv()

    def mlp_keep(w):
        return pltpu.make_async_copy(mlp_native.at[w], kept[w].at[here.t], mlp_local.at[w])

    def to_line(w):
        @pl.when(sends)
        def _():
            for step in range(1, 4):
                mlp_line(w, step).start()

    to_line(0)
    to_line(1)
    to_line(2)
    for w in range(3):
        mlp_keep(w).start()

    def from_line(w):
        @pl.when(sends)
        def _():
            for n in (1, 3, 2):
                quarter = lax.rem(here.t + n, 4)
                piece = mlp_piece(w, quarter, here.pair, here.c)
                remote(
                    piece, piece, share_sent.at[0, 0, 0], line_got.at[w, quarter], partner
                ).wait_recv()
                for step in range(1, pairs):
                    mlp_plane(w, n, step).start()
                mlp_core(w, n, here.pair).start()

    def spread(core, step):
        piece = weight_piece(weights, here.pair, core)
        return remote(
            piece, piece, spread_sent.at[core, step - 1], weight_got.at[here.pair, core], here.across(step)
        )

    def weight_arrived(pair, core):
        piece = weight_piece(weights, pair, core)
        remote(piece, piece, weight_sent, weight_got.at[pair, core], partner).wait_recv()

    @pl.when(jnp.logical_not(here.main))
    def _():
        @pl.when(sends)
        def _():
            for core in range(2):
                weight_arrived(here.pair, core)
                for step in range(1, pairs):
                    spread(core, step).start()

        for pair in range(split):
            @pl.when(here.pair != pair)
            def _(pair=pair):
                for core in range(2):
                    weight_arrived(pair, core)

    @pl.when(here.main)
    def _():
        native_copy.wait()
        keep.wait()

    @pl.when(here.pos == 1)
    def _():
        for ch in range(CHUNKS):
            arrived(2, ch)
            pass_copy(2, ch, near, send_z).start()
            pass_copy(2, ch, partner, send_c).start()
            arrived(0, ch)
            pass_copy(0, ch, partner, send_c).start()
        for ch in range(CHUNKS):
            arrived(3, ch)
            pass_copy(3, ch, near, send_z).start()
            pass_copy(3, ch, partner, send_c).start()

    quarter = here.quarter()

    def into(q):
        return rows_out.at[pl.ds(pl.multiple_of(q * width, width), width)]

    def done_columns(i):
        return out.at[:, pl.ds(pl.multiple_of(i * TILE, TILE), TILE)]

    def rows_copy(i):
        return remote(
            done_columns(i), into(quarter), rows_sent.at[i], rows_got.at[quarter], (here.base + here.g, i)
        )

    rows_keep = pltpu.make_async_copy(done_columns(here.t), into(here.t), rows_local)

    def finish(i):
        qs = pl.ds(pl.multiple_of(i * TILE, TILE), TILE)
        for h in range(heads):
            hs = pl.ds(h * dim, dim)
            sums = summed[h : h + 1, qs]
            out[hs, qs] = (total[hs, qs] / sums).astype(out.dtype)
            logsum[h : h + 1, qs] = highest[h : h + 1, qs] + jnp.log(sums)
        stays = here.main & (here.t == i)

        @pl.when(stays)
        def _():
            rows_keep.start()

        @pl.when(jnp.logical_not(stays))
        def _():
            rows_copy(i).start()

    highest[...] = jnp.full_like(highest, MASKED)
    summed[...] = jnp.zeros_like(summed)
    total[...] = jnp.zeros_like(total)

    @pl.loop(0, blocks)
    def _(s):
        b = jnp.where(here.g == 0, s, blocks - 1 - s)
        last = (here.g == 1) & (s == blocks - 1)

        @pl.when((here.pos == 0) & (s >= 1))
        def _():
            for ch in range(CHUNKS):
                arrived(s, ch)
                pass_copy(s, ch, partner, send_c).start()

        @pl.when(jnp.logical_not(here.main))
        def _():
            for ch in range(CHUNKS):
                arrived(s, ch)

        @pl.when(s == 0)
        def _():
            from_line(0)

        @pl.when(s == 1)
        def _():
            from_line(1)

        @pl.when(s == 2)
        def _():
            from_line(2)

        bs = pl.ds(pl.multiple_of(b * TILE, TILE), TILE)
        for w in range(3):
            at = pl.ds(w * width, width)
            qkv[at, bs] = (dg(weights[at], gathered[bs], 1, 1) * factor[at]).astype(low)

        def tile(i, j, diagonal):
            qs = pl.ds(pl.multiple_of(i * TILE, TILE), TILE)
            ks = pl.ds(pl.multiple_of(j * TILE, TILE), TILE)
            if diagonal:
                allowed = readable(span, j * TILE, i * TILE)
            else:
                bias = key_bias(span, j * TILE)
            for h in range(heads):
                hs = pl.ds(h * dim, dim)
                scores = dg(qkv[pl.ds(width + h * dim, dim), ks], qkv[hs, qs], 0, 0)
                scores = jnp.where(allowed, scores, MASKED) if diagonal else scores + bias
                before = highest[h : h + 1, qs]
                after = jnp.maximum(before, jnp.max(scores, axis=0, keepdims=True))
                expo = jnp.exp(scores - after)
                scale = jnp.exp(before - after)
                summed[h : h + 1, qs] = summed[h : h + 1, qs] * scale + jnp.sum(expo, axis=0, keepdims=True)
                highest[h : h + 1, qs] = after
                total[hs, qs] = total[hs, qs] * scale + dg(
                    qkv[pl.ds(2 * width + h * dim, dim), ks], expo.astype(low), 1, 0
                )

        tile(b, b, True)

        @pl.when(last)
        def _():
            finish(b)

        @pl.loop(0, s)
        def _(n):
            i = jnp.where(here.g == 0, b, b + 1 + n)
            tile(i, jnp.where(here.g == 0, n, b), False)

            @pl.when(last)
            def _():
                finish(i)

        @pl.when(here.g == 0)
        def _():
            finish(b)


    for w in range(3):
        for n in (1, 3, 2):
            for pair in range(split):
                @pl.when(here.pair != pair)
                def _(w=w, n=n, pair=pair):
                    mlp_arrived(w, n, pair, here.c)
                    mlp_core(w, n, pair).start()

    for block in range(4):
        stays = here.main & (here.t == block)

        @pl.when(stays)
        def _():
            rows_keep.wait()

        @pl.when(jnp.logical_not(stays))
        def _(block=block):
            rows_copy(block).wait_send()
            remote(
                done_columns(0), into(block), rows_sent.at[0], rows_got.at[block], partner
            ).wait_recv()

    for w in range(3):
        for n in range(1, 4):
            for pair in range(split):
                mlp_arrived(w, n, pair, 1 - here.c)
                mlp_core(w, n, pair).wait_send()
        mlp_keep(w).wait()

    @pl.when(sends)
    def _():
        weight_copy.wait_send()
        for w in range(3):
            for step in range(1, 4):
                mlp_line(w, step).wait_send()
                for across in range(1, pairs):
                    mlp_plane(w, step, across).wait_send()

    @pl.when(sends & jnp.logical_not(here.main))
    def _():
        for core in range(2):
            for step in range(1, pairs):
                spread(core, step).wait_send()

    for ch in range(CHUNKS):
        own_copy(here.pos, ch, near, send_z).wait_send()

    @pl.when(here.main)
    def _():
        for ch in range(CHUNKS):
            own_copy(here.pos, ch, partner, send_c).wait_send()

    @pl.when(here.pos == 0)
    def _():
        for k in (1, 2, 3):
            for ch in range(CHUNKS):
                pass_copy(k, ch, partner, send_c).wait_send()

    @pl.when(here.pos == 1)
    def _():
        for ch in range(CHUNKS):
            pass_copy(0, ch, partner, send_c).wait_send()
            for k in (2, 3):
                pass_copy(k, ch, near, send_z).wait_send()
                pass_copy(k, ch, partner, send_c).wait_send()


def attention_forward(span, own, native, factor, mlp_native, heads):
    rows, model = own.shape
    slots = 4 * rows
    width = native.shape[0] // 3
    _, split, tall, _ = mlp_native.shape
    pairs = lax.axis_size("dp") // 2
    low, f32 = own.dtype, jnp.float32
    vmem = pl.BlockSpec(memory_space=pltpu.VMEM)
    hbm = pl.BlockSpec(memory_space=pl.ANY)
    dma = pltpu.SemaphoreType.DMA
    return pl.pallas_call(
        forward_kernel,
        out_shape=(
            jax.ShapeDtypeStruct((slots, model), low),
            jax.ShapeDtypeStruct(native.shape, low),
            jax.ShapeDtypeStruct((3 * width, slots), low),
            jax.ShapeDtypeStruct((width, slots), low),
            jax.ShapeDtypeStruct((heads, slots), f32),
            jax.ShapeDtypeStruct((4 * width, rows), low),
        )
        + (jax.ShapeDtypeStruct((4, split, tall, model), low),) * 3,
        in_specs=[pl.BlockSpec(memory_space=pltpu.SMEM), hbm, hbm, vmem, hbm],
        out_specs=(vmem,) * 5 + (hbm,) * 4,
        scratch_shapes=[
            pltpu.VMEM((heads, slots), f32),
            pltpu.VMEM((heads, slots), f32),
            pltpu.VMEM((width, slots), f32),
            dma,
            dma((4, CHUNKS)),
            dma((4, CHUNKS)),
            dma((4, CHUNKS)),
            dma,
            dma,
            dma((2, pairs - 1)),
            dma((split, 2)),
            dma((4,)),
            dma((4,)),
            dma,
            dma((3,)),
            dma((3, 3)),
            dma((3, 4)),
            dma((3, 3, pairs)),
            dma((3, 3, split)),
            dma((3, 4, split, 2)),
        ],
        compiler_params=pltpu.CompilerParams(
            collective_id=1, has_side_effects=True, vmem_limit_bytes=50 * 1024 * 1024
        ),
        name="attention_forward",
    )(span, own, native, factor, mlp_native)


def middle_kernel(
    span, gain, attended, residual, cotangent, w_out_in, w_up_in, w_down_in,
    output, grad_hidden, chip_sum, small, grad,
    w_out, w_up, w_down, second, activated, grad_low, grad_pre, branch, grad_att, weight_grad,
    load_sem, split_sent, split_got, local_sem, give_sent, give_got,
):
    here = Place()
    low, f32 = output.dtype, jnp.float32
    rows, model = output.shape
    width = grad.shape[0]
    pairs, tall = weight_grad.shape[2], weight_grad.shape[3]
    half_rows = rows // 2
    partner = here.partner()
    loads = [
        pltpu.make_async_copy(src, dst, load_sem.at[w])
        for w, (src, dst) in enumerate(((w_out_in, w_out), (w_up_in, w_up), (w_down_in, w_down)))
    ]
    for load in loads:
        load.start()
    pair_barrier(here)

    def of(q, r):
        return grad_att.at[
            pl.ds(pl.multiple_of(q * width, width), width), pl.ds(pl.multiple_of(r * half_rows, half_rows), half_rows)
        ]

    def into(block, r):
        return grad.at[:, pl.ds(pl.multiple_of(block * rows + r * half_rows, half_rows), half_rows)]

    def split_copy(q, r):
        native = (q // 2) == here.c
        seq = jnp.where(native, here.c, 1 - here.c)
        line = jnp.where(native, q, (q + 2) % 4)
        return remote(
            of(q, r), into(here.t, r), split_sent.at[q, r], split_got.at[here.t, r], (here.base + seq, line)
        )

    def keep(r):
        return pltpu.make_async_copy(of(here.t, r), into(here.t, r), local_sem.at[r])

    loads[0].wait()

    @pl.loop(0, 2)
    def _(r):
        at = pl.ds(pl.multiple_of(r * half_rows, half_rows), half_rows)
        hidden = residual[at].astype(f32) + dg(attended[:, at], w_out[...], 0, 0)
        inverse = lax.rsqrt(jnp.mean(hidden * hidden, axis=-1, keepdims=True) + EPSILON)
        scaled = hidden * inverse
        second[at] = (scaled * gain[...]).astype(low)

        @pl.when(r == 0)
        def _():
            loads[1].wait()

        before = dg(second[at], w_up[...], 1, 1)
        sigmoid = jax.nn.sigmoid(before)
        activated[at] = (before * sigmoid).astype(low)

        @pl.when(r == 0)
        def _():
            loads[2].wait()

        position = here.t * rows + r * half_rows + lax.broadcasted_iota(jnp.int32, (half_rows, 1), 0)
        valid = (position >= span[1]) & (position < span[1] + span[0])
        grad_out = jnp.where(valid, cotangent[at].astype(f32), 0.0)
        grad_low[at] = grad_out.astype(low)
        grad_act = dg(grad_low[at], w_down[...], 1, 1)
        grad_pre[at] = (grad_act * (sigmoid * (1.0 + before * (1.0 - sigmoid)))).astype(low)
        grad_scaled = dg(grad_pre[at], w_up[...], 1, 0) * gain[...]
        grad_rows = grad_out + inverse * (
            grad_scaled - scaled * jnp.mean(grad_scaled * scaled, axis=-1, keepdims=True)
        )
        grad_hidden[at] = grad_rows
        branch[at] = grad_rows.astype(low)
        grad_att[:, at] = dg(w_out[...], branch[at], 1, 1).astype(low)
        for q in range(4):
            stays = here.main & (here.t == q)

            @pl.when(stays)
            def _():
                keep(r).start()

            @pl.when(jnp.logical_not(stays))
            def _(q=q):
                split_copy(q, r).start()

        output[at] = (hidden + dg(activated[at], w_down[...], 1, 0)).astype(low)

    columns = chip_sum.shape[-1]
    two = 2 * width

    def half(core):
        return pl.ds(pl.multiple_of(core * columns, columns), columns)

    def give(w):
        return remote(
            weight_grad.at[w, :, :, :, half(1 - here.c)], chip_sum.at[w], give_sent.at[w], give_got.at[w], partner
        )

    small[...] = jnp.zeros_like(small)
    for w in range(3):
        for quarters in range(2):
            at = pl.ds(quarters * two, two)
            if w == 0:
                grads = dg(attended[at], branch[...], 1, 0)
            elif w == 1:
                grads = dg(grad_pre[:, at], second[...], 0, 0)
                small[1:2] += jnp.sum(grads * w_up[at].astype(f32), axis=0, keepdims=True)
            else:
                grads = dg(activated[:, at], grad_low[...], 0, 0)
            for q in range(2):
                for p in range(pairs):
                    first = q * width + p * tall
                    weight_grad[w, 2 * quarters + q, p] = grads[first : first + tall].astype(low)
        give(w).start()

    for w in range(3):
        give(w).wait_recv()

        @pl.loop(0, 4)
        def _(q, w=w):
            @pl.loop(0, pairs)
            def _(p):
                mine = weight_grad[w, q, p, :, half(here.c)]
                chip_sum[w, q, p] = (chip_sum[w, q, p].astype(f32) + mine.astype(f32)).astype(low)

    for r in range(2):
        for q in range(4):
            stays = here.main & (here.t == q)

            @pl.when(stays)
            def _(r=r):
                keep(r).wait()

            @pl.when(jnp.logical_not(stays))
            def _(q=q, r=r):
                remote(of(0, r), into(q, r), split_sent.at[0, r], split_got.at[q, r], partner).wait_recv()
                split_copy(q, r).wait_send()

    for w in range(3):
        give(w).wait_send()


def feed_forward(span, gain, attended, residual, cotangent, w_out, w_up, w_down, width, pairs):
    rows, model = residual.shape
    low, f32 = residual.dtype, jnp.float32
    vmem = pl.BlockSpec(memory_space=pltpu.VMEM)
    hbm = pl.BlockSpec(memory_space=pl.ANY)
    dma = pltpu.SemaphoreType.DMA
    tall = width // pairs
    return pl.pallas_call(
        middle_kernel,
        out_shape=(
            jax.ShapeDtypeStruct((rows, model), low),
            jax.ShapeDtypeStruct((rows, model), f32),
            jax.ShapeDtypeStruct((3, 4, pairs, tall, model // 2), low),
            jax.ShapeDtypeStruct((8, model), f32),
            jax.ShapeDtypeStruct((width, 4 * rows), low),
        ),
        in_specs=[pl.BlockSpec(memory_space=pltpu.SMEM)] + [vmem] * 4 + [hbm] * 3,
        out_specs=(vmem,) * 4 + (hbm,),
        scratch_shapes=[pltpu.VMEM((model, model), low)] * 3
        + [pltpu.VMEM((rows, model), low)] * 5
        + [
            pltpu.VMEM((model, rows), low),
            pltpu.VMEM((3, 4, pairs, tall, model), low),
            dma((3,)),
            dma((4, 2)),
            dma((4, 2)),
            dma((2,)),
            dma((3,)),
            dma((3,)),
        ],
        compiler_params=pltpu.CompilerParams(
            collective_id=3, has_side_effects=True, vmem_limit_bytes=65_000_000
        ),
        name="feed_forward",
    )(span, gain, attended, residual, cotangent, w_out, w_up, w_down)


def backward_kernel(
    span, qkv, out, logsum, factor, weights, small, grad, chip_sum, gathered,
    rows_grad, out_final, up_final, down_final, qkv_all, small_all,
    result, query_sum, key_sum, value_sum, term,
    partial, from_core, from_line, own_sum, pass_sum, plane_in,
    normed, scale_sum, weight_grad, qkv_in, qkv_swap, mlp_in, mlp_sum,
    small_own, small_pair, small_plane, small_line,
    own_sem, pass_sem, plane_sent, plane_got,
    send_c, send_z, recv_c, recv_z,
    out_sem, normed_sem, qkv_sent, qkv_got, cross_sent, cross_got, qkv_spread, qkv_share, qkv_have, qkv_local,
    line_sent, line_got, mlp_spread, mlp_share, mlp_have, mlp_local,
    small_sems, small_across_sent, small_across_got, small_along_sent, small_along_got,
):
    heads = logsum.shape[0]
    width, slots = out.shape
    dim = width // heads
    low, f32 = qkv.dtype, jnp.float32
    here = Place()
    pairs = here.pairs
    rows = rows_grad.shape[0]
    part = rows // BACK_CHUNKS
    partner = here.partner()
    pair_barrier(here, plane=True)
    blocks = slots // TILE

    columns = chip_sum.shape[-1]

    def half(core):
        return pl.ds(pl.multiple_of(core * columns, columns), columns)

    square = pairs == 4
    by_x = here.pair + 1 - 2 * lax.rem(here.pair, 2)
    by_y = lax.rem(here.pair + 2, 4)
    corner = 3 - here.pair

    def at_pair(pair):
        return (2 * pair + here.c, here.t)

    def plane_first(w, side, kind):
        to, pair = (by_x, by_y)[side], ((by_x, by_y)[side], corner)[kind]
        return remote(
            chip_sum.at[w, pl.ds(2 * side, 2), pair], plane_in.at[w, side, kind],
            plane_sent.at[w, 2 * side + kind], plane_got.at[w, 2 * side + kind], at_pair(to),
        )

    def plane_second(w, side):
        return remote(
            pass_sum.at[w, side], plane_in.at[w, side, 2], plane_sent.at[w, 4 + side], plane_got.at[w, 4 + side],
            at_pair((by_y, by_x)[side]),
        )

    def plane_copy(w, step):
        return remote(
            chip_sum.at[w, :, lax.rem(here.pair + step, pairs)],
            plane_in.at[step - 1, w],
            plane_sent.at[w, step - 1],
            plane_got.at[w, step - 1],
            here.across(step),
        )

    def plane_start(w):
        if square:
            for kind in (1, 0):
                for side in range(2):
                    plane_first(w, side, kind).start()
        else:
            for step in range(1, pairs):
                plane_copy(w, step).start()

    def plane_pass(w):
        if square:
            for side in range(2):
                plane_first(w, side, 1).wait_recv()
                for q in range(2):
                    pass_sum[w, side, q] = (
                        pass_sum[w, side, q].astype(f32) + plane_in[w, side, 1, q].astype(f32)
                    ).astype(low)
                plane_second(w, side).start()

    def plane_sent_all(w):
        if square:
            for side in range(2):
                plane_first(w, side, 0).wait_send()
                plane_first(w, side, 1).wait_send()
                plane_second(w, side).wait_send()
        else:
            for step in range(1, pairs):
                plane_copy(w, step).wait_send()

    pass_loads = []
    if square:
        pass_loads = [
            pltpu.make_async_copy(
                chip_sum.at[:, pl.ds(2 * side, 2), (by_y, by_x)[side]], pass_sum.at[:, side], pass_sem.at[side]
            )
            for side in range(2)
        ]
    for load in pass_loads:
        load.start()
    own_load = pltpu.make_async_copy(chip_sum.at[:, :, here.pair], own_sum, own_sem)
    own_load.start()
    for w in range(3):
        plane_start(w)
    out_copy = pltpu.make_async_copy(out, result.at[pl.ds(0, width)], out_sem)
    out_copy.start()
    query_sum[...] = jnp.zeros_like(query_sum)
    key_sum[...] = jnp.zeros_like(key_sum)
    value_sum[...] = jnp.zeros_like(value_sum)
    out_copy.wait()
    own_load.wait()
    for load in pass_loads:
        load.wait()
    for h in range(heads):
        hs = pl.ds(h * dim, dim)
        term[h : h + 1] = jnp.sum(grad[hs].astype(f32) * result[hs].astype(f32), axis=0, keepdims=True)

    def span_of(seq, k, ch):
        block = jnp.where(seq == 0, k, 3 - k)
        return pl.ds(pl.multiple_of(block * rows + ch * part, part), part)

    def piece(k, ch):
        return pl.ds(pl.multiple_of(k * rows + ch * part, part), part)

    def line_piece(k, ch):
        return piece(k % 3 if isinstance(k, int) else lax.rem(k, 3), ch)

    def line_rows(ch):
        return pl.ds(ch * part, part)

    def core_copy(k, ch):
        at = span_of(here.g, k, ch)
        return remote(partial.at[at], from_core.at[piece(k, ch)], send_c.at[k, ch], recv_c.at[k, ch], partner)

    def line_copy(k, ch):
        at = span_of(here.g, k, ch)
        return remote(
            partial.at[at],
            from_line.at[line_piece(k, ch)],
            send_z.at[k, ch],
            recv_z.at[k, ch],
            here.device(here.c, jnp.where(here.pos == 0, 1, 0)),
        )

    def home_copy(k, ch):
        at = span_of(here.g, k, ch)
        return remote(
            partial.at[at], rows_grad.at[line_rows(ch)], send_z.at[k, ch], recv_z.at[k, ch], here.device(here.c, k)
        )

    def core_sum(k, ch):
        core_copy(k, ch).wait_recv()
        return partial[span_of(here.g, k, ch)].astype(f32) + from_core[piece(k, ch)].astype(f32)

    def with_line(k, ch):
        line_copy(k, ch).wait_recv()
        return core_sum(k, ch) + from_line[line_piece(k, ch)].astype(f32)

    def pass_on(k):
        for ch in range(BACK_CHUNKS):
            partial[span_of(here.g, k, ch)] = core_sum(k, ch).astype(low)
            line_copy(k, ch).start()

    def send_home(k):
        for ch in range(BACK_CHUNKS):
            partial[span_of(here.g, k, ch)] = with_line(k, ch).astype(low)
            home_copy(k, ch).start()

    def mlp_line(w, step):
        line = lax.rem(here.t + step, 4)
        return remote(
            own_sum.at[w, line], mlp_in.at[w, step - 1], line_sent.at[w, step - 1],
            line_got.at[w, step - 1], (here.d, line),
        )

    def plane_total(w):
        if square:
            for side in range(2):
                plane_first(w, side, 0).wait_recv()
                plane_second(w, side).wait_recv()
                for q in range(2):
                    own_sum[w, 2 * side + q] = (
                        own_sum[w, 2 * side + q].astype(f32)
                        + plane_in[w, side, 0, q].astype(f32)
                        + plane_in[w, side, 2, q].astype(f32)
                    ).astype(low)
        else:
            for step in range(1, pairs):
                plane_copy(w, step).wait_recv()

            @pl.loop(0, 4)
            def _(q):
                total = own_sum[w, q].astype(f32)
                for step in range(1, pairs):
                    total += plane_in[step - 1, w, q].astype(f32)
                own_sum[w, q] = total.astype(low)

        for step in range(1, 4):
            mlp_line(w, step).start()

    @pl.loop(0, blocks)
    def _(s):
        b = jnp.where(here.g == 0, blocks - 1 - s, s)
        k = blocks - 1 - s

        def tile(i, j, diagonal):
            qs = pl.ds(pl.multiple_of(i * TILE, TILE), TILE)
            ks = pl.ds(pl.multiple_of(j * TILE, TILE), TILE)
            if diagonal:
                allowed = readable(span, j * TILE, i * TILE)
            else:
                bias = key_bias(span, j * TILE)
            for h in range(heads):
                hs = pl.ds(h * dim, dim)
                ke = pl.ds(width + h * dim, dim)
                va = pl.ds(2 * width + h * dim, dim)
                scores = dg(qkv[ke, ks], qkv[hs, qs], 0, 0)
                scores = jnp.where(allowed, scores, MASKED) if diagonal else scores + bias
                probs = jnp.exp(scores - logsum[h : h + 1, qs])
                grad_probs = dg(qkv[va, ks], grad[hs, qs], 0, 0)
                grad_scores = (probs * (grad_probs - term[h : h + 1, qs])).astype(low)
                value_sum[hs, ks] += dg(grad[hs, qs], probs.astype(low), 1, 1)
                key_sum[hs, ks] += dg(qkv[hs, qs], grad_scores, 1, 1)
                query_sum[hs, qs] += dg(qkv[ke, ks], grad_scores, 1, 0)

        tile(b, b, True)

        @pl.when((here.pos == 0) & (s >= 1))
        def _():
            pass_on(k + 1)

        @pl.when(s >= 1)
        def _():
            plane_pass(s - 1)

        @pl.when(s >= 2)
        def _():
            plane_total(s - 2)

        @pl.loop(0, blocks - 1 - s)
        def _(n):
            tile(jnp.where(here.g == 0, b, b + 1 + n), jnp.where(here.g == 0, n, b), False)

        bs = pl.ds(pl.multiple_of(b * TILE, TILE), TILE)
        result[pl.ds(0, width), bs] = (query_sum[:, bs] * factor[...]).astype(low)
        result[pl.ds(width, width), bs] = key_sum[:, bs].astype(low)
        result[pl.ds(2 * width, width), bs] = value_sum[:, bs].astype(low)
        partial[bs] = dg(result[:, bs], weights[...], 0, 0).astype(low)

        @pl.when(jnp.logical_not(here.main))
        def _():
            for ch in range(BACK_CHUNKS):
                core_copy(k, ch).start()

    plane_total(2)

    @pl.when(here.pos == 1)
    def _():
        send_home(3)

    chunks, _, share, depth = weight_grad.shape

    half_slots = slots // 2

    def load(i, part_of):
        return pltpu.make_async_copy(
            gathered.at[
                pl.ds(part_of * half_slots, half_slots), pl.ds(pl.multiple_of(i * depth, depth), depth)
            ],
            normed.at[part_of],
            normed_sem.at[part_of],
        )

    def turn(i):
        even = lax.rem(i, 2) == 0
        return jnp.where(even, by_x, by_y), jnp.where(even, by_y, by_x)

    def qkv_send(i, step):
        if square:
            first, second = turn(i)
            to = (first, first, second)[step - 1]
            pair = (first, corner, second)[step - 1]
            device = at_pair(to)
        else:
            pair, device = lax.rem(here.pair + step, pairs), here.across(step)
        return remote(
            weight_grad.at[i, pair], qkv_in.at[i, step - 1], qkv_sent.at[i, step - 1], qkv_got.at[i, step - 1], device
        )

    first_steps = (2, 1) if square else range(1, pairs)

    small_own[...] = small[...]
    scale_sum[...] = jnp.zeros_like(scale_sum)
    load(0, 0).start()
    load(0, 1).start()

    @pl.loop(0, chunks)
    def _(i):
        at = pl.ds(pl.multiple_of(i * depth, depth), depth)
        load(i, 0).wait()
        grads = dg(result[:, :half_slots], normed[0], 1, 0)

        @pl.when(i + 1 < chunks)
        def _():
            load(i + 1, 0).start()

        load(i, 1).wait()
        grads += dg(result[:, half_slots:], normed[1], 1, 0)

        @pl.when(i + 1 < chunks)
        def _():
            load(i + 1, 1).start()

        for p in range(pairs):
            weight_grad[i, p] = grads[p * share : (p + 1) * share].astype(low)
        for step in first_steps:
            qkv_send(i, step).start()
        weighted = grads * weights[:, at].astype(f32)
        small_own[0:1, at] = jnp.sum(weighted, axis=0, keepdims=True)
        scale_sum[pl.ds(0, width)] += jnp.broadcast_to(
            jnp.sum(weighted[:width], axis=1, keepdims=True), (width, 128)
        )

    padded = scale_sum.shape[0]
    small_own[2:3, pl.ds(0, padded)] = jnp.transpose(scale_sum[...])[0:1]
    small_copy = remote(small_own, small_pair, small_sems.at[0], small_sems.at[1], partner)
    small_copy.start()

    @pl.when(here.pos == 1)
    def _():
        pass_on(0)

    def mlp_piece(w, pair, core):
        return (out_final, up_final, down_final)[w].at[pair, :, half(core)]

    def mlp_out(w, step):
        return remote(
            mlp_sum.at[w], mlp_piece(w, here.pair, here.c), mlp_spread.at[w, step], mlp_have.at[w, here.d],
            here.across(step),
        )

    def mlp_own(w):
        return remote(
            mlp_sum.at[w], mlp_piece(w, here.pair, here.c), mlp_share.at[w, 0], mlp_have.at[w, here.d], partner
        )

    def mlp_keep(w):
        return pltpu.make_async_copy(mlp_sum.at[w], mlp_piece(w, here.pair, here.c), mlp_local.at[w])

    def mlp_core(w, step):
        pair = lax.rem(here.pair + step, pairs)
        piece = mlp_piece(w, pair, here.c)
        return remote(piece, piece, mlp_share.at[w, step], mlp_have.at[w, 2 * pair + here.c], partner)

    def mlp_arrived(w, pair, core):
        remote(
            mlp_sum.at[w], mlp_piece(w, pair, core), mlp_share.at[w, 0], mlp_have.at[w, 2 * pair + core], partner
        ).wait_recv()

    @pl.when(here.pos == 1)
    def _():
        send_home(2)

    line = lax.rem(here.t + 2, 4)

    def cross(i):
        return remote(
            qkv_swap.at[0, i], qkv_swap.at[1, i], cross_sent.at[i], cross_got.at[i],
            (here.base + line // 2, line),
        )

    def qkv_piece(i, pair):
        return qkv_all.at[pair, :, pl.ds(pl.multiple_of(i * depth, depth), depth)]

    def qkv_out(i, step):
        return remote(
            qkv_swap.at[0, i], qkv_piece(i, here.pair), qkv_spread.at[i, step], qkv_have.at[i, here.pair],
            here.across(step),
        )

    def qkv_own(i):
        return remote(
            qkv_swap.at[0, i], qkv_piece(i, here.pair), qkv_share.at[i, 0], qkv_have.at[i, here.pair], partner
        )

    def qkv_keep(i):
        return pltpu.make_async_copy(qkv_swap.at[0, i], qkv_piece(i, here.pair), qkv_local.at[i])

    def qkv_core(i, step):
        pair = lax.rem(here.pair + step, pairs)
        return remote(
            qkv_piece(i, pair), qkv_piece(i, pair), qkv_share.at[i, step], qkv_have.at[i, pair], partner
        )

    def finish(i):
        @pl.when(here.main)
        def _():
            cross(i).wait_recv()
            qkv_swap[0, i] = (qkv_swap[0, i].astype(f32) + qkv_swap[1, i].astype(f32)).astype(low)
            qkv_keep(i).start()
            for step in range(1, pairs):
                qkv_out(i, step).start()
            qkv_own(i).start()

    def qkv_pass(i):
        if square:
            qkv_send(i, 2).wait_recv()
            _, second = turn(i)
            weight_grad[i, second] = (weight_grad[i, second].astype(f32) + qkv_in[i, 1].astype(f32)).astype(low)
            qkv_send(i, 3).start()

    def qkv_total(i):
        total = weight_grad[i, here.pair].astype(f32)
        for step in (1, 3) if square else range(1, pairs):
            qkv_send(i, step).wait_recv()
            total += qkv_in[i, step - 1].astype(f32)
        qkv_swap[0, i] = total.astype(low)

        @pl.when(jnp.logical_not(here.main))
        def _():
            cross(i).start()

    @pl.loop(0, chunks + 2)
    def _(n):
        @pl.when(n < chunks)
        def _():
            qkv_pass(n)

        @pl.when((n >= 1) & (n <= chunks))
        def _():
            qkv_total(n - 1)

        @pl.when(n >= 2)
        def _():
            finish(n - 2)

    for w in range(3):
        total = own_sum[w, here.t].astype(f32)
        for step in range(1, 4):
            mlp_line(w, step).wait_recv()
            total += mlp_in[w, step - 1].astype(f32)
        mlp_sum[w] = total.astype(low)
        for step in range(1, pairs):
            mlp_out(w, step).start()
        mlp_own(w).start()
        mlp_keep(w).start()

    small_copy.wait_recv()
    small_plane[here.pair] = small_own[...] + small_pair[...]

    def small_across(step):
        return remote(
            small_plane.at[here.pair], small_plane.at[here.pair], small_across_sent.at[step],
            small_across_got.at[here.pair], here.across(step),
        )

    def small_along(step):
        return remote(
            small_line.at[here.t], small_line.at[here.t], small_along_sent.at[step], small_along_got.at[here.t],
            (here.d, lax.rem(here.t + step, 4)),
        )

    for step in range(1, pairs):
        small_across(step).start()

    for step in range(1, pairs):
        pair = lax.rem(here.pair + step, pairs)
        remote(
            small_own, small_plane.at[pair], small_across_sent.at[0], small_across_got.at[pair], partner
        ).wait_recv()
    plane_total = small_plane[0]
    for pair in range(1, pairs):
        plane_total += small_plane[pair]
    small_line[here.t] = plane_total
    for step in range(1, 4):
        small_along(step).start()

    @pl.when(here.pos == 0)
    def _():
        for ch in range(BACK_CHUNKS):
            rows_grad[line_rows(ch)] = with_line(0, ch).astype(low)
        for k in (1, 2, 3):
            for ch in range(BACK_CHUNKS):
                line_copy(k, ch).wait_send()

    @pl.when(here.pos == 1)
    def _():
        for ch in range(BACK_CHUNKS):
            rows_grad[line_rows(ch)] = with_line(1, ch).astype(low)
        for ch in range(BACK_CHUNKS):
            line_copy(0, ch).wait_send()
            for k in (2, 3):
                home_copy(k, ch).wait_send()

    for k in (2, 3):
        @pl.when(here.pos == k)
        def _(k=k):
            for ch in range(BACK_CHUNKS):
                remote(
                    partial.at[piece(0, ch)], rows_grad.at[line_rows(ch)], send_z.at[0, ch], recv_z.at[k, ch], partner
                ).wait_recv()

    for step in range(1, 4):
        other = lax.rem(here.t + step, 4)
        remote(
            small_own, small_line.at[other], small_along_sent.at[0], small_along_got.at[other], partner
        ).wait_recv()
    small_all[...] = (small_line[0] + small_line[1]) + (small_line[2] + small_line[3])

    @pl.when(here.main)
    def _():
        @pl.loop(0, chunks)
        def _(i):
            for step in range(1, pairs):
                qkv_core(i, step).wait_recv()
                qkv_core(i, step).start()

    for w in range(3):
        for step in range(1, pairs):
            mlp_arrived(w, lax.rem(here.pair + step, pairs), here.c)
            mlp_core(w, step).start()

    @pl.when(here.main)
    def _():
        @pl.loop(0, chunks)
        def _(i):
            qkv_keep(i).wait()
            qkv_own(i).wait_send()
            for step in range(1, pairs):
                qkv_out(i, step).wait_send()
                qkv_core(i, step).wait_send()

    @pl.when(jnp.logical_not(here.main))
    def _():
        @pl.loop(0, chunks)
        def _(i):
            cross(i).wait_send()
            for step in range(pairs):
                qkv_core(i, step).wait_recv()

        for k in range(4):
            for ch in range(BACK_CHUNKS):
                core_copy(k, ch).wait_send()

    for w in range(3):
        for step in range(pairs):
            mlp_arrived(w, lax.rem(here.pair + step, pairs), 1 - here.c)
        mlp_keep(w).wait()
        mlp_own(w).wait_send()
        for step in range(1, pairs):
            mlp_out(w, step).wait_send()
            mlp_core(w, step).wait_send()
        for step in range(1, 4):
            mlp_line(w, step).wait_send()

    for w in range(3):
        plane_sent_all(w)

    @pl.loop(0, chunks)
    def _(i):
        for step in range(1, pairs):
            qkv_send(i, step).wait_send()

    for step in range(1, pairs):
        small_across(step).wait_send()
    for step in range(1, 4):
        small_along(step).wait_send()
    small_copy.wait_send()


DEPTH = 256


def attention_backward(
    span, qkv, out, logsum, factor, weights, small, grad, chip_sum, gathered
):
    width, slots = out.shape
    heads = logsum.shape[0]
    rows, model = slots // 4, weights.shape[1]
    low, f32 = qkv.dtype, jnp.float32
    _, _, pairs, slice_rows, columns = chip_sum.shape
    chunks, share = model // DEPTH, 3 * width // pairs
    vmem = pl.BlockSpec(memory_space=pltpu.VMEM)
    hbm = pl.BlockSpec(memory_space=pl.ANY)
    dma = pltpu.SemaphoreType.DMA
    buffer = pltpu.VMEM
    return pl.pallas_call(
        backward_kernel,
        out_shape=(
            jax.ShapeDtypeStruct((rows, model), low),
            jax.ShapeDtypeStruct((pairs, slice_rows, model), low),
            jax.ShapeDtypeStruct((pairs, slice_rows, model), low),
            jax.ShapeDtypeStruct((pairs, slice_rows, model), low),
            jax.ShapeDtypeStruct((pairs, share, model), low),
            jax.ShapeDtypeStruct(small.shape, f32),
        ),
        in_specs=[pl.BlockSpec(memory_space=pltpu.SMEM), vmem, hbm] + [vmem] * 5 + [hbm] * 2,
        out_specs=(vmem, hbm, hbm, hbm, hbm, vmem),
        scratch_shapes=[
            buffer(qkv.shape, low),
            buffer((width, slots), f32),
            buffer((width, slots), f32),
            buffer((width, slots), f32),
            buffer((heads, slots), f32),
            buffer((slots, model), low),
            buffer((slots, model), low),
            buffer((3 * rows, model), low),
            buffer((3, 4, slice_rows, columns), low),
            buffer((3, 2, 2, slice_rows, columns) if pairs == 4 else (8, 128), low),
            buffer(
                (3, 2, 3, 2, slice_rows, columns) if pairs == 4 else (pairs - 1, 3, 4, slice_rows, columns), low
            ),
            buffer((2, slots // 2, DEPTH), low),
            buffer((width + -width % 128, 128), f32),
            buffer((chunks, pairs, share, DEPTH), low),
            buffer((chunks, pairs - 1, share, DEPTH), low),
            buffer((2, chunks, share, DEPTH), low),
            buffer((3, 3, slice_rows, columns), low),
            buffer((3, slice_rows, columns), low),
            buffer(small.shape, f32),
            buffer(small.shape, f32),
            buffer((pairs,) + small.shape, f32),
            buffer((4,) + small.shape, f32),
            dma,
            dma((2,)),
            dma((3, max(6, pairs - 1))),
            dma((3, max(6, pairs - 1))),
            dma((4, BACK_CHUNKS)),
            dma((4, BACK_CHUNKS)),
            dma((4, BACK_CHUNKS)),
            dma((4, BACK_CHUNKS)),
            dma,
            dma((2,)),
            dma((chunks, pairs - 1)),
            dma((chunks, pairs - 1)),
            dma((chunks,)),
            dma((chunks,)),
            dma((chunks, pairs)),
            dma((chunks, pairs)),
            dma((chunks, pairs)),
            dma((chunks,)),
            dma((3, 3)),
            dma((3, 3)),
            dma((3, pairs)),
            dma((3, pairs)),
            dma((3, 2 * pairs)),
            dma((3,)),
            dma((2,)),
            dma((pairs,)),
            dma((pairs,)),
            dma((4,)),
            dma((4,)),
        ],
        compiler_params=pltpu.CompilerParams(
            collective_id=2, has_side_effects=True, vmem_limit_bytes=65_500_000
        ),
        name="attention_backward",
    )(span, qkv, out, logsum, factor, weights, small, grad, chip_sum, gathered)


def per_device(
    inputs,
    cotangent,
    gain_attn,
    gain_mlp,
    query_scale,
    w_query,
    w_key,
    w_value,
    w_out,
    w_up,
    w_down,
    lengths,
    offsets,
):
    low = jnp.bfloat16
    f32 = jnp.float32
    here = Place()
    n_dp = lax.axis_size("dp")
    local_rows, model = inputs.shape
    seq_slots = local_rows * 4
    width_local = w_query.shape[1]
    head_dim = query_scale.shape[0]
    heads_local = width_local // head_dim
    pairs = n_dp // 2
    swap_core = [(i, i ^ 1) for i in range(n_dp)]

    split = min(pairs, 4)
    mlp_native = jnp.stack([w_out, jnp.transpose(w_up), w_down])
    mlp_native = mlp_native.reshape(3, split, width_local // split, model)
    native = jnp.concatenate(
        [jnp.transpose(w_query), jnp.transpose(w_key), jnp.transpose(w_value)]
    )
    own_span = jnp.concatenate([lengths, offsets])
    other_span = lax.ppermute(own_span, "dp", swap_core)
    group_span = jnp.where(here.main, own_span, other_span)
    residual = inputs.astype(f32)
    normed, inverse_one = rms_forward(residual, gain_attn)
    scale_const = LOG_TWO_E / math.sqrt(head_dim)
    soft = jax.nn.softplus(query_scale)
    factor = jnp.tile(soft * scale_const, heads_local)[:, None]
    gathered, stacked_w, qkv, attended, logsum, attended_rows, *mlp_w = attention_forward(
        group_span,
        normed.astype(low),
        native,
        jnp.concatenate([factor, jnp.ones((2 * width_local, 1), f32)]),
        mlp_native,
        heads_local,
    )
    w_out_all, w_up_all, w_down_all = (weight.reshape(model, model) for weight in mlp_w)
    output, grad_hidden, chip_sum, small, grad_attended = feed_forward(
        own_span, gain_mlp[None], attended_rows, inputs, cotangent, w_out_all, w_up_all, w_down_all,
        width_local, pairs,
    )
    grad_first, grad_out, grad_up, grad_down, qkv_all, small = attention_backward(
        group_span, qkv, attended, logsum, factor, stacked_w, small, grad_attended, chip_sum, gathered
    )
    grad_input = grad_hidden + rms_backward(
        residual, inverse_one, gain_attn, grad_first.astype(f32)
    )
    grad_gain_one = small[0] / gain_attn
    grad_gain_two = small[1] / gain_mlp
    scale_sum = jnp.sum(small[2, :width_local].reshape(heads_local, head_dim), axis=0)
    grad_scale = scale_sum * jax.nn.sigmoid(query_scale) / soft
    qkv_all = qkv_all.reshape(3 * width_local, model)

    def final(weight):
        return weight.reshape(width_local, model).astype(f32)

    return (
        output,
        grad_input,
        grad_gain_one,
        grad_gain_two,
        grad_scale,
        jnp.transpose(final(qkv_all[:width_local])),
        jnp.transpose(final(qkv_all[width_local:2 * width_local])),
        jnp.transpose(final(qkv_all[2 * width_local:3 * width_local])),
        final(grad_out),
        jnp.transpose(final(grad_up)),
        final(grad_down),
    )


def solution(mesh):
    rows = P(("dp", "tensor"), None)
    cols_t = P(None, "tensor")
    rows_t = P("tensor", None)
    return jax.shard_map(
        per_device,
        mesh=mesh,
        in_specs=(
            rows, rows, P(), P(), P(), cols_t, cols_t, cols_t, rows_t, cols_t, rows_t, P("dp"), P("dp"),
        ),
        out_specs=(
            rows, rows, P(), P(), P(), cols_t, cols_t, cols_t, rows_t, cols_t, rows_t,
        ),
        check_vma=False,
    )
```
